256 devices in a mesh: tm: 32 (over z, x), trk: 8 (over y, core).
Axes of the slice: x: 4, y: 4, z: 8, core: 2. Of those that a mesh axis runs over, the one named last changes fastest.
Arguments:
- track_embed: bfloat16 [8192, 1024], P(('tm', 'trk')), may hold values from -6 to 6
- view_ids: int32 [8192, 16], P(('tm', 'trk')), may hold values from 0 to 255, all different within a row; in each aligned block of 32 rows (0 to 31, 32 to 63, ...) at most 4 rows name the same one
- view_count: int32 [8192], P(('tm', 'trk')), may hold values from 1 to 16
- key_feats: bfloat16 [32, 8, 512, 1024], P('tm', 'trk'), may hold values from -160 to 160
- value_feats: bfloat16 [32, 8, 512, 1024], P('tm', 'trk'), may hold values from -6 to 6
- track_gain: float32 [1024], replicated, may hold values from 0.5 to 1.5
- w_temporal: bfloat16 [1024, 3072], replicated, may hold values from -0.1875 to 0.1875
- temporal_scale: float32 [8], replicated, may hold values from 0.5 to 40
- w_merge: bfloat16 [1024, 1024], replicated, may hold values from -0.1875 to 0.1875
- box_gain: float32 [1024], replicated, may hold values from 0.5 to 1.5
- w_hidden: bfloat16 [1024, 512], replicated, may hold values from -0.1875 to 0.1875
- b_hidden: float32 [512], replicated, may hold values from -4 to 4
- w_box: bfloat16 [512, 10], replicated, may hold values from -0.25 to 0.25
Outputs:
- refined: bfloat16 [8192, 16, 1024], P(('tm', 'trk'))
- boxes: float32 [8192, 16, 10], P(('tm', 'trk'))
The draws below stay inside these ranges and needn't reach their ends.
Inputs may be any that keep to these rules, and one draw needn't show every extreme that they name: `view_ids`: entry v stands for frame v // 8 seen by camera v % 8. The 16 entries of one track are distinct. Counting padding entries too, at most 4 of the tracks of one device name any one view, and in some of the devices exactly 4 name one view. Only the first view_count entries of a track's list are visible; the others are padding.
All inputs are finite; a program needn't handle non-finite values.
Results may differ from the reference program's by a relative error of at most 0.0055.
The reference program's roundings to bfloat16 on the way count: a program that leaves them out, or rounds other values in their place, can miss the bound.
Values may be sent and summed in bfloat16 or wider, within the bound.
A program may use at most 64 MiB of HBM per device.

```python
import math
import jax
import jax.numpy as jnp
import numpy as np
from jax import lax

D = 1024
HEADS = 8
MLPW = 512
BOX = 10
CAMS = 8
VMAX = 16
PIX = 512
TRK_DEV = 32
FR_DEV = 1
FRAMES = 32
TRACKS = 8192
CAP = 4
N_TM = 32
N_TRK = 8


def draw_key_feats(key, part):
    base_draw = jax.random.normal(key, (FRAMES, CAMS, PIX, D), jnp.float32)
    return jnp.clip(base_draw, -6.0, 6.0).astype(jnp.bfloat16)


def draw_temporal_scale(key, part):
    return jax.random.uniform(key, (HEADS,), jnp.float32, 0.5, 2.0)


def plant(drawn, rng, low, largest):
    dims = drawn.shape
    place = [jax.random.randint(jax.random.fold_in(rng, axis), (), 0, dims[axis]) for axis in range(len(dims))]
    drawn = drawn.at[tuple(place)].set(low)
    longest = dims.index(max(dims))
    place[longest] = (place[longest] + 1) % dims[longest]
    return drawn.at[tuple(place)].set(largest)


def levels(own_key, dims, shards, low, top_value):
    def one(axis_at, parts):
        heights = jax.random.uniform(jax.random.fold_in(jax.random.fold_in(own_key, 6), axis_at), (parts,), jnp.float32, low / len(shards), top_value / len(shards))
        return jnp.repeat(jnp.exp(heights), dims[axis_at] // parts).reshape((-1,) + (1,) * (len(dims) - axis_at - 1))

    factor_of = one(*shards[0])
    for cut in shards[1:]:
        factor_of = factor_of * one(*cut)
    return factor_of


def assign_block(rng, own, number, rows, amount, top, reach, lean):
    order = jax.random.permutation(rng, amount)
    crowded, common = shares(amount, rows * top, reach, lean, True), shares(amount, rows * top, reach, lean, False)
    places = jnp.arange(amount)

    def named(sizes, turn):
        used = int((sizes > 0).sum())
        fixed = max(1, used // 4)
        moved = fixed + (places - fixed + turn * (used - fixed)) % max(1, amount - fixed)
        return jnp.zeros((amount,), jnp.int32).at[order[jnp.where(places < fixed, places, moved)]].set(jnp.asarray(sizes, jnp.int32))

    sizes = jnp.where(number % 4 == 0, named(crowded, number // 4), named(common, number - number // 4 - 1))
    mixed = jax.random.permutation(jax.random.fold_in(own, 3), amount)
    donor, sink = mixed[0:amount // 2 * 2:2], mixed[1:amount // 2 * 2:2]
    margin = jnp.minimum(sizes[donor] - 1, reach - sizes[sink]) // 2
    margin = jnp.where((donor == order[0]) | (sink == order[0]) | (sizes[sink] == 0), 0, jnp.maximum(margin, 0))
    moved = jax.random.randint(jax.random.fold_in(own, 4), (amount // 2,), 0, 1 << 20) % (margin + 1)
    sizes = sizes.at[donor].add(-moved).at[sink].add(moved)
    members = jnp.searchsorted(jnp.cumsum(sizes), jnp.arange(rows * top), side="right").astype(jnp.int32)
    listing = members.reshape(top, rows).T
    listing = listing[jax.random.permutation(jax.random.fold_in(own, 1), rows)]
    turn = jax.random.randint(jax.random.fold_in(own, 2), (rows, 1), 0, top)
    return jnp.take_along_axis(listing, (jnp.arange(top)[None, :] + turn) % top, axis=1)


def shares(number_of, total, limit, lean, full):
    loads = [(1 << 20) // math.isqrt(grade ** lean) + 1 for grade in range(1, number_of + 1)]
    largest = limit if full else min(limit, max(-(-total // number_of), total * loads[0] // sum(loads)))
    least = 1 if total - largest >= number_of - 1 else 0
    given, rest = [largest] + [least] * (number_of - 1), total - largest - least * (number_of - 1)
    while rest > 0:
        candidates = [i for i in range(1, number_of) if given[i] < largest] or [i for i in range(1, number_of) if given[i] < limit]
        mass, left = sum([loads[i] for i in candidates]), rest
        for i in candidates:
            extra = min(limit - given[i], max(1, left * loads[i] // mass), rest)
            given[i] = given[i] + extra
            rest = rest - extra
    return np.array(given)


def gaussian(rng, shape, scale, reach, shards=(), held_as=jnp.bfloat16):
    values = scale * jax.random.normal(rng, shape, jnp.float32)
    if shards:
        values = values * levels(rng, shape, shards, -0.22, 0.18)
    return jnp.clip(values, -reach, reach).astype(held_as)


def setup_inputs(seed: int = 0) -> dict:
    streams_of = jax.random.split(jax.random.key(seed), 14)
    track_embed = gaussian(streams_of[0], (TRACKS, D), 1.0, 6.0, ((0, 256),))
    view_ids_keys = jax.random.split(jax.random.fold_in(streams_of[1], 1), TRACKS // TRK_DEV)
    view_ids_turns = jax.random.permutation(jax.random.fold_in(streams_of[1], 3), TRACKS // TRK_DEV)
    view_ids = jax.vmap(lambda own, number: assign_block(jax.random.fold_in(streams_of[1], 2), own, number, TRK_DEV, FR_DEV * N_TM * CAMS, VMAX, CAP, 2))(view_ids_keys, view_ids_turns).reshape((TRACKS, VMAX))
    view_count = plant(jax.random.randint(streams_of[2], (TRACKS,), 1, VMAX + 1), jax.random.fold_in(streams_of[2], 1), 1, VMAX).astype(jnp.int32)
    key_feats = draw_key_feats(jax.random.fold_in(streams_of[13], 71), 0)
    value_feats = gaussian(streams_of[4], (FRAMES, CAMS, PIX, D), 1.0, 6.0, ((0, 32), (1, 8)))
    track_gain = jnp.clip(1.0 + 0.1 * jax.random.normal(streams_of[5], (D,), jnp.float32), 0.5, 1.5)
    w_temporal = gaussian(streams_of[6], (D, 3 * D), D ** -0.5, 0.1875)
    temporal_scale = draw_temporal_scale(jax.random.fold_in(streams_of[13], 71), 0)
    w_merge = gaussian(streams_of[8], (D, D), D ** -0.5, 0.1875)
    box_gain = jnp.clip(1.0 + 0.1 * jax.random.normal(streams_of[9], (D,), jnp.float32), 0.5, 1.5)
    w_hidden = gaussian(streams_of[10], (D, MLPW), D ** -0.5, 0.1875)
    b_hidden = gaussian(streams_of[11], (MLPW,), 1.0, 4.0, (), jnp.float32)
    w_box = gaussian(streams_of[12], (MLPW, BOX), MLPW ** -0.5, 0.25)
    return dict(track_embed=track_embed, view_ids=view_ids, view_count=view_count, key_feats=key_feats, value_feats=value_feats, track_gain=track_gain, w_temporal=w_temporal, temporal_scale=temporal_scale, w_merge=w_merge, box_gain=box_gain, w_hidden=w_hidden, b_hidden=b_hidden, w_box=w_box)


epsilon = 1e-05
masked_score = -1e+30

def layer_norm(values):
    centre = lax.optimization_barrier(jnp.mean(values, axis=-1, keepdims=True))
    shifted = values - centre
    spread = lax.optimization_barrier(jnp.mean(shifted * shifted, axis=-1, keepdims=True))
    return shifted * lax.rsqrt(spread + epsilon)

def time_code(frame_ids, model_width):
    half_width = model_width // 2
    freq_index = jnp.arange(half_width).astype(jnp.float32)
    freq_rates = jnp.exp(freq_index * (-2.0 * math.log(10000.0) / model_width))
    angles = frame_ids.astype(jnp.float32)[..., None] * freq_rates
    return jnp.concatenate([jnp.sin(angles), jnp.cos(angles)], axis=-1)

def view_attention(picked, key_rows, value_rows):
    row_count = picked.shape[0]
    head_feature_width = D // HEADS
    per_head_queries = picked.astype(jnp.float32).reshape(row_count, HEADS, head_feature_width)
    per_head_keys = key_rows.astype(jnp.float32).reshape(key_rows.shape[0], HEADS, head_feature_width)
    per_head_values = value_rows.astype(jnp.float32).reshape(value_rows.shape[0], HEADS, head_feature_width)
    attention_scores = jnp.einsum('ljk,fjk->jlf', per_head_queries, per_head_keys) * head_feature_width ** (-0.5)
    row_top = lax.optimization_barrier(jnp.max(attention_scores, axis=-1, keepdims=True))
    weights = jnp.exp(attention_scores - row_top)
    totals = lax.optimization_barrier(jnp.sum(weights, axis=-1))
    rounded_scores = lax.optimization_barrier(weights.astype(jnp.bfloat16)).astype(jnp.float32)
    softmax_numerator = jnp.einsum('tnz,ztr->ntr', rounded_scores, per_head_values)
    result_rows = softmax_numerator / jnp.transpose(totals)[:, :, None]
    return result_rows.reshape(row_count, D).astype(jnp.bfloat16)

def track_block(states, attended, counts, w_temporal, temporal_scale, w_merge, box_gain, w_hidden, b_hidden, w_box):
    track_rows = states.shape[0]
    list_length = attended.shape[1]
    model_width = states.shape[1]
    head_feature_width = model_width // HEADS
    residual_rows = states[:, None, :] + attended.astype(jnp.float32)
    normed = layer_norm(residual_rows).astype(jnp.bfloat16)
    projected = jnp.dot(normed.reshape(track_rows * list_length, model_width), w_temporal, preferred_element_type=jnp.float32).astype(jnp.bfloat16)
    projected = lax.optimization_barrier(projected)
    projected = projected.reshape(track_rows, list_length, 3, HEADS, head_feature_width).astype(jnp.float32)
    per_head_queries = projected[:, :, 0]
    per_head_keys = projected[:, :, 1]
    per_head_values = projected[:, :, 2]
    attention_scores = jnp.einsum('bqhd,bkhd->bhqk', per_head_queries, per_head_keys) * (temporal_scale[None, :, None, None] * head_feature_width ** (-0.5))
    positions = jnp.arange(list_length).astype(jnp.int32)
    key_valid = positions[None, :] < counts.astype(jnp.int32)[:, None]
    attention_scores = jnp.where(key_valid[:, None, None, :], attention_scores, masked_score)
    row_top = lax.optimization_barrier(jnp.max(attention_scores, axis=-1, keepdims=True))
    weights = jnp.exp(attention_scores - row_top)
    probs = (weights / lax.optimization_barrier(jnp.sum(weights, axis=-1, keepdims=True))).astype(jnp.bfloat16)
    probs = lax.optimization_barrier(probs).astype(jnp.float32)
    mixed_heads = jnp.einsum('bhqk,bkhd->bqhd', probs, per_head_values).astype(jnp.bfloat16)
    mixed_heads = mixed_heads.reshape(track_rows * list_length, model_width)
    updated = residual_rows + jnp.dot(mixed_heads, w_merge, preferred_element_type=jnp.float32).reshape(track_rows, list_length, model_width)
    row_valid = key_valid.astype(jnp.float32)[:, :, None]
    refined = (updated * row_valid).astype(jnp.bfloat16)
    box_input = (layer_norm(updated) * box_gain).astype(jnp.bfloat16)
    box_hidden = jax.nn.gelu(jnp.dot(box_input.reshape(track_rows * list_length, model_width), w_hidden, preferred_element_type=jnp.float32) + b_hidden).astype(jnp.bfloat16)
    box_values = jnp.dot(box_hidden, w_box, preferred_element_type=jnp.float32).reshape(track_rows, list_length, w_box.shape[1]) * row_valid
    return (refined, box_values)

def reference(track_embed, view_ids, view_count, key_feats, value_feats, track_gain, w_temporal, temporal_scale, w_merge, box_gain, w_hidden, b_hidden, w_box):
    tracks_total = track_embed.shape[0]
    states = layer_norm(track_embed.astype(jnp.float32)) * track_gain
    frame_ids = view_ids // CAMS
    queries = (states[:, None, :] + time_code(frame_ids, D)).astype(jnp.bfloat16)
    row_total = tracks_total * VMAX
    flat_queries = queries.reshape(row_total, D)
    flat_views = view_ids.reshape(row_total).astype(jnp.int32)
    per_view = CAP * N_TM * N_TRK
    view_total = FRAMES * CAMS

    def one_view(scan_carry, view_id):
        row_ids = jnp.nonzero(flat_views == view_id, size=per_view, fill_value=row_total)[0].astype(jnp.int32)
        frame_id = view_id // CAMS
        camera_id = view_id % CAMS
        neighbour = (camera_id + 1) % CAMS
        key_rows = jnp.concatenate([key_feats[frame_id, camera_id], key_feats[frame_id, neighbour]], axis=0)
        value_rows = jnp.concatenate([value_feats[frame_id, camera_id], value_feats[frame_id, neighbour]], axis=0)
        picked = jnp.take(flat_queries, row_ids, axis=0, mode='fill', fill_value=0)
        return (scan_carry, (row_ids, view_attention(picked, key_rows, value_rows)))
    scan_carry, outcome = lax.scan(one_view, jnp.int32(0), jnp.arange(view_total, dtype=jnp.int32))
    row_lists, results = outcome
    attended = jnp.zeros((row_total, D), jnp.bfloat16).at[row_lists.reshape(-1)].set(results.reshape(-1, D), mode='drop')
    blocks = tracks_total // TRK_DEV
    block_parts = (states.reshape(blocks, TRK_DEV, D), attended.reshape(blocks, TRK_DEV, VMAX, D), view_count.reshape(blocks, TRK_DEV))

    def one_block(parts_here):
        return track_block(parts_here[0], parts_here[1], parts_here[2], w_temporal, temporal_scale, w_merge, box_gain, w_hidden, b_hidden, w_box)
    refined, box_values = lax.map(one_block, block_parts)
    return (refined.reshape(tracks_total, VMAX, D), box_values.reshape(tracks_total, VMAX, BOX))
```

```python
import functools
import math

import jax
import jax.numpy as jnp
from jax import lax
from jax.experimental import pallas as pl
from jax.experimental.pallas import tpu as pltpu
from jax.sharding import PartitionSpec as P

HEADS = 8
CAMS = 8
CAP = 4
NX = 4
EPS = 1e-05
MASKED = -1e30
MESH = pl.DeviceIdType.MESH
BF = jnp.bfloat16
F32 = jnp.float32


def layer_norm(values):
    centre = jnp.mean(values, axis=-1, keepdims=True)
    shifted = values - centre
    spread = jnp.mean(shifted * shifted, axis=-1, keepdims=True)
    return shifted * lax.rsqrt(spread + EPS)


def time_code(frame_ids, model_width):
    half_width = model_width // 2
    freq_index = jnp.arange(half_width).astype(F32)
    freq_rates = jnp.exp(freq_index * (-2.0 * math.log(10000.0) / model_width))
    angles = frame_ids.astype(F32)[..., None] * freq_rates
    return jnp.concatenate([jnp.sin(angles), jnp.cos(angles)], axis=-1)


def iota(shape, dim):
    return lax.broadcasted_iota(jnp.int32, shape, dim)


def nt_dot(a, b):
    return lax.dot_general(a, b, (((1,), (1,)), ((), ())), preferred_element_type=F32)


def tn_dot(a, b):
    return lax.dot_general(a, b, (((0,), (0,)), ((), ())), preferred_element_type=F32)


def place(nt):
    tm = lax.axis_index("tm")
    trk = lax.axis_index("trk")
    z = tm // NX
    x = tm % NX
    return z, x, trk, x * nt + trk


def greet(nz, nt):
    z, x, trk, me = place(nt)
    npl = NX * nt
    barrier = pltpu.get_barrier_semaphore()

    @pl.loop(1, npl)
    def _(k):
        p = lax.rem(me + k, npl)
        pl.semaphore_signal(barrier, inc=1, device_id=(z * NX + p // nt, p % nt), device_id_type=MESH)

    @pl.loop(1, nz)
    def _(k):
        zz = lax.rem(z + k, nz)
        pl.semaphore_signal(barrier, inc=1, device_id=(zz * NX + x, trk), device_id_type=MESH)

    pl.semaphore_wait(barrier, npl - 1 + nz - 1)


def await_bytes(like, sem):
    pltpu.make_async_copy(like, like, sem).wait()


def forward_kernel(
    nz, nt, rows, cap_z,
    embed_ref, ids_ref, code_ref, gain_ref, key_ref, value_ref,
    q_ref, kn_ref, vn_ref, target_ref,
    emb_z, ids_z, q_send,
    z_send, z_recv, zi_send, zi_recv, kv_send, kv_recv, q_ssem, q_rsem, own_sem,
):
    z, x, trk, me = place(nt)
    npl = NX * nt
    width = embed_ref.shape[1]
    cols = nz * rows
    per = nz * CAP
    greet(nz, nt)

    before = (z * NX + x, lax.rem(trk + nt - 1, nt))
    k_copy = pltpu.make_async_remote_copy(
        src_ref=key_ref, dst_ref=kn_ref, send_sem=kv_send.at[0], recv_sem=kv_recv.at[0],
        device_id=before, device_id_type=MESH)
    v_copy = pltpu.make_async_remote_copy(
        src_ref=value_ref, dst_ref=vn_ref, send_sem=kv_send.at[1], recv_sem=kv_recv.at[1],
        device_id=before, device_id_type=MESH)

    own_e = pltpu.make_async_copy(embed_ref, emb_z.at[z], z_recv)
    own_i = pltpu.make_async_copy(ids_ref, ids_z.at[z], zi_recv)
    own_e.start()
    own_i.start()

    @pl.loop(1, nz)
    def _(k):
        zz = lax.rem(z + k, nz)
        to = (zz * NX + x, trk)
        pltpu.make_async_remote_copy(
            src_ref=ids_ref, dst_ref=ids_z.at[z], send_sem=zi_send, recv_sem=zi_recv,
            device_id=to, device_id_type=MESH).start()
        pltpu.make_async_remote_copy(
            src_ref=embed_ref, dst_ref=emb_z.at[z], send_sem=z_send, recv_sem=z_recv,
            device_id=to, device_id_type=MESH).start()

    k_copy.start()
    v_copy.start()

    await_bytes(ids_z, zi_recv)
    ids = ids_z[0]
    for s in range(1, nz):
        ids = jnp.maximum(ids, ids_z[s])
    listing = ids.shape[0]
    view = z * npl + iota((npl, cols), 0)
    named = jnp.zeros((npl, cols), F32)
    for j in range(listing):
        named = jnp.where(ids[j : j + 1, :] == view, 1.0, named)
    named_b = named.astype(BF)
    c0 = iota((cols, cols), 0)
    c1 = iota((cols, cols), 1)
    earlier = jnp.where((c0 < c1) & (c0 // rows == c1 // rows), 1.0, 0.0).astype(BF)
    rank = jnp.dot(named_b, earlier, preferred_element_type=F32)
    ranked = jnp.where(named > 0.5, rank, -1.0)

    zr = iota((per, cols), 0)
    zc = iota((per, cols), 1) // rows
    same_z = zr // CAP == zc
    slot_r = (zr % CAP).astype(F32)
    counts = nt_dot(jnp.where(same_z, 1.0, 0.0).astype(BF), named_b)
    v0 = iota((npl, npl), 0)
    v1 = iota((npl, npl), 1)
    base = jnp.dot(counts.astype(BF), jnp.where(v0 < v1, 1.0, 0.0).astype(BF), preferred_element_type=F32)
    t0 = iota((per, npl), 0)
    tr = (t0 % CAP).astype(F32)
    target_ref[...] = jnp.where(tr < counts, base + tr + ((t0 // CAP) * cap_z).astype(F32), -1.0)

    await_bytes(emb_z, z_recv)
    states = layer_norm(emb_z[...].reshape(cols, width).astype(F32)) * gain_ref[...]
    high = states.astype(BF)
    rest = states - high.astype(F32)
    middle = rest.astype(BF)
    low = (rest - middle.astype(F32)).astype(BF)

    group = 4
    for g in range(npl // group):
        picks = []
        for v in range(g * group, (g + 1) * group):
            picks.append(jnp.where(same_z & (ranked[v : v + 1, :] == slot_r), 1.0, 0.0).astype(BF))
        pick = jnp.concatenate(picks, axis=0)
        made = jnp.dot(pick, high, preferred_element_type=F32)
        made = made + jnp.dot(pick, middle, preferred_element_type=F32)
        made = made + jnp.dot(pick, low, preferred_element_type=F32)
        frame = (g * group) // nt
        made = (made + code_ref[frame : frame + 1, :]).astype(BF)
        q_send[g * group * per : (g + 1) * group * per, :] = made

    mine = pl.ds(pl.multiple_of(me * per, per), per)
    pltpu.make_async_copy(q_send.at[mine], q_ref.at[mine], q_rsem).start()

    @pl.loop(1, npl)
    def _(k):
        p = lax.rem(me + k, npl)
        pltpu.make_async_remote_copy(
            src_ref=q_send.at[pl.ds(pl.multiple_of(p * per, per), per)], dst_ref=q_ref.at[mine],
            send_sem=q_ssem, recv_sem=q_rsem,
            device_id=(z * NX + p // nt, p % nt), device_id_type=MESH).start()

    await_bytes(emb_z.at[pl.ds(0, nz - 1)], z_send)
    await_bytes(ids_z.at[pl.ds(0, nz - 1)], zi_send)
    await_bytes(q_send.at[pl.ds(0, (npl - 1) * per)], q_ssem)
    await_bytes(q_send, q_rsem)
    k_copy.wait()
    v_copy.wait()


def return_kernel(
    nz, nt, cap_z, pair,
    q_ref, k_ref, kn_ref, v_ref, vn_ref, target_ref,
    out_ref,
    a_send, a_recv, moves, b_send,
    a_ssem, a_rsem, b_ssem, b_rsem,
):
    z, x, trk, me = place(nt)
    npl = NX * nt
    per = nz * CAP
    total = npl * per
    tokens = k_ref.shape[0]
    head = 128
    chunks = HEADS // pair
    wide = pair * head
    scale = head ** (-0.5)
    mine = pl.ds(pl.multiple_of(me * per, per), per)
    block = 256
    greet(nz, nt)

    def attend(c):
        @pl.loop(0, total // block)
        def _(b):
            at = pl.ds(pl.multiple_of(b * block, block), block)
            for h in range(pair):
                lanes = slice((c * pair + h) * head, (c * pair + h + 1) * head)
                q = q_ref[at, lanes]
                s0 = nt_dot(q, k_ref[:, lanes])
                s1 = nt_dot(q, kn_ref[:, lanes])
                top = jnp.maximum(jnp.max(s0, axis=-1, keepdims=True), jnp.max(s1, axis=-1, keepdims=True))
                w0 = jnp.exp((s0 - top) * scale)
                w1 = jnp.exp((s1 - top) * scale)
                sums = jnp.sum(w0, axis=-1, keepdims=True) + jnp.sum(w1, axis=-1, keepdims=True)
                o = jnp.dot(w0.astype(BF), v_ref[:, lanes], preferred_element_type=F32)
                o = o + jnp.dot(w1.astype(BF), vn_ref[:, lanes], preferred_element_type=F32)
                a_send[c, at, h * head : (h + 1) * head] = (o / sums).astype(BF)

    def send_in_plane(c):
        pltpu.make_async_copy(a_send.at[c, mine], a_recv.at[c, mine], a_rsem.at[c]).start()

        @pl.loop(1, npl)
        def _(k):
            p = lax.rem(me + k, npl)
            pltpu.make_async_remote_copy(
                src_ref=a_send.at[c, pl.ds(pl.multiple_of(p * per, per), per)], dst_ref=a_recv.at[c, mine],
                send_sem=a_ssem.at[c], recv_sem=a_rsem.at[c],
                device_id=(z * NX + p // nt, p % nt), device_id_type=MESH).start()

    line = pl.ds(pl.multiple_of(z * cap_z, cap_z), cap_z)

    def send_along_z(c):
        await_bytes(a_recv.at[c], a_rsem.at[c])
        b_send[c] = tn_dot(moves[...], a_recv[c]).astype(BF)
        pltpu.make_async_copy(b_send.at[c, line], out_ref.at[c, line], b_rsem.at[c]).start()

        @pl.loop(1, nz)
        def _(k):
            zz = lax.rem(z + k, nz)
            pltpu.make_async_remote_copy(
                src_ref=b_send.at[c, pl.ds(pl.multiple_of(zz * cap_z, cap_z), cap_z)], dst_ref=out_ref.at[c, line],
                send_sem=b_ssem.at[c], recv_sem=b_rsem.at[c],
                device_id=(zz * NX + x, trk), device_id_type=MESH).start()

    for c in range(chunks):
        attend(c)
        send_in_plane(c)
        if c == 0:
            lane = iota((per, nz * cap_z), 1).astype(F32)
            for v in range(npl):
                moves[v * per : (v + 1) * per, :] = jnp.where(target_ref[:, v : v + 1] == lane, 1.0, 0.0).astype(BF)
        else:
            send_along_z(c - 1)
    send_along_z(chunks - 1)
    for c in range(chunks):
        await_bytes(a_send.at[c, pl.ds(0, (npl - 1) * per)], a_ssem.at[c])
        await_bytes(b_send.at[c, pl.ds(0, (nz - 1) * cap_z)], b_ssem.at[c])
        await_bytes(out_ref.at[c], b_rsem.at[c])


def track_kernel(
    chunks,
    back_ref, slot_ref, embed_ref, gain_ref, valid_ref, keys_ref, scale_ref,
    wt_ref, wm_ref, bgain_ref, wh_ref, bh_ref, wb_ref,
    refined_ref, box_ref,
    projected, mixed,
):
    rows, width = embed_ref.shape
    entries = slot_ref.shape[0]
    listing = entries // rows
    slots = back_ref.shape[1]
    pick = jnp.where(slot_ref[...] == iota((entries, slots), 1), 1.0, 0.0).astype(BF)
    attended = jnp.concatenate(
        [jnp.dot(pick, back_ref[c], preferred_element_type=F32) for c in range(chunks)], axis=1)
    states = layer_norm(embed_ref[...].astype(F32)) * gain_ref[...]
    states = jnp.broadcast_to(states[:, None, :], (rows, listing, width)).reshape(entries, width)
    residual = states + attended
    normed = layer_norm(residual).astype(BF)
    projected[...] = jnp.dot(normed, wt_ref[...], preferred_element_type=F32).astype(BF)
    block = 128
    head = width // HEADS
    same = iota((block, block), 0) // listing == iota((block, block), 1) // listing
    for b in range(entries // block):
        at = slice(b * block, (b + 1) * block)
        open_keys = same & (keys_ref[:, at] > 0.5)
        for h in range(HEADS):
            q = projected[at, h * head : (h + 1) * head]
            k = projected[at, width + h * head : width + (h + 1) * head]
            v = projected[at, 2 * width + h * head : 2 * width + (h + 1) * head]
            scores = nt_dot(q, k) * (scale_ref[0, h] * head ** (-0.5))
            scores = jnp.where(open_keys, scores, MASKED)
            weights = jnp.exp(scores - jnp.max(scores, axis=-1, keepdims=True))
            probs = (weights / jnp.sum(weights, axis=-1, keepdims=True)).astype(BF)
            mixed[at, h * head : (h + 1) * head] = jnp.dot(probs, v, preferred_element_type=F32).astype(BF)
    updated = residual + jnp.dot(mixed[...], wm_ref[...], preferred_element_type=F32)
    valid = valid_ref[...]
    refined_ref[...] = (updated * valid).astype(BF)
    box_input = (layer_norm(updated) * bgain_ref[...]).astype(BF)
    hidden = jax.nn.gelu(jnp.dot(box_input, wh_ref[...], preferred_element_type=F32) + bh_ref[...]).astype(BF)
    box_ref[...] = jnp.dot(hidden, wb_ref[...], preferred_element_type=F32) * valid


def local(
    track_embed, view_ids, view_count, key_feats, value_feats, track_gain, w_temporal,
    temporal_scale, w_merge, box_gain, w_hidden, b_hidden, w_box,
):
    tm_count = lax.axis_size("tm")
    nt = lax.axis_size("trk")
    nz = tm_count // NX
    npl = NX * nt
    rows, width = track_embed.shape
    listing = view_ids.shape[1]
    entries = rows * listing
    tokens = key_feats.shape[2]
    per = nz * CAP
    total = npl * per
    cap_z = npl * CAP
    pair = 2
    chunks = HEADS // pair
    z = lax.axis_index("tm") // NX

    valid = jnp.arange(listing, dtype=jnp.int32)[None, :] < view_count[:, None]
    shown = jnp.where(valid, view_ids, -1)
    turned = jnp.tile(shown.T, (1, nz))
    lane = jnp.arange(nz * rows, dtype=jnp.int32)[None, :]
    turned = jnp.where(lane // rows == z, turned, -1)
    codes = time_code(z * NX + jnp.arange(NX, dtype=jnp.int32), width)
    flat = (shown * rows + jnp.arange(rows, dtype=jnp.int32)[:, None]).reshape(entries)
    plane = flat // (npl * rows)
    ahead = (flat[None, :] < flat[:, None]) & (flat[None, :] >= (plane * (npl * rows))[:, None])
    slot = plane * cap_z + jnp.sum(ahead.astype(jnp.int32), axis=1)
    slot = jnp.where(valid.reshape(entries), slot, -1)[:, None]

    anywhere = pl.BlockSpec(memory_space=pl.ANY)
    vmem = pl.BlockSpec(memory_space=pltpu.VMEM)
    dma = pltpu.SemaphoreType.DMA
    gain = track_gain[None, :]
    keys = key_feats.reshape(tokens, width)
    values = value_feats.reshape(tokens, width)
    arrived, next_keys, next_values, target = pl.pallas_call(
        functools.partial(forward_kernel, nz, nt, rows, cap_z),
        out_shape=(
            jax.ShapeDtypeStruct((total, width), BF),
            jax.ShapeDtypeStruct((tokens, width), BF),
            jax.ShapeDtypeStruct((tokens, width), BF),
            jax.ShapeDtypeStruct((per, npl), F32),
        ),
        in_specs=[vmem, vmem, vmem, vmem, anywhere, anywhere],
        out_specs=(anywhere, anywhere, anywhere, vmem),
        scratch_shapes=[
            pltpu.VMEM((nz, rows, width), BF),
            pltpu.VMEM((nz, listing, nz * rows), jnp.int32),
            pltpu.VMEM((total, width), BF),
            dma, dma, dma, dma, dma((2,)), dma((2,)), dma, dma, dma,
        ],
        compiler_params=pltpu.CompilerParams(
            collective_id=0, has_side_effects=True, vmem_limit_bytes=40 * 1024 * 1024),
        name="forward",
    )(track_embed, turned, codes, gain, keys, values)

    back = pl.pallas_call(
        functools.partial(return_kernel, nz, nt, cap_z, pair),
        out_shape=jax.ShapeDtypeStruct((chunks, nz * cap_z, pair * 128), BF),
        in_specs=[vmem] * 6,
        out_specs=anywhere,
        scratch_shapes=[
            pltpu.VMEM((chunks, total, pair * 128), BF),
            pltpu.VMEM((chunks, total, pair * 128), BF),
            pltpu.VMEM((total, nz * cap_z), BF),
            pltpu.VMEM((chunks, nz * cap_z, pair * 128), BF),
            dma((chunks,)), dma((chunks,)), dma((chunks,)), dma((chunks,)),
        ],
        compiler_params=pltpu.CompilerParams(
            collective_id=1, has_side_effects=True, vmem_limit_bytes=48 * 1024 * 1024),
        name="attend_and_return",
    )(arrived, keys, next_keys, values, next_values, target)

    seen = valid.astype(F32)
    boxes_wide = w_box.shape[1]
    refined, boxes = pl.pallas_call(
        functools.partial(track_kernel, chunks),
        out_shape=(
            jax.ShapeDtypeStruct((entries, width), BF),
            jax.ShapeDtypeStruct((entries, boxes_wide), F32),
        ),
        in_specs=[vmem] * 6 + [pl.BlockSpec(memory_space=pltpu.SMEM)] + [vmem] * 6,
        out_specs=(vmem, vmem),
        scratch_shapes=[pltpu.VMEM((entries, 3 * width), BF), pltpu.VMEM((entries, width), BF)],
        compiler_params=pltpu.CompilerParams(vmem_limit_bytes=56 * 1024 * 1024),
        name="track",
    )(
        back, slot, track_embed, gain, seen.reshape(entries, 1), seen.reshape(1, entries), temporal_scale[None, :],
        w_temporal, w_merge, box_gain[None, :], w_hidden, b_hidden[None, :], w_box,
    )
    return refined.reshape(rows, listing, width), boxes.reshape(rows, listing, boxes_wide)


def solution(mesh):
    placed = (
        P(("tm", "trk"), None),
        P(("tm", "trk"), None),
        P(("tm", "trk")),
        P("tm", "trk", None, None),
        P("tm", "trk", None, None),
    ) + (P(),) * 8
    return jax.shard_map(
        local,
        mesh=mesh,
        in_specs=placed,
        out_specs=(P(("tm", "trk"), None, None), P(("tm", "trk"), None, None)),
        check_vma=False,
    )
```

```python
import functools
import math

import jax
import jax.numpy as jnp
from jax import lax
from jax.experimental import pallas as pl
from jax.experimental.pallas import tpu as pltpu
from jax.sharding import PartitionSpec as P

HEADS = 8
CAMS = 8
CAP = 4
NX = 4
EPS = 1e-05
MASKED = -1e30
MESH = pl.DeviceIdType.MESH
BF = jnp.bfloat16
F32 = jnp.float32


def layer_norm(values):
    centre = jnp.mean(values, axis=-1, keepdims=True)
    shifted = values - centre
    spread = jnp.mean(shifted * shifted, axis=-1, keepdims=True)
    return shifted * lax.rsqrt(spread + EPS)


def time_code(frame_ids, model_width):
    half_width = model_width // 2
    freq_index = jnp.arange(half_width).astype(F32)
    freq_rates = jnp.exp(freq_index * (-2.0 * math.log(10000.0) / model_width))
    angles = frame_ids.astype(F32)[..., None] * freq_rates
    return jnp.concatenate([jnp.sin(angles), jnp.cos(angles)], axis=-1)


def iota(shape, dim):
    return lax.broadcasted_iota(jnp.int32, shape, dim)


def nt_dot(a, b):
    return lax.dot_general(a, b, (((1,), (1,)), ((), ())), preferred_element_type=F32)


def tn_dot(a, b):
    return lax.dot_general(a, b, (((0,), (0,)), ((), ())), preferred_element_type=F32)


def place(nt):
    tm = lax.axis_index("tm")
    trk = lax.axis_index("trk")
    z = tm // NX
    x = tm % NX
    return z, x, trk, x * nt + trk


def greet(nz, nt):
    z, x, trk, me = place(nt)
    npl = NX * nt
    barrier = pltpu.get_barrier_semaphore()

    @pl.loop(1, npl)
    def _(k):
        p = lax.rem(me + k, npl)
        pl.semaphore_signal(barrier, inc=1, device_id=(z * NX + p // nt, p % nt), device_id_type=MESH)

    @pl.loop(1, nz)
    def _(k):
        zz = lax.rem(z + k, nz)
        pl.semaphore_signal(barrier, inc=1, device_id=(zz * NX + x, trk), device_id_type=MESH)

    pl.semaphore_wait(barrier, npl - 1 + nz - 1)


def await_bytes(like, sem):
    pltpu.make_async_copy(like, like, sem).wait()


def z_order(nz):
    near = [0]
    for k in range(1, nz // 2 + 1):
        near += [k] if 2 * k == nz else [k, nz - k]
    return near


def mega_kernel(
    nz, nt, rows, cap, chunks, block,
    embed_ref, ids_ref, code_ref, gain_ref, key_ref, value_ref,
    back_ref, kept_ref, target_ref, most_ref,
    emb_z, ids_z, q_send, q_recv, kn_ref, vn_ref, a_send, a_recv, moves, b_send, most_one, most_all,
    z_send, z_recv, zi_send, zi_recv, kv_send, kv_recv, q_ssem, q_rsem, a_ssem, a_rsem, b_ssem, b_rsem,
    most_ssem, most_rsem, keep_sem,
):
    z, x, trk, me = place(nt)
    npl = NX * nt
    width = embed_ref.shape[1]
    order = z_order(nz)
    half = nz // 2
    per = half * CAP
    gcols = half * rows
    cols = nz * rows
    grows = npl * per
    head = 128
    wide = width // chunks
    scale = head ** (-0.5) * math.log2(math.e)
    listing = ids_ref.shape[0] - 8
    mine = pl.ds(pl.multiple_of(me * per, per), per)
    line = pl.ds(pl.multiple_of(z * cap, cap), cap)
    greet(nz, nt)

    def part(p):
        return pl.ds(pl.multiple_of(p * per, per), per)

    def in_plane(copy_to):
        @pl.loop(1, npl)
        def _(k):
            p = lax.rem(me + k, npl)
            copy_to(p, (z * NX + lax.div(p, nt), lax.rem(p, nt)))

    own_e = pltpu.make_async_copy(embed_ref, emb_z.at[0], z_recv.at[0])
    own_e.start()
    own_i = pltpu.make_async_copy(ids_ref, ids_z.at[0], zi_recv)
    own_i.start()
    for k in order[1:]:
        to = (lax.rem(z + k, nz) * NX + x, trk)
        pltpu.make_async_remote_copy(
            src_ref=ids_ref, dst_ref=ids_z.at[order.index(nz - k)], send_sem=zi_send, recv_sem=zi_recv,
            device_id=to, device_id_type=MESH).start()
    for k in order[1:]:
        to = (lax.rem(z + k, nz) * NX + x, trk)
        i = order.index(nz - k)
        pltpu.make_async_remote_copy(
            src_ref=embed_ref, dst_ref=emb_z.at[i], send_sem=z_send, recv_sem=z_recv.at[i],
            device_id=to, device_id_type=MESH).start()

    before = (z * NX + x, lax.rem(trk + nt - 1, nt))
    k_copy = pltpu.make_async_remote_copy(
        src_ref=key_ref, dst_ref=kn_ref, send_sem=kv_send.at[0], recv_sem=kv_recv.at[0],
        device_id=before, device_id_type=MESH)
    v_copy = pltpu.make_async_remote_copy(
        src_ref=value_ref, dst_ref=vn_ref, send_sem=kv_send.at[1], recv_sem=kv_recv.at[1],
        device_id=before, device_id_type=MESH)
    k_copy.start()
    v_copy.start()

    await_bytes(ids_z, zi_recv)
    lane = iota((listing, cols), 1) // rows
    ids = ids_z[0, :listing, :]
    most = ids_z[0, listing:, :128]
    for i in range(1, nz):
        ids = jnp.where(lane == i, ids_z[i, :listing, :], ids)
        most = jnp.maximum(most, ids_z[i, listing:, :128])
    most_one[...] = most
    pltpu.make_async_copy(most_one, most_all.at[me], most_rsem).start()
    in_plane(lambda p, to: pltpu.make_async_remote_copy(
        src_ref=most_one, dst_ref=most_all.at[me], send_sem=most_ssem, recv_sem=most_rsem,
        device_id=to, device_id_type=MESH).start())

    view = z * npl + iota((npl, cols), 0)
    named = jnp.zeros((npl, cols), F32)
    for j in range(listing):
        named = jnp.where(ids[j : j + 1, :] == view, 1.0, named)
    named_b = named.astype(BF)
    c0 = iota((cols, cols), 0)
    c1 = iota((cols, cols), 1)
    earlier = jnp.where((c0 < c1) & (c0 // rows == c1 // rows), 1.0, 0.0).astype(BF)
    rank = jnp.dot(named_b, earlier, preferred_element_type=F32)
    ranked = jnp.where(named > 0.5, rank, -1.0)

    same_z = iota((per, gcols), 0) // CAP == iota((per, gcols), 1) // rows
    slot_r = (iota((per, gcols), 0) % CAP).astype(F32)
    v0 = iota((npl, npl), 0)
    v1 = iota((npl, npl), 1)
    before_v = jnp.where(v0 < v1, 1.0, 0.0).astype(BF)
    t0 = iota((per, npl), 0)
    tr = (t0 % CAP).astype(F32)
    for g in range(2):
        counts = nt_dot(jnp.where(same_z, 1.0, 0.0).astype(BF), named_b[:, g * gcols : (g + 1) * gcols])
        base = jnp.dot(counts.astype(BF), before_v, preferred_element_type=F32)
        target_ref[g] = jnp.where(tr < counts, base + tr, -1.0)

    for g in range(2):
        for i in range(g * half, (g + 1) * half):
            await_bytes(emb_z.at[i], z_recv.at[i])
        states = emb_z[g * half : (g + 1) * half].reshape(gcols, width).astype(F32)
        states = layer_norm(states) * gain_ref[...]
        high = states.astype(BF)
        rest = states - high.astype(F32)
        middle = rest.astype(BF)
        low = (rest - middle.astype(F32)).astype(BF)
        parts = jnp.concatenate([high, middle, low], axis=0)
        picks = []
        for v in range(npl):
            here = ranked[v : v + 1, g * gcols : (g + 1) * gcols]
            picks.append(jnp.where(same_z & (here == slot_r), 1.0, 0.0).astype(BF))
        pick = jnp.concatenate(picks, axis=0)
        pick = jnp.concatenate([pick, pick, pick], axis=1)
        made = jnp.dot(pick, parts, preferred_element_type=F32)
        frow = grows // NX
        for f in range(NX):
            at = slice(f * frow, (f + 1) * frow)
            q_send[g, at] = (made[at] + code_ref[f : f + 1, :]).astype(BF)
        pltpu.make_async_copy(q_send.at[g, mine], q_recv.at[g, mine], q_rsem.at[g]).start()
        in_plane(lambda p, to: pltpu.make_async_remote_copy(
            src_ref=q_send.at[g, part(p)], dst_ref=q_recv.at[g, mine],
            send_sem=q_ssem.at[g], recv_sem=q_rsem.at[g], device_id=to, device_id_type=MESH).start())

    def attend(g, c):
        @pl.loop(0, grows // block)
        def _(b):
            at = pl.ds(pl.multiple_of(b * block, block), block)
            for h in range(wide // head):
                lanes = slice(c * wide + h * head, c * wide + (h + 1) * head)
                q = q_recv[g, at, lanes]
                s0 = nt_dot(q, key_ref[:, lanes])
                s1 = nt_dot(q, kn_ref[:, lanes])
                top = jnp.maximum(jnp.max(s0, axis=-1, keepdims=True), jnp.max(s1, axis=-1, keepdims=True))
                w0 = jnp.exp2((s0 - top) * scale)
                w1 = jnp.exp2((s1 - top) * scale)
                sums = jnp.sum(w0, axis=-1, keepdims=True) + jnp.sum(w1, axis=-1, keepdims=True)
                o = jnp.dot(w0.astype(BF), value_ref[:, lanes], preferred_element_type=F32)
                o = o + jnp.dot(w1.astype(BF), vn_ref[:, lanes], preferred_element_type=F32)
                a_send[g * chunks + c, at, h * head : (h + 1) * head] = (o / sums).astype(BF)

    def send_in_plane(n):
        pltpu.make_async_copy(a_send.at[n, mine], a_recv.at[n, mine], a_rsem.at[n]).start()
        in_plane(lambda p, to: pltpu.make_async_remote_copy(
            src_ref=a_send.at[n, part(p)], dst_ref=a_recv.at[n, mine],
            send_sem=a_ssem.at[n], recv_sem=a_rsem.at[n], device_id=to, device_id_type=MESH).start())

    def send_along_z(n):
        g, c = n // chunks, n % chunks
        await_bytes(a_recv.at[n], a_rsem.at[n])
        pltpu.make_async_copy(a_recv.at[n], kept_ref.at[n], keep_sem.at[n]).start()
        b_send[n] = tn_dot(moves[g], a_recv[n]).astype(BF)
        for i in range(half):
            dz = order[g * half + i]
            src = b_send.at[n, pl.ds(i * cap, cap)]
            if dz == 0:
                pltpu.make_async_copy(src, back_ref.at[c, line], b_rsem.at[n]).start()
            else:
                pltpu.make_async_remote_copy(
                    src_ref=src, dst_ref=back_ref.at[c, line], send_sem=b_ssem.at[n], recv_sem=b_rsem.at[n],
                    device_id=(lax.rem(z + dz, nz) * NX + x, trk), device_id_type=MESH).start()

    k_copy.wait()
    v_copy.wait()
    for n in range(2 * chunks):
        g, c = n // chunks, n % chunks
        if c == 0:
            await_bytes(q_recv.at[g], q_rsem.at[g])
        attend(g, c)
        send_in_plane(n)
        if n == 0:
            goal = iota((per, half * cap), 1)
            goal_z = iota((per, half * cap), 0) // CAP == goal // cap
            goal_at = (goal % cap).astype(F32)
            for gg in range(2):
                for v in range(npl):
                    hit = goal_z & (target_ref[gg, :, v : v + 1] == goal_at)
                    moves[gg, v * per : (v + 1) * per, :] = jnp.where(hit, 1.0, 0.0).astype(BF)
        else:
            send_along_z(n - 1)
    send_along_z(2 * chunks - 1)

    await_bytes(emb_z.at[pl.ds(0, nz - 1)], z_send)
    await_bytes(ids_z.at[pl.ds(0, nz - 1)], zi_send)
    await_bytes(most_all.at[pl.ds(0, npl - 1)], most_ssem)
    await_bytes(most_all, most_rsem)
    most_ref[...] = jnp.max(most_all[...], axis=0)
    for g in range(2):
        await_bytes(q_send.at[g, pl.ds(0, (npl - 1) * per)], q_ssem.at[g])
    for n in range(2 * chunks):
        remote = sum(1 for i in range(half) if order[n // chunks * half + i] != 0)
        await_bytes(a_send.at[n, pl.ds(0, (npl - 1) * per)], a_ssem.at[n])
        await_bytes(b_send.at[n, pl.ds(0, remote * cap)], b_ssem.at[n])
        await_bytes(back_ref.at[0, pl.ds(0, half * cap)], b_rsem.at[n])
        await_bytes(kept_ref.at[n], keep_sem.at[n])


def rest_kernel(
    nz, nt, cap, chunks,
    kept_ref, target_ref,
    back_ref,
    kept, moves, b_send, load_sem, b_ssem, b_rsem,
):
    z, x, trk, me = place(nt)
    npl = NX * nt
    order = z_order(nz)
    half = nz // 2
    per = half * CAP
    line = pl.ds(pl.multiple_of(z * cap, cap), cap)
    greet(nz, nt)
    load = pltpu.make_async_copy(kept_ref, kept, load_sem)
    load.start()
    load.wait()
    goal = iota((per, half * cap), 1)
    goal_z = iota((per, half * cap), 0) // CAP == goal // cap
    goal_at = (goal % cap + cap).astype(F32)
    for g in range(2):
        for v in range(npl):
            hit = goal_z & (target_ref[g, :, v : v + 1] == goal_at)
            moves[g, v * per : (v + 1) * per, :] = jnp.where(hit, 1.0, 0.0).astype(BF)
    for n in range(2 * chunks):
        g, c = n // chunks, n % chunks
        b_send[n] = tn_dot(moves[g], kept[n]).astype(BF)
        for i in range(half):
            dz = order[g * half + i]
            src = b_send.at[n, pl.ds(i * cap, cap)]
            if dz == 0:
                pltpu.make_async_copy(src, back_ref.at[c, line], b_rsem.at[n]).start()
            else:
                pltpu.make_async_remote_copy(
                    src_ref=src, dst_ref=back_ref.at[c, line], send_sem=b_ssem.at[n], recv_sem=b_rsem.at[n],
                    device_id=(lax.rem(z + dz, nz) * NX + x, trk), device_id_type=MESH).start()
    for n in range(2 * chunks):
        remote = sum(1 for i in range(half) if order[n // chunks * half + i] != 0)
        await_bytes(b_send.at[n, pl.ds(0, remote * cap)], b_ssem.at[n])
        await_bytes(back_ref.at[0, pl.ds(0, half * cap)], b_rsem.at[n])


def track_kernel(
    chunks, lists, cap, *refs,
):
    backs, refs = refs[:lists], refs[lists:]
    (
        slot_ref, embed_ref, gain_ref, valid_ref, keys_ref, scale_ref,
        wt_ref, wm_ref, bgain_ref, wh_ref, bh_ref, wb_ref,
        refined_ref, box_ref,
        projected, mixed,
    ) = refs
    rows, width = embed_ref.shape
    entries = slot_ref.shape[0]
    listing = entries // rows
    slots = backs[0].shape[1]
    column = iota((entries, slots), 1)
    attended = 0.0
    for k in range(lists):
        sought = (column // cap) * (CAP * NX * CAMS) + column % cap + k * cap
        pick = jnp.where(slot_ref[...] == sought, 1.0, 0.0).astype(BF)
        attended = attended + jnp.concatenate(
            [jnp.dot(pick, backs[k][c], preferred_element_type=F32) for c in range(chunks)], axis=1)
    states = layer_norm(embed_ref[...].astype(F32)) * gain_ref[...]
    states = jnp.broadcast_to(states[:, None, :], (rows, listing, width)).reshape(entries, width)
    residual = states + attended
    normed = layer_norm(residual).astype(BF)
    projected[...] = jnp.dot(normed, wt_ref[...], preferred_element_type=F32).astype(BF)
    block = 128
    head = width // HEADS
    same = iota((block, block), 0) // listing == iota((block, block), 1) // listing
    for b in range(entries // block):
        at = slice(b * block, (b + 1) * block)
        open_keys = same & (keys_ref[:, at] > 0.5)
        for h in range(HEADS):
            q = projected[at, h * head : (h + 1) * head]
            k = projected[at, width + h * head : width + (h + 1) * head]
            v = projected[at, 2 * width + h * head : 2 * width + (h + 1) * head]
            scores = nt_dot(q, k) * (scale_ref[0, h] * head ** (-0.5))
            scores = jnp.where(open_keys, scores, MASKED)
            weights = jnp.exp(scores - jnp.max(scores, axis=-1, keepdims=True))
            probs = (weights / jnp.sum(weights, axis=-1, keepdims=True)).astype(BF)
            mixed[at, h * head : (h + 1) * head] = jnp.dot(probs, v, preferred_element_type=F32).astype(BF)
    updated = residual + jnp.dot(mixed[...], wm_ref[...], preferred_element_type=F32)
    valid = valid_ref[...]
    refined_ref[...] = (updated * valid).astype(BF)
    box_input = (layer_norm(updated) * bgain_ref[...]).astype(BF)
    hidden = jax.nn.gelu(jnp.dot(box_input, wh_ref[...], preferred_element_type=F32) + bh_ref[...]).astype(BF)
    box_ref[...] = jnp.dot(hidden, wb_ref[...], preferred_element_type=F32) * valid


def local(
    track_embed, view_ids, view_count, key_feats, value_feats, track_gain, w_temporal,
    temporal_scale, w_merge, box_gain, w_hidden, b_hidden, w_box,
):
    tm_count = lax.axis_size("tm")
    nt = lax.axis_size("trk")
    nz = tm_count // NX
    npl = NX * nt
    rows, width = track_embed.shape
    listing = view_ids.shape[1]
    entries = rows * listing
    tokens = key_feats.shape[2]
    per = nz * CAP
    total = npl * per
    longest = npl * CAP
    cap = longest // 2
    chunks = 2
    z = lax.axis_index("tm") // NX

    valid = jnp.arange(listing, dtype=jnp.int32)[None, :] < view_count[:, None]
    shown = jnp.where(valid, view_ids, -1)
    codes = time_code(z * NX + jnp.arange(NX, dtype=jnp.int32), width)
    flat = (shown * rows + jnp.arange(rows, dtype=jnp.int32)[:, None]).reshape(entries)
    plane = flat // (npl * rows)
    ahead = (flat[None, :] < flat[:, None]) & (flat[None, :] >= (plane * (npl * rows))[:, None])
    slot = plane * longest + jnp.sum(ahead.astype(jnp.int32), axis=1)
    slot = jnp.where(valid.reshape(entries), slot, -1)[:, None]

    in_plane_of = jnp.arange(nz, dtype=jnp.int32)
    crowd = jnp.max(jnp.sum((plane[None, :] == in_plane_of[:, None]).astype(jnp.int32), axis=1))
    turned = jnp.concatenate(
        [jnp.tile(shown.T, (1, nz)), jnp.broadcast_to(crowd, (8, nz * rows))], axis=0)

    anywhere = pl.BlockSpec(memory_space=pl.ANY)
    vmem = pl.BlockSpec(memory_space=pltpu.VMEM)
    dma = pltpu.SemaphoreType.DMA
    gain = track_gain[None, :]
    keys = key_feats.reshape(tokens, width)
    values = value_feats.reshape(tokens, width)
    count = 2 * chunks
    wide = width // chunks
    per = nz // 2 * CAP
    grows = npl * per
    back, kept, target, most = pl.pallas_call(
        functools.partial(mega_kernel, nz, nt, rows, cap, chunks, 256),
        out_shape=(
            jax.ShapeDtypeStruct((chunks, nz * cap, wide), BF),
            jax.ShapeDtypeStruct((count, grows, wide), BF),
            jax.ShapeDtypeStruct((2, per, npl), F32),
            jax.ShapeDtypeStruct((8, 128), jnp.int32),
        ),
        in_specs=[vmem] * 6,
        out_specs=(anywhere, anywhere, vmem, vmem),
        scratch_shapes=[
            pltpu.VMEM((nz, rows, width), BF),
            pltpu.VMEM((nz, listing + 8, nz * rows), jnp.int32),
            pltpu.VMEM((2, grows, width), BF),
            pltpu.VMEM((2, grows, width), BF),
            pltpu.VMEM((tokens, width), BF),
            pltpu.VMEM((tokens, width), BF),
            pltpu.VMEM((count, grows, wide), BF),
            pltpu.VMEM((count, grows, wide), BF),
            pltpu.VMEM((2, grows, nz // 2 * cap), BF),
            pltpu.VMEM((count, nz // 2 * cap, wide), BF),
            pltpu.VMEM((8, 128), jnp.int32),
            pltpu.VMEM((npl, 8, 128), jnp.int32),
            dma, dma((nz,)), dma, dma, dma((2,)), dma((2,)), dma((2,)), dma((2,)),
            dma((count,)), dma((count,)), dma((count,)), dma((count,)), dma, dma, dma((count,)),
        ],
        compiler_params=pltpu.CompilerParams(
            collective_id=0, has_side_effects=True, vmem_limit_bytes=52 * 1024 * 1024),
        name="mega",
    )(track_embed, turned, codes, gain, keys, values)

    seen = valid.astype(F32)
    boxes_wide = w_box.shape[1]
    shared = (
        slot, track_embed, gain, seen.reshape(entries, 1), seen.reshape(1, entries), temporal_scale[None, :],
        w_temporal, w_merge, box_gain[None, :], w_hidden, b_hidden[None, :], w_box,
    )

    def finish(*backs):
        return pl.pallas_call(
            functools.partial(track_kernel, chunks, len(backs), cap),
            out_shape=(
                jax.ShapeDtypeStruct((entries, width), BF),
                jax.ShapeDtypeStruct((entries, boxes_wide), F32),
            ),
            in_specs=[vmem] * (len(backs) + 5) + [pl.BlockSpec(memory_space=pltpu.SMEM)] + [vmem] * 6,
            out_specs=(vmem, vmem),
            scratch_shapes=[pltpu.VMEM((entries, 3 * width), BF), pltpu.VMEM((entries, width), BF)],
            compiler_params=pltpu.CompilerParams(vmem_limit_bytes=56 * 1024 * 1024),
            name="track",
        )(*backs, *shared)

    def finish_long():
        rest = pl.pallas_call(
            functools.partial(rest_kernel, nz, nt, cap, chunks),
            out_shape=jax.ShapeDtypeStruct((chunks, nz * cap, wide), BF),
            in_specs=[anywhere, vmem],
            out_specs=anywhere,
            scratch_shapes=[
                pltpu.VMEM((count, grows, wide), BF),
                pltpu.VMEM((2, grows, nz // 2 * cap), BF),
                pltpu.VMEM((count, nz // 2 * cap, wide), BF),
                dma, dma((count,)), dma((count,)),
            ],
            compiler_params=pltpu.CompilerParams(
                collective_id=1, has_side_effects=True, vmem_limit_bytes=32 * 1024 * 1024),
            name="rest",
        )(kept, target)
        return finish(back, rest)

    refined, boxes = lax.cond(most[0, 0] > cap, finish_long, lambda: finish(back))
    return refined.reshape(rows, listing, width), boxes.reshape(rows, listing, boxes_wide)


def solution(mesh):
    placed = (
        P(("tm", "trk"), None),
        P(("tm", "trk"), None),
        P(("tm", "trk")),
        P("tm", "trk", None, None),
        P("tm", "trk", None, None),
    ) + (P(),) * 8
    return jax.shard_map(
        local,
        mesh=mesh,
        in_specs=placed,
        out_specs=(P(("tm", "trk"), None, None), P(("tm", "trk"), None, None)),
        check_vma=False,
    )
```

```python
import functools
import math

import jax
import jax.numpy as jnp
from jax import lax
from jax.experimental import pallas as pl
from jax.experimental.pallas import tpu as pltpu
from jax.sharding import PartitionSpec as P

HEADS = 8
CAMS = 8
CAP = 4
CORES = 2
NX = 4
EPS = 1e-05
MASKED = -1e30
MESH = pl.DeviceIdType.MESH
BF = jnp.bfloat16
F32 = jnp.float32


def layer_norm(values):
    centre = jnp.mean(values, axis=-1, keepdims=True)
    shifted = values - centre
    spread = jnp.mean(shifted * shifted, axis=-1, keepdims=True)
    return shifted * lax.rsqrt(spread + EPS)


def time_code(frame_ids, model_width):
    half_width = model_width // 2
    freq_index = jnp.arange(half_width).astype(F32)
    freq_rates = jnp.exp(freq_index * (-2.0 * math.log(10000.0) / model_width))
    angles = frame_ids.astype(F32)[..., None] * freq_rates
    return jnp.concatenate([jnp.sin(angles), jnp.cos(angles)], axis=-1)


def iota(shape, dim):
    return lax.broadcasted_iota(jnp.int32, shape, dim)


def nt_dot(a, b):
    return lax.dot_general(a, b, (((1,), (1,)), ((), ())), preferred_element_type=F32)


def tn_dot(a, b):
    return lax.dot_general(a, b, (((0,), (0,)), ((), ())), preferred_element_type=F32)


def place(nt):
    tm = lax.axis_index("tm")
    trk = lax.axis_index("trk")
    z = tm // NX
    x = tm % NX
    return z, x, trk, x * nt + trk


def greet(nz, nt):
    z, x, trk, me = place(nt)
    npl = NX * nt
    barrier = pltpu.get_barrier_semaphore()

    @pl.loop(1, npl)
    def _(k):
        p = lax.rem(me + k, npl)
        pl.semaphore_signal(barrier, inc=1, device_id=(z * NX + p // nt, p % nt), device_id_type=MESH)

    @pl.loop(1, nz)
    def _(k):
        zz = lax.rem(z + k, nz)
        pl.semaphore_signal(barrier, inc=1, device_id=(zz * NX + x, trk), device_id_type=MESH)

    pl.semaphore_wait(barrier, npl - 1 + nz - 1)


def await_bytes(like, sem):
    pltpu.make_async_copy(like, like, sem).wait()


def z_order(nz):
    near = [0]
    for k in range(1, nz // 2 + 1):
        near += [k] if 2 * k == nz else [k, nz - k]
    return near


def mega_kernel(
    nz, nt, rows, cap, chunks, block,
    embed_ref, ids_ref, code_ref, gain_ref, key_ref, value_ref,
    back_ref, kept_ref, target_ref, most_ref,
    emb_z, ids_y, ids_z, q_send, q_recv, kk_ref, vv_ref, a_send, a_recv, moves, b_send, most_one, most_all,
    y_send, y_recv, yi_send, yi_recv, z_send, z_recv, zi_send, zi_recv, kv_own, kv_send, kv_recv,
    q_ssem, q_rsem, a_ssem, a_rsem, b_ssem, b_rsem, most_ssem, most_rsem, keep_sem,
):
    z, x, trk, me = place(nt)
    y, core = trk // CORES, trk % CORES
    ny = nt // CORES
    npl = NX * nt
    nx = NX * CORES
    me_x = x * CORES + core
    width = embed_ref.shape[1]
    tokens = key_ref.shape[0]
    order = z_order(nz)
    half = nz // 2
    per = half * CAP
    lot = ny * per
    lanes = ny * rows
    grows = npl * per
    head = 128
    wide = width // chunks
    scale = head ** (-0.5) * math.log2(math.e)
    listing = ids_ref.shape[0] - 8
    mine = pl.ds(pl.multiple_of(me * per, per), per)
    line = pl.ds(pl.multiple_of(z * cap, cap), cap)
    greet(nz, nt)

    own_e = pltpu.make_async_copy(embed_ref, emb_z.at[0, 0], y_recv)
    own_e.start()
    own_i = pltpu.make_async_copy(ids_ref, ids_y.at[0], yi_recv)
    own_i.start()
    for k in range(1, ny):
        to = (z * NX + x, lax.rem(y + k, ny) * CORES + core)
        pltpu.make_async_remote_copy(
            src_ref=ids_ref, dst_ref=ids_y.at[ny - k], send_sem=yi_send, recv_sem=yi_recv,
            device_id=to, device_id_type=MESH).start()
    for k in range(1, ny):
        to = (z * NX + x, lax.rem(y + k, ny) * CORES + core)
        pltpu.make_async_remote_copy(
            src_ref=embed_ref, dst_ref=emb_z.at[0, ny - k], send_sem=y_send, recv_sem=y_recv,
            device_id=to, device_id_type=MESH).start()

    before = (z * NX + x, lax.rem(trk + nt - 1, nt))
    first, second = pl.ds(0, tokens), pl.ds(tokens, tokens)
    copies = []
    for i, (own, both) in enumerate(((key_ref, kk_ref), (value_ref, vv_ref))):
        copies.append(pltpu.make_async_copy(own, both.at[first], kv_own.at[i]))
        copies.append(pltpu.make_async_remote_copy(
            src_ref=own, dst_ref=both.at[second], send_sem=kv_send.at[i], recv_sem=kv_recv.at[i],
            device_id=before, device_id_type=MESH))

    await_bytes(ids_y, yi_recv)
    lane = iota(ids_y.shape[1:], 1) // rows
    ids = ids_y[0]
    most = ids_y[0, listing:, :]
    for i in range(1, ny):
        ids = jnp.where(lane == i, ids_y[i], ids)
        most = jnp.maximum(most, ids_y[i, listing:, :])
    ids_z[0, :listing, :] = ids[:listing]
    ids_z[0, listing:, :] = most
    await_bytes(emb_z.at[0], y_recv)

    def to_z(source, step, part=None):
        target = (source - step) % nz
        device = (lax.rem(z + nz + step, nz) * NX + x, trk)
        if part is None or part == 0:
            pltpu.make_async_remote_copy(
                src_ref=ids_z.at[source], dst_ref=ids_z.at[target], send_sem=zi_send, recv_sem=zi_recv.at[target],
                device_id=device, device_id_type=MESH).start()
        src, dst = emb_z.at[source], emb_z.at[target]
        if part is not None:
            few = pl.ds(part * (ny // 2), ny // 2)
            src, dst = emb_z.at[source, few], emb_z.at[target, few]
        pltpu.make_async_remote_copy(
            src_ref=src, dst_ref=dst, send_sem=z_send, recv_sem=z_recv.at[target],
            device_id=device, device_id_type=MESH).start()

    def arrive(slot):
        await_bytes(ids_z.at[slot], zi_recv.at[slot])
        await_bytes(emb_z.at[slot], z_recv.at[slot])

    to_z(0, 1)
    to_z(0, -1)
    for copy in copies:
        copy.start()

    view_x = iota((nx, lanes), 0)
    view_x = (z * NX + view_x // CORES) * nt + y * CORES + view_x % CORES
    view_p = z * npl + iota((npl, lanes), 0)
    c0 = iota((lanes, lanes), 0)
    c1 = iota((lanes, lanes), 1)
    earlier = jnp.where((c0 < c1) & (c0 // rows == c1 // rows), 1.0, 0.0).astype(BF)
    lane_at = iota((nx, lanes), 1) // rows
    slot_row = iota((per, lanes), 0)
    same_z = slot_row // CAP == iota((per, lanes), 1) // rows
    slot_r = (slot_row % CAP).astype(F32)
    own_lane = iota((per, lanes), 1) < rows
    v0 = iota((npl, npl), 0)
    v1 = iota((npl, npl), 1)
    before_v = jnp.where(v0 < v1, 1.0, 0.0).astype(BF)
    tr = (iota((per, npl), 0) % CAP).astype(F32)

    def names(ids, view):
        named = jnp.zeros(view.shape, F32)
        for j in range(listing):
            named = jnp.where(ids[j : j + 1, :] == view, 1.0, named)
        return named

    def build(g):
        slots = order[g * half : (g + 1) * half]
        ranked, parts = [], []
        counts = jnp.zeros((per, npl), F32)
        for i, slot in enumerate(slots):
            ids = ids_z[slot, :listing, :]
            named = names(ids, view_x)
            rank = jnp.dot(named.astype(BF), earlier, preferred_element_type=F32)
            ranked.append(jnp.where(named > 0.5, rank, -1.0))
            here = jnp.where((slot_row // CAP == i) & own_lane, 1.0, 0.0).astype(BF)
            counts = counts + nt_dot(here, names(ids, view_p).astype(BF))
            states = layer_norm(emb_z[slot].reshape(lanes, width).astype(F32)) * gain_ref[...]
            high = states.astype(BF)
            rest = states - high.astype(F32)
            middle = rest.astype(BF)
            low = (rest - middle.astype(F32)).astype(BF)
            parts.append((high, middle, low))
        base = jnp.dot(counts.astype(BF), before_v, preferred_element_type=F32)
        target_ref[g] = jnp.where(tr < counts, base + tr, -1.0)
        for dy in range(ny):
            here = jnp.zeros((nx, lanes), F32)
            for i in range(half):
                shift = (i - dy) * rows % lanes
                moved = pltpu.roll(ranked[i], shift, 1) if shift else ranked[i]
                here = jnp.where(lane_at == i, moved, here)
            picks = [jnp.where(same_z & (here[v : v + 1, :] == slot_r), 1.0, 0.0).astype(BF) for v in range(nx)]
            pick = jnp.concatenate(picks, axis=0)
            pick = jnp.concatenate([pick, pick, pick], axis=1)
            at = slice(dy * rows, (dy + 1) * rows)
            source = jnp.concatenate([parts[i][k][at] for k in range(3) for i in range(half)], axis=0)
            made = jnp.dot(pick, source, preferred_element_type=F32)
            for v in range(nx):
                f = v // CORES
                one = made[v * per : (v + 1) * per] + code_ref[f : f + 1, :]
                q_send[g, v * lot + dy * per : v * lot + (dy + 1) * per, :] = one.astype(BF)
        block_x = pl.ds(pl.multiple_of(me_x * lot, lot), lot)
        pltpu.make_async_copy(q_send.at[g, block_x], q_recv.at[g, block_x], q_rsem.at[g]).start()
        for k in range(1, nx):
            p = lax.rem(me_x + k, nx)
            pltpu.make_async_remote_copy(
                src_ref=q_send.at[g, pl.ds(pl.multiple_of(p * lot, lot), lot)], dst_ref=q_recv.at[g, block_x],
                send_sem=q_ssem.at[g], recv_sem=q_rsem.at[g],
                device_id=(z * NX + lax.div(p, CORES), y * CORES + lax.rem(p, CORES)), device_id_type=MESH).start()

    for k in range(1, half):
        arrive(nz - k)
        if k < half - 1:
            to_z(nz - k, 1)
        else:
            to_z(nz - k, 1, 0)
        arrive(k)
        if k < half - 1:
            to_z(k, -1)
        else:
            to_z(k, -1, 1)
        if k == 2:
            build(0)
    arrive(half)
    build(1)

    most = ids_z[0, listing:, :]
    for i in range(1, nz):
        most = jnp.maximum(most, ids_z[i, listing:, :])
    most_one[...] = most
    pltpu.make_async_copy(most_one, most_all.at[me_x], most_rsem).start()
    for k in range(1, nx):
        p = lax.rem(me_x + k, nx)
        pltpu.make_async_remote_copy(
            src_ref=most_one, dst_ref=most_all.at[me_x], send_sem=most_ssem, recv_sem=most_rsem,
            device_id=(z * NX + lax.div(p, CORES), y * CORES + lax.rem(p, CORES)), device_id_type=MESH).start()

    def attend(g, c):
        def score(at, h):
            some = slice(c * wide + h * head, c * wide + (h + 1) * head)
            return nt_dot(q_recv[g, at, some], kk_ref[:, some])

        @pl.loop(0, grows // block)
        def _(b):
            at = pl.ds(pl.multiple_of(b * block, block), block)
            ahead = score(at, 0)
            for h in range(wide // head):
                scores = ahead
                if h + 1 < wide // head:
                    ahead = score(at, h + 1)
                top = jnp.max(scores, axis=-1, keepdims=True)
                weights = jnp.exp2((scores - top) * scale)
                sums = jnp.sum(weights, axis=-1, keepdims=True)
                some = slice(c * wide + h * head, c * wide + (h + 1) * head)
                o = jnp.dot(weights.astype(BF), vv_ref[:, some], preferred_element_type=F32)
                a_send[g * chunks + c, at, h * head : (h + 1) * head] = (o / sums).astype(BF)

    def rows_of(px, dy):
        return pl.ds(pl.multiple_of(px * lot + dy * per, per), per)

    def send_in_plane(n):
        pltpu.make_async_copy(a_send.at[n, rows_of(me_x, 0)], a_recv.at[n, mine], a_rsem.at[n]).start()

        @pl.loop(1, npl)
        def _(k):
            p = lax.rem(me + k, npl)
            px, pt = lax.div(p, nt), lax.rem(p, nt)
            dy = lax.rem(lax.div(pt, CORES) + ny - y, ny)
            pltpu.make_async_remote_copy(
                src_ref=a_send.at[n, rows_of(px * CORES + lax.rem(pt, CORES), dy)], dst_ref=a_recv.at[n, mine],
                send_sem=a_ssem.at[n], recv_sem=a_rsem.at[n],
                device_id=(z * NX + px, pt), device_id_type=MESH).start()

    def send_along_z(n):
        g, c = n // chunks, n % chunks
        await_bytes(a_recv.at[n], a_rsem.at[n])
        pltpu.make_async_copy(a_recv.at[n], kept_ref.at[n], keep_sem.at[n]).start()
        b_send[n] = tn_dot(moves[g], a_recv[n]).astype(BF)
        for i in range(half):
            dz = order[g * half + i]
            src = b_send.at[n, pl.ds(i * cap, cap)]
            if dz == 0:
                pltpu.make_async_copy(src, back_ref.at[c, line], b_rsem.at[n]).start()
            else:
                pltpu.make_async_remote_copy(
                    src_ref=src, dst_ref=back_ref.at[c, line], send_sem=b_ssem.at[n], recv_sem=b_rsem.at[n],
                    device_id=(lax.rem(z + dz, nz) * NX + x, trk), device_id_type=MESH).start()

    for copy in copies:
        copy.wait()
    for n in range(2 * chunks):
        g, c = n // chunks, n % chunks
        if c == 0:
            await_bytes(q_recv.at[g], q_rsem.at[g])
        attend(g, c)
        send_in_plane(n)
        if n == 0:
            goal = iota((per, half * cap), 1)
            goal_z = iota((per, half * cap), 0) // CAP == goal // cap
            goal_at = (goal % cap).astype(F32)
            for gg in range(2):
                for v in range(npl):
                    hit = goal_z & (target_ref[gg, :, v : v + 1] == goal_at)
                    moves[gg, v * per : (v + 1) * per, :] = jnp.where(hit, 1.0, 0.0).astype(BF)
        else:
            send_along_z(n - 1)
    send_along_z(2 * chunks - 1)

    await_bytes(ids_y.at[pl.ds(0, ny - 1)], yi_send)
    await_bytes(emb_z.at[0, pl.ds(0, ny - 1)], y_send)
    await_bytes(emb_z.at[pl.ds(0, nz - 1)], z_send)
    await_bytes(ids_z.at[pl.ds(0, nz - 1)], zi_send)
    await_bytes(most_all.at[pl.ds(0, nx - 1)], most_ssem)
    await_bytes(most_all, most_rsem)
    most_ref[...] = jnp.max(most_all[...], axis=0)
    for g in range(2):
        await_bytes(q_send.at[g, pl.ds(0, (nx - 1) * lot)], q_ssem.at[g])
    for n in range(2 * chunks):
        remote = sum(1 for i in range(half) if order[n // chunks * half + i] != 0)
        await_bytes(a_send.at[n, pl.ds(0, (npl - 1) * per)], a_ssem.at[n])
        await_bytes(b_send.at[n, pl.ds(0, remote * cap)], b_ssem.at[n])
        await_bytes(back_ref.at[0, pl.ds(0, half * cap)], b_rsem.at[n])
        await_bytes(kept_ref.at[n], keep_sem.at[n])


def rest_kernel(
    nz, nt, cap, chunks,
    kept_ref, target_ref,
    back_ref,
    kept, moves, b_send, load_sem, b_ssem, b_rsem,
):
    z, x, trk, me = place(nt)
    npl = NX * nt
    order = z_order(nz)
    half = nz // 2
    per = half * CAP
    line = pl.ds(pl.multiple_of(z * cap, cap), cap)
    greet(nz, nt)
    load = pltpu.make_async_copy(kept_ref, kept, load_sem)
    load.start()
    load.wait()
    goal = iota((per, half * cap), 1)
    goal_z = iota((per, half * cap), 0) // CAP == goal // cap
    goal_at = (goal % cap + cap).astype(F32)
    for g in range(2):
        for v in range(npl):
            hit = goal_z & (target_ref[g, :, v : v + 1] == goal_at)
            moves[g, v * per : (v + 1) * per, :] = jnp.where(hit, 1.0, 0.0).astype(BF)
    for n in range(2 * chunks):
        g, c = n // chunks, n % chunks
        b_send[n] = tn_dot(moves[g], kept[n]).astype(BF)
        for i in range(half):
            dz = order[g * half + i]
            src = b_send.at[n, pl.ds(i * cap, cap)]
            if dz == 0:
                pltpu.make_async_copy(src, back_ref.at[c, line], b_rsem.at[n]).start()
            else:
                pltpu.make_async_remote_copy(
                    src_ref=src, dst_ref=back_ref.at[c, line], send_sem=b_ssem.at[n], recv_sem=b_rsem.at[n],
                    device_id=(lax.rem(z + dz, nz) * NX + x, trk), device_id_type=MESH).start()
    for n in range(2 * chunks):
        remote = sum(1 for i in range(half) if order[n // chunks * half + i] != 0)
        await_bytes(b_send.at[n, pl.ds(0, remote * cap)], b_ssem.at[n])
        await_bytes(back_ref.at[0, pl.ds(0, half * cap)], b_rsem.at[n])


def track_kernel(
    chunks, lists, cap, *refs,
):
    backs, refs = refs[:lists], refs[lists:]
    (
        slot_ref, embed_ref, gain_ref, valid_ref, keys_ref, scale_ref,
        wt_ref, wm_ref, bgain_ref, wh_ref, bh_ref, wb_ref,
        refined_ref, box_ref,
        projected, mixed,
    ) = refs
    rows, width = embed_ref.shape
    entries = slot_ref.shape[0]
    listing = entries // rows
    slots = backs[0].shape[1]
    column = iota((entries, slots), 1)
    attended = 0.0
    for k in range(lists):
        sought = (column // cap) * (CAP * NX * CAMS) + column % cap + k * cap
        pick = jnp.where(slot_ref[...] == sought, 1.0, 0.0).astype(BF)
        attended = attended + jnp.concatenate(
            [jnp.dot(pick, backs[k][c], preferred_element_type=F32) for c in range(chunks)], axis=1)
    states = layer_norm(embed_ref[...].astype(F32)) * gain_ref[...]
    states = jnp.broadcast_to(states[:, None, :], (rows, listing, width)).reshape(entries, width)
    residual = states + attended
    normed = layer_norm(residual).astype(BF)
    projected[...] = jnp.dot(normed, wt_ref[...], preferred_element_type=F32).astype(BF)
    block = 128
    head = width // HEADS
    same = iota((block, block), 0) // listing == iota((block, block), 1) // listing
    for b in range(entries // block):
        at = slice(b * block, (b + 1) * block)
        open_keys = same & (keys_ref[:, at] > 0.5)
        for h in range(HEADS):
            q = projected[at, h * head : (h + 1) * head]
            k = projected[at, width + h * head : width + (h + 1) * head]
            v = projected[at, 2 * width + h * head : 2 * width + (h + 1) * head]
            scores = nt_dot(q, k) * (scale_ref[0, h] * head ** (-0.5))
            scores = jnp.where(open_keys, scores, MASKED)
            weights = jnp.exp(scores - jnp.max(scores, axis=-1, keepdims=True))
            probs = (weights / jnp.sum(weights, axis=-1, keepdims=True)).astype(BF)
            mixed[at, h * head : (h + 1) * head] = jnp.dot(probs, v, preferred_element_type=F32).astype(BF)
    updated = residual + jnp.dot(mixed[...], wm_ref[...], preferred_element_type=F32)
    valid = valid_ref[...]
    refined_ref[...] = (updated * valid).astype(BF)
    box_input = (layer_norm(updated) * bgain_ref[...]).astype(BF)
    hidden = jax.nn.gelu(jnp.dot(box_input, wh_ref[...], preferred_element_type=F32) + bh_ref[...]).astype(BF)
    box_ref[...] = jnp.dot(hidden, wb_ref[...], preferred_element_type=F32) * valid


def local(
    track_embed, view_ids, view_count, key_feats, value_feats, track_gain, w_temporal,
    temporal_scale, w_merge, box_gain, w_hidden, b_hidden, w_box,
):
    tm_count = lax.axis_size("tm")
    nt = lax.axis_size("trk")
    nz = tm_count // NX
    ny = nt // CORES
    npl = NX * nt
    rows, width = track_embed.shape
    listing = view_ids.shape[1]
    entries = rows * listing
    tokens = key_feats.shape[2]
    per = nz * CAP
    total = npl * per
    longest = npl * CAP
    cap = longest // 2
    chunks = 2
    z = lax.axis_index("tm") // NX

    valid = jnp.arange(listing, dtype=jnp.int32)[None, :] < view_count[:, None]
    shown = jnp.where(valid, view_ids, -1)
    codes = time_code(z * NX + jnp.arange(NX, dtype=jnp.int32), width)
    flat = (shown * rows + jnp.arange(rows, dtype=jnp.int32)[:, None]).reshape(entries)
    plane = flat // (npl * rows)
    ahead = (flat[None, :] < flat[:, None]) & (flat[None, :] >= (plane * (npl * rows))[:, None])
    slot = plane * longest + jnp.sum(ahead.astype(jnp.int32), axis=1)
    slot = jnp.where(valid.reshape(entries), slot, -1)[:, None]

    in_plane_of = jnp.arange(nz, dtype=jnp.int32)
    crowd = jnp.max(jnp.sum((plane[None, :] == in_plane_of[:, None]).astype(jnp.int32), axis=1))
    turned = jnp.concatenate(
        [jnp.tile(shown.T, (1, ny)), jnp.broadcast_to(crowd, (8, ny * rows))], axis=0)

    anywhere = pl.BlockSpec(memory_space=pl.ANY)
    vmem = pl.BlockSpec(memory_space=pltpu.VMEM)
    dma = pltpu.SemaphoreType.DMA
    gain = track_gain[None, :]
    keys = key_feats.reshape(tokens, width)
    values = value_feats.reshape(tokens, width)
    count = 2 * chunks
    wide = width // chunks
    per = nz // 2 * CAP
    grows = npl * per
    back, kept, target, most = pl.pallas_call(
        functools.partial(mega_kernel, nz, nt, rows, cap, chunks, 256),
        out_shape=(
            jax.ShapeDtypeStruct((chunks, nz * cap, wide), BF),
            jax.ShapeDtypeStruct((count, grows, wide), BF),
            jax.ShapeDtypeStruct((2, per, npl), F32),
            jax.ShapeDtypeStruct((8, ny * rows), jnp.int32),
        ),
        in_specs=[vmem] * 4 + [anywhere] * 2,
        out_specs=(anywhere, anywhere, vmem, vmem),
        scratch_shapes=[
            pltpu.VMEM((nz, ny, rows, width), BF),
            pltpu.VMEM((ny, listing + 8, ny * rows), jnp.int32),
            pltpu.VMEM((nz, listing + 8, ny * rows), jnp.int32),
            pltpu.VMEM((2, grows, width), BF),
            pltpu.VMEM((2, grows, width), BF),
            pltpu.VMEM((2 * tokens, width), BF),
            pltpu.VMEM((2 * tokens, width), BF),
            pltpu.VMEM((count, grows, wide), BF),
            pltpu.VMEM((count, grows, wide), BF),
            pltpu.VMEM((2, grows, nz // 2 * cap), BF),
            pltpu.VMEM((count, nz // 2 * cap, wide), BF),
            pltpu.VMEM((8, ny * rows), jnp.int32),
            pltpu.VMEM((NX * CORES, 8, ny * rows), jnp.int32),
            dma, dma, dma, dma, dma, dma((nz,)), dma, dma((nz,)), dma((2,)), dma((2,)), dma((2,)),
            dma((2,)), dma((2,)), dma((count,)), dma((count,)), dma((count,)), dma((count,)), dma, dma, dma((count,)),
        ],
        compiler_params=pltpu.CompilerParams(
            collective_id=0, has_side_effects=True, vmem_limit_bytes=52 * 1024 * 1024),
        name="mega",
    )(track_embed, turned, codes, gain, keys, values)

    seen = valid.astype(F32)
    boxes_wide = w_box.shape[1]
    shared = (
        slot, track_embed, gain, seen.reshape(entries, 1), seen.reshape(1, entries), temporal_scale[None, :],
        w_temporal, w_merge, box_gain[None, :], w_hidden, b_hidden[None, :], w_box,
    )

    def finish(*backs):
        return pl.pallas_call(
            functools.partial(track_kernel, chunks, len(backs), cap),
            out_shape=(
                jax.ShapeDtypeStruct((entries, width), BF),
                jax.ShapeDtypeStruct((entries, boxes_wide), F32),
            ),
            in_specs=[vmem] * (len(backs) + 5) + [pl.BlockSpec(memory_space=pltpu.SMEM)] + [vmem] * 6,
            out_specs=(vmem, vmem),
            scratch_shapes=[pltpu.VMEM((entries, 3 * width), BF), pltpu.VMEM((entries, width), BF)],
            compiler_params=pltpu.CompilerParams(vmem_limit_bytes=56 * 1024 * 1024),
            name="track",
        )(*backs, *shared)

    def finish_long():
        rest = pl.pallas_call(
            functools.partial(rest_kernel, nz, nt, cap, chunks),
            out_shape=jax.ShapeDtypeStruct((chunks, nz * cap, wide), BF),
            in_specs=[anywhere, vmem],
            out_specs=anywhere,
            scratch_shapes=[
                pltpu.VMEM((count, grows, wide), BF),
                pltpu.VMEM((2, grows, nz // 2 * cap), BF),
                pltpu.VMEM((count, nz // 2 * cap, wide), BF),
                dma, dma((count,)), dma((count,)),
            ],
            compiler_params=pltpu.CompilerParams(
                collective_id=1, has_side_effects=True, vmem_limit_bytes=32 * 1024 * 1024),
            name="rest",
        )(kept, target)
        return finish(back, rest)

    refined, boxes = lax.cond(most[0, 0] > cap, finish_long, lambda: finish(back))
    return refined.reshape(rows, listing, width), boxes.reshape(rows, listing, boxes_wide)


def solution(mesh):
    placed = (
        P(("tm", "trk"), None),
        P(("tm", "trk"), None),
        P(("tm", "trk")),
        P("tm", "trk", None, None),
        P("tm", "trk", None, None),
    ) + (P(),) * 8
    return jax.shard_map(
        local,
        mesh=mesh,
        in_specs=placed,
        out_specs=(P(("tm", "trk"), None, None), P(("tm", "trk"), None, None)),
        check_vma=False,
    )
```

```python
import functools
import math

import jax
import jax.numpy as jnp
from jax import lax
from jax.experimental import pallas as pl
from jax.experimental.pallas import tpu as pltpu
from jax.sharding import PartitionSpec as P

HEADS = 8
CAMS = 8
CAP = 4
CORES = 2
NX = 4
EPS = 1e-05
MASKED = -1e30
MESH = pl.DeviceIdType.MESH
BF = jnp.bfloat16
F32 = jnp.float32


def layer_norm(values):
    centre = jnp.mean(values, axis=-1, keepdims=True)
    shifted = values - centre
    spread = jnp.mean(shifted * shifted, axis=-1, keepdims=True)
    return shifted * lax.rsqrt(spread + EPS)


def time_code(frame_ids, model_width):
    half_width = model_width // 2
    freq_index = jnp.arange(half_width).astype(F32)
    freq_rates = jnp.exp(freq_index * (-2.0 * math.log(10000.0) / model_width))
    angles = frame_ids.astype(F32)[..., None] * freq_rates
    return jnp.concatenate([jnp.sin(angles), jnp.cos(angles)], axis=-1)


def iota(shape, dim):
    return lax.broadcasted_iota(jnp.int32, shape, dim)


def nt_dot(a, b):
    return lax.dot_general(a, b, (((1,), (1,)), ((), ())), preferred_element_type=F32)


def tn_dot(a, b):
    return lax.dot_general(a, b, (((0,), (0,)), ((), ())), preferred_element_type=F32)


def place(nt):
    tm = lax.axis_index("tm")
    trk = lax.axis_index("trk")
    z = tm // NX
    x = tm % NX
    return z, x, trk, x * nt + trk


def greet(nz, nt):
    z, x, trk, me = place(nt)
    npl = NX * nt
    barrier = pltpu.get_barrier_semaphore()

    @pl.loop(1, npl)
    def _(k):
        p = lax.rem(me + k, npl)
        pl.semaphore_signal(barrier, inc=1, device_id=(z * NX + p // nt, p % nt), device_id_type=MESH)

    @pl.loop(1, nz)
    def _(k):
        zz = lax.rem(z + k, nz)
        pl.semaphore_signal(barrier, inc=1, device_id=(zz * NX + x, trk), device_id_type=MESH)

    pl.semaphore_wait(barrier, npl - 1 + nz - 1)


def await_bytes(like, sem):
    pltpu.make_async_copy(like, like, sem).wait()


def z_order(nz):
    half = nz // 2
    middle = [k for d in range(2, half) for k in (d, nz - d)]
    return middle + [0, 1, nz - 1, half]


def mega_kernel(
    nz, nt, rows, cap, chunks, block,
    embed_ref, ids_ref, code_ref, gain_ref, key_ref, value_ref,
    back_ref, kept_ref, target_ref, most_ref,
    emb_z, ids_y, ids_z, parts, q_send, q_recv, kk_ref, vv_ref, a_send, a_recv, moves, b_send, most_one, most_all,
    y_send, y_recv, yi_send, yi_recv, z_send, z_recv, zi_send, zi_recv, kv_own, kv_send, kv_recv,
    q_ssem, q_rsem, a_ssem, a_rsem, b_ssem, b_rsem, most_ssem, most_rsem, keep_sem,
):
    z, x, trk, me = place(nt)
    y, core = trk // CORES, trk % CORES
    ny = nt // CORES
    npl = NX * nt
    nx = NX * CORES
    me_x = x * CORES + core
    width = embed_ref.shape[1]
    tokens = key_ref.shape[0]
    order = z_order(nz)
    half = nz // 2
    per = half * CAP
    lot = ny * per
    lanes = ny * rows
    grows = npl * per
    head = 128
    wide = width // chunks
    scale = head ** (-0.5) * math.log2(math.e)
    listing = ids_ref.shape[0] - 8
    mine = pl.ds(pl.multiple_of(me * per, per), per)
    line = pl.ds(pl.multiple_of(z * cap, cap), cap)
    greet(nz, nt)

    own_e = pltpu.make_async_copy(embed_ref, emb_z.at[0, 0], y_recv)
    own_e.start()
    own_i = pltpu.make_async_copy(ids_ref, ids_y.at[0], yi_recv)
    own_i.start()
    for k in range(1, ny):
        to = (z * NX + x, lax.rem(y + k, ny) * CORES + core)
        pltpu.make_async_remote_copy(
            src_ref=ids_ref, dst_ref=ids_y.at[ny - k], send_sem=yi_send, recv_sem=yi_recv,
            device_id=to, device_id_type=MESH).start()
    for k in range(1, ny):
        to = (z * NX + x, lax.rem(y + k, ny) * CORES + core)
        pltpu.make_async_remote_copy(
            src_ref=embed_ref, dst_ref=emb_z.at[0, ny - k], send_sem=y_send, recv_sem=y_recv,
            device_id=to, device_id_type=MESH).start()

    before = (z * NX + x, lax.rem(trk + nt - 1, nt))
    first, second = pl.ds(0, tokens), pl.ds(tokens, tokens)
    copies = []
    for i, (own, both) in enumerate(((key_ref, kk_ref), (value_ref, vv_ref))):
        copies.append(pltpu.make_async_copy(own, both.at[first], kv_own.at[i]))
        copies.append(pltpu.make_async_remote_copy(
            src_ref=own, dst_ref=both.at[second], send_sem=kv_send.at[i], recv_sem=kv_recv.at[i],
            device_id=before, device_id_type=MESH))

    await_bytes(ids_y, yi_recv)
    lane = iota(ids_y.shape[1:], 1) // rows
    ids = ids_y[0]
    most = ids_y[0, listing:, :]
    for i in range(1, ny):
        ids = jnp.where(lane == i, ids_y[i], ids)
        most = jnp.maximum(most, ids_y[i, listing:, :])
    ids_z[0, :listing, :] = ids[:listing]
    ids_z[0, listing:, :] = most
    await_bytes(emb_z.at[0], y_recv)

    def to_z(source, step, part):
        target = (source - step) % nz
        device = (lax.rem(z + nz + step, nz) * NX + x, trk)
        if part == 0:
            pltpu.make_async_remote_copy(
                src_ref=ids_z.at[source], dst_ref=ids_z.at[target], send_sem=zi_send, recv_sem=zi_recv.at[target],
                device_id=device, device_id_type=MESH).start()
        few = pl.ds(part * (ny // 2), ny // 2)
        pltpu.make_async_remote_copy(
            src_ref=emb_z.at[source, few], dst_ref=emb_z.at[target, few], send_sem=z_send,
            recv_sem=z_recv.at[2 * target + part], device_id=device, device_id_type=MESH).start()

    def arrive(slot, part):
        if part == 0:
            await_bytes(ids_z.at[slot], zi_recv.at[slot])
        await_bytes(emb_z.at[slot, pl.ds(part * (ny // 2), ny // 2)], z_recv.at[2 * slot + part])

    for part in range(2):
        to_z(0, 1, part)
        to_z(0, -1, part)
    for copy in copies:
        copy.start()

    view_x = iota((nx, lanes), 0)
    view_x = (z * NX + view_x // CORES) * nt + y * CORES + view_x % CORES
    view_p = z * npl + iota((npl, lanes), 0)
    c0 = iota((lanes, lanes), 0)
    c1 = iota((lanes, lanes), 1)
    earlier = jnp.where((c0 < c1) & (c0 // rows == c1 // rows), 1.0, 0.0).astype(BF)
    lane_at = iota((nx, lanes), 1) // rows
    slot_row = iota((per, lanes), 0)
    same_z = slot_row // CAP == iota((per, lanes), 1) // rows
    slot_r = (slot_row % CAP).astype(F32)
    own_lane = iota((per, lanes), 1) < rows
    v0 = iota((npl, npl), 0)
    v1 = iota((npl, npl), 1)
    before_v = jnp.where(v0 < v1, 1.0, 0.0).astype(BF)
    tr = (iota((per, npl), 0) % CAP).astype(F32)

    def names(ids, view):
        named = jnp.zeros(view.shape, F32)
        for j in range(listing):
            named = jnp.where(ids[j : j + 1, :] == view, 1.0, named)
        return named

    ranked, found = {}, {}

    def prepare(slot):
        ids = ids_z[slot, :listing, :]
        named = names(ids, view_x)
        rank = jnp.dot(named.astype(BF), earlier, preferred_element_type=F32)
        ranked[slot] = jnp.where(named > 0.5, rank, -1.0)
        here = jnp.where((slot_row // CAP == order.index(slot) % half) & own_lane, 1.0, 0.0).astype(BF)
        found[slot] = nt_dot(here, names(ids, view_p).astype(BF))
        states = layer_norm(emb_z[slot].reshape(lanes, width).astype(F32)) * gain_ref[...]
        high = states.astype(BF)
        rest = states - high.astype(F32)
        middle = rest.astype(BF)
        parts[0, slot] = high
        parts[1, slot] = middle
        parts[2, slot] = (rest - middle.astype(F32)).astype(BF)

    def build(g):
        slots = order[g * half : (g + 1) * half]
        counts = found[slots[0]]
        for slot in slots[1:]:
            counts = counts + found[slot]
        base = jnp.dot(counts.astype(BF), before_v, preferred_element_type=F32)
        target_ref[g] = jnp.where(tr < counts, base + tr, -1.0)
        for dy in range(ny):
            here = jnp.zeros((nx, lanes), F32)
            for i in range(half):
                shift = (i - dy) * rows % lanes
                moved = pltpu.roll(ranked[slots[i]], shift, 1) if shift else ranked[slots[i]]
                here = jnp.where(lane_at == i, moved, here)
            picks = [jnp.where(same_z & (here[v : v + 1, :] == slot_r), 1.0, 0.0).astype(BF) for v in range(nx)]
            pick = jnp.concatenate(picks, axis=0)
            pick = jnp.concatenate([pick, pick, pick], axis=1)
            at = slice(dy * rows, (dy + 1) * rows)
            source = jnp.concatenate([parts[k, slots[i], at] for k in range(3) for i in range(half)], axis=0)
            made = jnp.dot(pick, source, preferred_element_type=F32)
            for v in range(nx):
                f = v // CORES
                one = made[v * per : (v + 1) * per] + code_ref[f : f + 1, :]
                q_send[g, v * lot + dy * per : v * lot + (dy + 1) * per, :] = one.astype(BF)
        block_x = pl.ds(pl.multiple_of(me_x * lot, lot), lot)
        pltpu.make_async_copy(q_send.at[g, block_x], q_recv.at[g, block_x], q_rsem.at[g]).start()
        for k in range(1, nx):
            p = lax.rem(me_x + k, nx)
            pltpu.make_async_remote_copy(
                src_ref=q_send.at[g, pl.ds(pl.multiple_of(p * lot, lot), lot)], dst_ref=q_recv.at[g, block_x],
                send_sem=q_ssem.at[g], recv_sem=q_rsem.at[g],
                device_id=(z * NX + lax.div(p, CORES), y * CORES + lax.rem(p, CORES)), device_id_type=MESH).start()

    prepare(0)
    for k in range(1, half):
        for part in range(2):
            arrive(nz - k, part)
            if k < half - 1 or part == 0:
                to_z(nz - k, 1, part)
            arrive(k, part)
            if k < half - 1 or part == 1:
                to_z(k, -1, part)
        prepare(nz - k)
        prepare(k)
    build(0)
    for part in range(2):
        arrive(half, part)
    prepare(half)
    build(1)

    most = ids_z[0, listing:, :]
    for i in range(1, nz):
        most = jnp.maximum(most, ids_z[i, listing:, :])
    most_one[...] = most
    pltpu.make_async_copy(most_one, most_all.at[me_x], most_rsem).start()
    for k in range(1, nx):
        p = lax.rem(me_x + k, nx)
        pltpu.make_async_remote_copy(
            src_ref=most_one, dst_ref=most_all.at[me_x], send_sem=most_ssem, recv_sem=most_rsem,
            device_id=(z * NX + lax.div(p, CORES), y * CORES + lax.rem(p, CORES)), device_id_type=MESH).start()

    def attend(g, c):
        def score(at, h):
            some = slice(c * wide + h * head, c * wide + (h + 1) * head)
            return nt_dot(q_recv[g, at, some], kk_ref[:, some])

        @pl.loop(0, grows // block)
        def _(b):
            at = pl.ds(pl.multiple_of(b * block, block), block)
            ahead = score(at, 0)
            for h in range(wide // head):
                scores = ahead
                if h + 1 < wide // head:
                    ahead = score(at, h + 1)
                top = jnp.max(scores, axis=-1, keepdims=True)
                weights = jnp.exp2((scores - top) * scale)
                sums = jnp.sum(weights, axis=-1, keepdims=True)
                some = slice(c * wide + h * head, c * wide + (h + 1) * head)
                o = jnp.dot(weights.astype(BF), vv_ref[:, some], preferred_element_type=F32)
                a_send[g * chunks + c, at, h * head : (h + 1) * head] = (o / sums).astype(BF)

    def rows_of(px, dy):
        return pl.ds(pl.multiple_of(px * lot + dy * per, per), per)

    def send_in_plane(n):
        pltpu.make_async_copy(a_send.at[n, rows_of(me_x, 0)], a_recv.at[n, mine], a_rsem.at[n]).start()

        @pl.loop(1, npl)
        def _(k):
            p = lax.rem(me + k, npl)
            px, pt = lax.div(p, nt), lax.rem(p, nt)
            dy = lax.rem(lax.div(pt, CORES) + ny - y, ny)
            pltpu.make_async_remote_copy(
                src_ref=a_send.at[n, rows_of(px * CORES + lax.rem(pt, CORES), dy)], dst_ref=a_recv.at[n, mine],
                send_sem=a_ssem.at[n], recv_sem=a_rsem.at[n],
                device_id=(z * NX + px, pt), device_id_type=MESH).start()

    def send_along_z(n):
        g, c = n // chunks, n % chunks
        await_bytes(a_recv.at[n], a_rsem.at[n])
        pltpu.make_async_copy(a_recv.at[n], kept_ref.at[n], keep_sem.at[n]).start()
        b_send[n] = tn_dot(moves[g], a_recv[n]).astype(BF)
        for i in range(half):
            dz = order[g * half + i]
            src = b_send.at[n, pl.ds(i * cap, cap)]
            if dz == 0:
                pltpu.make_async_copy(src, back_ref.at[c, line], b_rsem.at[n]).start()
            else:
                pltpu.make_async_remote_copy(
                    src_ref=src, dst_ref=back_ref.at[c, line], send_sem=b_ssem.at[n], recv_sem=b_rsem.at[n],
                    device_id=(lax.rem(z + dz, nz) * NX + x, trk), device_id_type=MESH).start()

    for copy in copies:
        copy.wait()
    for n in range(2 * chunks):
        g, c = n // chunks, n % chunks
        if c == 0:
            await_bytes(q_recv.at[g], q_rsem.at[g])
        attend(g, c)
        send_in_plane(n)
        if n == 0:
            goal = iota((per, half * cap), 1)
            goal_z = iota((per, half * cap), 0) // CAP == goal // cap
            goal_at = (goal % cap).astype(F32)
            for gg in range(2):
                for v in range(npl):
                    hit = goal_z & (target_ref[gg, :, v : v + 1] == goal_at)
                    moves[gg, v * per : (v + 1) * per, :] = jnp.where(hit, 1.0, 0.0).astype(BF)
        else:
            send_along_z(n - 1)
    send_along_z(2 * chunks - 1)

    await_bytes(ids_y.at[pl.ds(0, ny - 1)], yi_send)
    await_bytes(emb_z.at[0, pl.ds(0, ny - 1)], y_send)
    await_bytes(emb_z.at[pl.ds(0, nz - 1)], z_send)
    await_bytes(ids_z.at[pl.ds(0, nz - 1)], zi_send)
    await_bytes(most_all.at[pl.ds(0, nx - 1)], most_ssem)
    await_bytes(most_all, most_rsem)
    most_ref[...] = jnp.max(most_all[...], axis=0)
    for g in range(2):
        await_bytes(q_send.at[g, pl.ds(0, (nx - 1) * lot)], q_ssem.at[g])
    for n in range(2 * chunks):
        remote = sum(1 for i in range(half) if order[n // chunks * half + i] != 0)
        await_bytes(a_send.at[n, pl.ds(0, (npl - 1) * per)], a_ssem.at[n])
        await_bytes(b_send.at[n, pl.ds(0, remote * cap)], b_ssem.at[n])
        await_bytes(back_ref.at[0, pl.ds(0, half * cap)], b_rsem.at[n])
        await_bytes(kept_ref.at[n], keep_sem.at[n])


def rest_kernel(
    nz, nt, cap, chunks,
    kept_ref, target_ref,
    back_ref,
    kept, moves, b_send, load_sem, b_ssem, b_rsem,
):
    z, x, trk, me = place(nt)
    npl = NX * nt
    order = z_order(nz)
    half = nz // 2
    per = half * CAP
    line = pl.ds(pl.multiple_of(z * cap, cap), cap)
    greet(nz, nt)
    load = pltpu.make_async_copy(kept_ref, kept, load_sem)
    load.start()
    load.wait()
    goal = iota((per, half * cap), 1)
    goal_z = iota((per, half * cap), 0) // CAP == goal // cap
    goal_at = (goal % cap + cap).astype(F32)
    for g in range(2):
        for v in range(npl):
            hit = goal_z & (target_ref[g, :, v : v + 1] == goal_at)
            moves[g, v * per : (v + 1) * per, :] = jnp.where(hit, 1.0, 0.0).astype(BF)
    for n in range(2 * chunks):
        g, c = n // chunks, n % chunks
        b_send[n] = tn_dot(moves[g], kept[n]).astype(BF)
        for i in range(half):
            dz = order[g * half + i]
            src = b_send.at[n, pl.ds(i * cap, cap)]
            if dz == 0:
                pltpu.make_async_copy(src, back_ref.at[c, line], b_rsem.at[n]).start()
            else:
                pltpu.make_async_remote_copy(
                    src_ref=src, dst_ref=back_ref.at[c, line], send_sem=b_ssem.at[n], recv_sem=b_rsem.at[n],
                    device_id=(lax.rem(z + dz, nz) * NX + x, trk), device_id_type=MESH).start()
    for n in range(2 * chunks):
        remote = sum(1 for i in range(half) if order[n // chunks * half + i] != 0)
        await_bytes(b_send.at[n, pl.ds(0, remote * cap)], b_ssem.at[n])
        await_bytes(back_ref.at[0, pl.ds(0, half * cap)], b_rsem.at[n])


def track_kernel(
    chunks, lists, cap, *refs,
):
    backs, refs = refs[:lists], refs[lists:]
    (
        slot_ref, embed_ref, gain_ref, count_ref, scale_ref, bgain_ref, bh_ref, wb_ref,
        wt_any, wm_any, wh_any,
        refined_ref, box_ref,
        projected, mixed, wt_ref, wm_ref, wh_ref, load_sem,
    ) = refs
    loads = [
        pltpu.make_async_copy(far, near, load_sem.at[i])
        for i, (far, near) in enumerate(((wt_any, wt_ref), (wm_any, wm_ref), (wh_any, wh_ref)))
    ]
    for load in loads:
        load.start()
    rows, width = embed_ref.shape
    entries = slot_ref.shape[0]
    listing = entries // rows
    slots = backs[0].shape[1]
    column = iota((entries, slots), 1)
    attended = 0.0
    for k in range(lists):
        sought = (column // cap) * (CAP * NX * CAMS) + column % cap + k * cap
        pick = jnp.where(slot_ref[...] == sought, 1.0, 0.0).astype(BF)
        attended = attended + jnp.concatenate(
            [jnp.dot(pick, backs[k][c], preferred_element_type=F32) for c in range(chunks)], axis=1)
    states = layer_norm(embed_ref[...].astype(F32)) * gain_ref[...]
    states = jnp.broadcast_to(states[:, None, :], (rows, listing, width)).reshape(entries, width)
    residual = states + attended
    normed = layer_norm(residual).astype(BF)
    loads[0].wait()
    projected[...] = jnp.dot(normed, wt_ref[...], preferred_element_type=F32).astype(BF)
    block = 128
    head = width // HEADS
    row = iota((block, block), 0) // listing
    col = iota((block, block), 1)
    for b in range(entries // block):
        at = slice(b * block, (b + 1) * block)
        open_keys = (row == col // listing) & (col % listing < count_ref[0:1, at])
        scores = []
        for h in range(HEADS):
            q = projected[at, h * head : (h + 1) * head]
            k = projected[at, width + h * head : width + (h + 1) * head]
            scores.append(nt_dot(q, k) * (scale_ref[0, h] * head ** (-0.5)))
        scores = jnp.where(open_keys[None], jnp.stack(scores, axis=0), MASKED)
        weights = jnp.exp(scores - jnp.max(scores, axis=-1, keepdims=True))
        probs = (weights * (1.0 / jnp.sum(weights, axis=-1, keepdims=True))).astype(BF)
        for h in range(HEADS):
            v = projected[at, 2 * width + h * head : 2 * width + (h + 1) * head]
            mixed[at, h * head : (h + 1) * head] = jnp.dot(probs[h], v, preferred_element_type=F32).astype(BF)
    loads[1].wait()
    updated = residual + jnp.dot(mixed[...], wm_ref[...], preferred_element_type=F32)
    refined_ref[...] = jnp.where(slot_ref[...] >= 0, updated, 0.0).astype(BF)
    box_input = (layer_norm(updated) * bgain_ref[...]).astype(BF)
    loads[2].wait()
    hidden = jax.nn.gelu(jnp.dot(box_input, wh_ref[...], preferred_element_type=F32) + bh_ref[...]).astype(BF)
    i0 = iota((entries, entries), 0)
    turn = jnp.where(iota((entries, entries), 1) == i0 % rows * listing + i0 // rows, 1.0, 0.0).astype(BF)
    hidden = jnp.dot(turn, hidden, preferred_element_type=F32).astype(BF)
    boxes = nt_dot(wb_ref[...], hidden)
    boxes = jnp.where(iota(boxes.shape, 1) // rows < count_ref[1:2, :], boxes, 0.0)
    for j in range(listing):
        box_ref[:, j, :] = boxes[:, j * rows : (j + 1) * rows]


def local(
    track_embed, view_ids, view_count, key_feats, value_feats, track_gain, w_temporal,
    temporal_scale, w_merge, box_gain, w_hidden, b_hidden, w_box,
):
    tm_count = lax.axis_size("tm")
    nt = lax.axis_size("trk")
    nz = tm_count // NX
    ny = nt // CORES
    npl = NX * nt
    rows, width = track_embed.shape
    listing = view_ids.shape[1]
    entries = rows * listing
    tokens = key_feats.shape[2]
    per = nz * CAP
    total = npl * per
    longest = npl * CAP
    cap = longest // 2
    chunks = 2
    z = lax.axis_index("tm") // NX

    valid = jnp.arange(listing, dtype=jnp.int32)[None, :] < view_count[:, None]
    shown = jnp.where(valid, view_ids, -1)
    codes = time_code(z * NX + jnp.arange(NX, dtype=jnp.int32), width)
    flat = (shown * rows + jnp.arange(rows, dtype=jnp.int32)[:, None]).reshape(entries)
    plane = flat // (npl * rows)
    ahead = (flat[None, :] < flat[:, None]) & (flat[None, :] >= (plane * (npl * rows))[:, None])
    slot = plane * longest + jnp.sum(ahead.astype(jnp.int32), axis=1)
    slot = jnp.where(valid.reshape(entries), slot, -1)[:, None]

    in_plane_of = jnp.arange(nz, dtype=jnp.int32)
    crowd = jnp.max(jnp.sum((plane[None, :] == in_plane_of[:, None]).astype(jnp.int32), axis=1))
    turned = jnp.concatenate(
        [jnp.tile(shown.T, (1, ny)), jnp.broadcast_to(crowd, (8, ny * rows))], axis=0)

    anywhere = pl.BlockSpec(memory_space=pl.ANY)
    vmem = pl.BlockSpec(memory_space=pltpu.VMEM)
    dma = pltpu.SemaphoreType.DMA
    gain = track_gain[None, :]
    keys = key_feats.reshape(tokens, width)
    values = value_feats.reshape(tokens, width)
    count = 2 * chunks
    wide = width // chunks
    per = nz // 2 * CAP
    grows = npl * per
    back, kept, target, most = pl.pallas_call(
        functools.partial(mega_kernel, nz, nt, rows, cap, chunks, 256),
        out_shape=(
            jax.ShapeDtypeStruct((chunks, nz * cap, wide), BF),
            jax.ShapeDtypeStruct((count, grows, wide), BF),
            jax.ShapeDtypeStruct((2, per, npl), F32),
            jax.ShapeDtypeStruct((8, ny * rows), jnp.int32),
        ),
        in_specs=[vmem] * 4 + [anywhere] * 2,
        out_specs=(anywhere, anywhere, vmem, vmem),
        scratch_shapes=[
            pltpu.VMEM((nz, ny, rows, width), BF),
            pltpu.VMEM((ny, listing + 8, ny * rows), jnp.int32),
            pltpu.VMEM((nz, listing + 8, ny * rows), jnp.int32),
            pltpu.VMEM((3, nz, ny * rows, width), BF),
            pltpu.VMEM((2, grows, width), BF),
            pltpu.VMEM((2, grows, width), BF),
            pltpu.VMEM((2 * tokens, width), BF),
            pltpu.VMEM((2 * tokens, width), BF),
            pltpu.VMEM((count, grows, wide), BF),
            pltpu.VMEM((count, grows, wide), BF),
            pltpu.VMEM((2, grows, nz // 2 * cap), BF),
            pltpu.VMEM((count, nz // 2 * cap, wide), BF),
            pltpu.VMEM((8, ny * rows), jnp.int32),
            pltpu.VMEM((NX * CORES, 8, ny * rows), jnp.int32),
            dma, dma, dma, dma, dma, dma((2 * nz,)), dma, dma((nz,)), dma((2,)), dma((2,)), dma((2,)),
            dma((2,)), dma((2,)), dma((count,)), dma((count,)), dma((count,)), dma((count,)), dma, dma, dma((count,)),
        ],
        compiler_params=pltpu.CompilerParams(
            collective_id=0, has_side_effects=True, vmem_limit_bytes=52 * 1024 * 1024),
        name="mega",
    )(track_embed, turned, codes, gain, keys, values)

    boxes_wide = w_box.shape[1]
    counts = jnp.stack([jnp.repeat(view_count, listing), jnp.tile(view_count, listing)])
    shared = (
        slot, track_embed, gain, counts, temporal_scale[None, :], box_gain[None, :], b_hidden[None, :], w_box.T,
        w_temporal, w_merge, w_hidden,
    )

    def finish(*backs):
        return pl.pallas_call(
            functools.partial(track_kernel, chunks, len(backs), cap),
            out_shape=(
                jax.ShapeDtypeStruct((entries, width), BF),
                jax.ShapeDtypeStruct((boxes_wide, listing, rows), F32),
            ),
            in_specs=[vmem] * (len(backs) + 4) + [pl.BlockSpec(memory_space=pltpu.SMEM)] + [vmem] * 3 + [anywhere] * 3,
            out_specs=(vmem, vmem),
            scratch_shapes=[
                pltpu.VMEM((entries, 3 * width), BF),
                pltpu.VMEM((entries, width), BF),
                pltpu.VMEM(w_temporal.shape, BF),
                pltpu.VMEM(w_merge.shape, BF),
                pltpu.VMEM(w_hidden.shape, BF),
                dma((3,)),
            ],
            compiler_params=pltpu.CompilerParams(vmem_limit_bytes=56 * 1024 * 1024),
            name="track",
        )(*backs, *shared)

    def finish_long():
        rest = pl.pallas_call(
            functools.partial(rest_kernel, nz, nt, cap, chunks),
            out_shape=jax.ShapeDtypeStruct((chunks, nz * cap, wide), BF),
            in_specs=[anywhere, vmem],
            out_specs=anywhere,
            scratch_shapes=[
                pltpu.VMEM((count, grows, wide), BF),
                pltpu.VMEM((2, grows, nz // 2 * cap), BF),
                pltpu.VMEM((count, nz // 2 * cap, wide), BF),
                dma, dma((count,)), dma((count,)),
            ],
            compiler_params=pltpu.CompilerParams(
                collective_id=1, has_side_effects=True, vmem_limit_bytes=32 * 1024 * 1024),
            name="rest",
        )(kept, target)
        return finish(back, rest)

    refined, boxes = lax.cond(most[0, 0] > cap, finish_long, lambda: finish(back))
    return refined.reshape(rows, listing, width), jnp.transpose(boxes, (2, 1, 0))


def solution(mesh):
    placed = (
        P(("tm", "trk"), None),
        P(("tm", "trk"), None),
        P(("tm", "trk")),
        P("tm", "trk", None, None),
        P("tm", "trk", None, None),
    ) + (P(),) * 8
    return jax.shard_map(
        local,
        mesh=mesh,
        in_specs=placed,
        out_specs=(P(("tm", "trk"), None, None), P(("tm", "trk"), None, None)),
        check_vma=False,
    )
```

```python
import functools
import math

import jax
import jax.numpy as jnp
from jax import lax
from jax.experimental import pallas as pl
from jax.experimental.pallas import tpu as pltpu
from jax.sharding import PartitionSpec as P

HEADS = 8
CAMS = 8
CAP = 4
CORES = 2
NX = 4
EPS = 1e-05
MASKED = -1e30
MESH = pl.DeviceIdType.MESH
BF = jnp.bfloat16
F32 = jnp.float32


def layer_norm(values):
    centre = jnp.mean(values, axis=-1, keepdims=True)
    shifted = values - centre
    spread = jnp.mean(shifted * shifted, axis=-1, keepdims=True)
    return shifted * lax.rsqrt(spread + EPS)


def time_code(frame_ids, model_width):
    half_width = model_width // 2
    freq_index = jnp.arange(half_width).astype(F32)
    freq_rates = jnp.exp(freq_index * (-2.0 * math.log(10000.0) / model_width))
    angles = frame_ids.astype(F32)[..., None] * freq_rates
    return jnp.concatenate([jnp.sin(angles), jnp.cos(angles)], axis=-1)


def iota(shape, dim):
    return lax.broadcasted_iota(jnp.int32, shape, dim)


def nt_dot(a, b):
    return lax.dot_general(a, b, (((1,), (1,)), ((), ())), preferred_element_type=F32)


def tn_dot(a, b):
    return lax.dot_general(a, b, (((0,), (0,)), ((), ())), preferred_element_type=F32)


def place(nt):
    tm = lax.axis_index("tm")
    trk = lax.axis_index("trk")
    z = tm // NX
    x = tm % NX
    return z, x, trk, x * nt + trk


def greet(nz, nt):
    z, x, trk, me = place(nt)
    npl = NX * nt
    barrier = pltpu.get_barrier_semaphore()

    @pl.loop(1, npl)
    def _(k):
        p = lax.rem(me + k, npl)
        pl.semaphore_signal(barrier, inc=1, device_id=(z * NX + p // nt, p % nt), device_id_type=MESH)

    @pl.loop(1, nz)
    def _(k):
        zz = lax.rem(z + k, nz)
        pl.semaphore_signal(barrier, inc=1, device_id=(zz * NX + x, trk), device_id_type=MESH)

    pl.semaphore_wait(barrier, npl - 1 + nz - 1)


def await_bytes(like, sem):
    pltpu.make_async_copy(like, like, sem).wait()


def z_order(nz):
    half = nz // 2
    return [k for d in range(1, half) for k in (d, nz - d)] + [half, 0]


def mega_kernel(
    nz, nt, rows, cap, chunks,
    embed_ref, ids_ref, code_ref, gain_ref, key_ref, value_ref,
    back_ref, kept_ref, target_ref, most_ref,
    emb_z, ids_y, ids_z, parts, q_send, q_recv, kk_ref, vv_ref, a_send, a_recv, moves, b_send, most_one, most_all,
    y_send, y_recv, yi_send, yi_recv, z_send, z_recv, zi_send, zi_recv, kv_own, kv_send, kv_recv,
    q_ssem, q_rsem, a_ssem, a_rsem, b_ssem, b_rsem, most_ssem, most_rsem, keep_sem,
):
    z, x, trk, me = place(nt)
    y, core = trk // CORES, trk % CORES
    ny = nt // CORES
    npl = NX * nt
    nx = NX * CORES
    me_x = x * CORES + core
    width = embed_ref.shape[1]
    tokens = key_ref.shape[0]
    order = z_order(nz)
    half = nz // 2
    per = half * CAP
    lot = ny * 2 * CAP
    lanes = ny * rows
    head = 128
    wide = width // chunks
    scale = head ** (-0.5) * math.log2(math.e)
    listing = ids_ref.shape[0] - 8
    mine = pl.ds(pl.multiple_of(me * per, per), per)
    line = pl.ds(pl.multiple_of(z * cap, cap), cap)
    greet(nz, nt)

    own_e = pltpu.make_async_copy(embed_ref, emb_z.at[0, 0], y_recv)
    own_e.start()
    own_i = pltpu.make_async_copy(ids_ref, ids_y.at[0], yi_recv)
    own_i.start()
    for k in range(1, ny):
        to = (z * NX + x, lax.rem(y + k, ny) * CORES + core)
        pltpu.make_async_remote_copy(
            src_ref=ids_ref, dst_ref=ids_y.at[ny - k], send_sem=yi_send, recv_sem=yi_recv,
            device_id=to, device_id_type=MESH).start()
    for k in range(1, ny):
        to = (z * NX + x, lax.rem(y + k, ny) * CORES + core)
        pltpu.make_async_remote_copy(
            src_ref=embed_ref, dst_ref=emb_z.at[0, ny - k], send_sem=y_send, recv_sem=y_recv,
            device_id=to, device_id_type=MESH).start()

    before = (z * NX + x, lax.rem(trk + nt - 1, nt))
    first, second = pl.ds(0, tokens), pl.ds(tokens, tokens)
    copies = []
    for i, (own, both) in enumerate(((key_ref, kk_ref), (value_ref, vv_ref))):
        copies.append(pltpu.make_async_copy(own, both.at[first], kv_own.at[i]))
        copies.append(pltpu.make_async_remote_copy(
            src_ref=own, dst_ref=both.at[second], send_sem=kv_send.at[i], recv_sem=kv_recv.at[i],
            device_id=before, device_id_type=MESH))

    await_bytes(ids_y, yi_recv)
    lane = iota(ids_y.shape[1:], 1) // rows
    ids = ids_y[0]
    most = ids_y[0, listing:, :]
    for i in range(1, ny):
        ids = jnp.where(lane == i, ids_y[i], ids)
        most = jnp.maximum(most, ids_y[i, listing:, :])
    ids_z[0, :listing, :] = ids[:listing]
    ids_z[0, listing:, :] = most
    await_bytes(emb_z.at[0], y_recv)

    def to_z(source, step, part):
        target = (source - step) % nz
        device = (lax.rem(z + nz + step, nz) * NX + x, trk)
        if part == 0:
            pltpu.make_async_remote_copy(
                src_ref=ids_z.at[source], dst_ref=ids_z.at[target], send_sem=zi_send, recv_sem=zi_recv.at[target],
                device_id=device, device_id_type=MESH).start()
        few = pl.ds(part * (ny // 2), ny // 2)
        pltpu.make_async_remote_copy(
            src_ref=emb_z.at[source, few], dst_ref=emb_z.at[target, few], send_sem=z_send,
            recv_sem=z_recv.at[2 * target + part], device_id=device, device_id_type=MESH).start()

    def arrive(slot, part):
        if part == 0:
            await_bytes(ids_z.at[slot], zi_recv.at[slot])
        await_bytes(emb_z.at[slot, pl.ds(part * (ny // 2), ny // 2)], z_recv.at[2 * slot + part])

    for part in range(2):
        to_z(0, 1, part)
        to_z(0, -1, part)
    for copy in copies:
        copy.start()

    view_x = iota((nx, lanes), 0)
    view_x = (z * NX + view_x // CORES) * nt + y * CORES + view_x % CORES
    view_p = z * npl + iota((npl, lanes), 0)
    c0 = iota((lanes, lanes), 0)
    c1 = iota((lanes, lanes), 1)
    earlier = jnp.where((c0 < c1) & (c0 // rows == c1 // rows), 1.0, 0.0).astype(BF)
    lane_at = iota((nx, lanes), 1) // rows
    slot_row = iota((per, lanes), 0)
    same_z = slot_row // CAP == iota((per, lanes), 1) // rows
    slot_r = (slot_row % CAP).astype(F32)
    own_lane = iota((per, lanes), 1) < rows
    v0 = iota((npl, npl), 0)
    v1 = iota((npl, npl), 1)
    before_v = jnp.where(v0 < v1, 1.0, 0.0).astype(BF)
    tr = (iota((per, npl), 0) % CAP).astype(F32)

    def names(ids, view):
        named = jnp.zeros(view.shape, F32)
        for j in range(listing):
            named = jnp.where(ids[j : j + 1, :] == view, 1.0, named)
        return named

    ranked, found = {}, {}

    def prepare(slot):
        ids = ids_z[slot, :listing, :]
        named = names(ids, view_x)
        rank = jnp.dot(named.astype(BF), earlier, preferred_element_type=F32)
        ranked[slot] = jnp.where(named > 0.5, rank, -1.0)
        here = jnp.where((slot_row // CAP == order.index(slot) % half) & own_lane, 1.0, 0.0).astype(BF)
        found[slot] = nt_dot(here, names(ids, view_p).astype(BF))
        states = layer_norm(emb_z[slot].reshape(lanes, width).astype(F32)) * gain_ref[...]
        high = states.astype(BF)
        rest = states - high.astype(F32)
        middle = rest.astype(BF)
        parts[0, slot] = high
        parts[1, slot] = middle
        parts[2, slot] = (rest - middle.astype(F32)).astype(BF)

    def build(f):
        slots = order[2 * f : 2 * f + 2]
        for side in range(ny // 2):
            here = jnp.zeros((nx, lanes), F32)
            sources = []
            for i in range(4):
                dy, slot = 2 * side + i // 2, slots[i % 2]
                shift = (i - dy) * rows % lanes
                moved = pltpu.roll(ranked[slot], shift, 1) if shift else ranked[slot]
                here = jnp.where(lane_at == i, moved, here)
                sources.append((slot, slice(dy * rows, (dy + 1) * rows)))
            picks = [jnp.where(same_z & (here[v : v + 1, :] == slot_r), 1.0, 0.0).astype(BF) for v in range(nx)]
            pick = jnp.concatenate(picks, axis=0)
            pick = jnp.concatenate([pick, pick, pick], axis=1)
            source = jnp.concatenate([parts[k, slot, at] for k in range(3) for slot, at in sources], axis=0)
            made = jnp.dot(pick, source, preferred_element_type=F32)
            for v in range(nx):
                frame = v // CORES
                one = made[v * per : (v + 1) * per] + code_ref[frame : frame + 1, :]
                q_send[f, v * lot + side * per : v * lot + (side + 1) * per, :] = one.astype(BF)
        block_x = pl.ds(pl.multiple_of(me_x * lot, lot), lot)
        pltpu.make_async_copy(q_send.at[f, block_x], q_recv.at[f, block_x], q_rsem.at[f]).start()
        for k in range(1, nx):
            p = lax.rem(me_x + k, nx)
            pltpu.make_async_remote_copy(
                src_ref=q_send.at[f, pl.ds(pl.multiple_of(p * lot, lot), lot)], dst_ref=q_recv.at[f, block_x],
                send_sem=q_ssem.at[f], recv_sem=q_rsem.at[f],
                device_id=(z * NX + lax.div(p, CORES), y * CORES + lax.rem(p, CORES)), device_id_type=MESH).start()

    def aim(g):
        slots = order[g * half : (g + 1) * half]
        counts = found[slots[0]]
        for slot in slots[1:]:
            counts = counts + found[slot]
        base = jnp.dot(counts.astype(BF), before_v, preferred_element_type=F32)
        target_ref[g] = jnp.where(tr < counts, base + tr, -1.0)

    prepare(0)
    for k in range(1, half):
        for part in range(2):
            arrive(nz - k, part)
            if k < half - 1 or part == 0:
                to_z(nz - k, 1, part)
            arrive(k, part)
            if k < half - 1 or part == 1:
                to_z(k, -1, part)
        prepare(nz - k)
        prepare(k)
        build(k - 1)
    for part in range(2):
        arrive(half, part)
    prepare(half)
    build(half - 1)
    aim(0)
    aim(1)

    most = ids_z[0, listing:, :]
    for i in range(1, nz):
        most = jnp.maximum(most, ids_z[i, listing:, :])
    most_one[...] = most
    pltpu.make_async_copy(most_one, most_all.at[me_x], most_rsem).start()
    for k in range(1, nx):
        p = lax.rem(me_x + k, nx)
        pltpu.make_async_remote_copy(
            src_ref=most_one, dst_ref=most_all.at[me_x], send_sem=most_ssem, recv_sem=most_rsem,
            device_id=(z * NX + lax.div(p, CORES), y * CORES + lax.rem(p, CORES)), device_id_type=MESH).start()

    def attend(f, c):
        n, part = f // 2 * chunks + c, f % 2 * 2 * CAP

        def score(h):
            some = slice(c * wide + h * head, c * wide + (h + 1) * head)
            return nt_dot(q_recv[f, :, some], kk_ref[:, some])

        ahead = score(0)
        for h in range(wide // head):
            scores = ahead
            if h + 1 < wide // head:
                ahead = score(h + 1)
            top = jnp.max(scores, axis=-1, keepdims=True)
            weights = jnp.exp2((scores - top) * scale)
            sums = jnp.sum(weights, axis=-1, keepdims=True)
            some = slice(c * wide + h * head, c * wide + (h + 1) * head)
            o = jnp.dot(weights.astype(BF), vv_ref[:, some], preferred_element_type=F32) / sums
            a_send[n, :, part : part + 2 * CAP, h * head : (h + 1) * head] = o.reshape(npl, 2 * CAP, head).astype(BF)

    def send_in_plane(n):
        pltpu.make_async_copy(a_send.at[n, me_x * ny], a_recv.at[n, mine], a_rsem.at[n]).start()

        @pl.loop(1, npl)
        def _(k):
            p = lax.rem(me + k, npl)
            px, pt = lax.div(p, nt), lax.rem(p, nt)
            dy = lax.rem(lax.div(pt, CORES) + ny - y, ny)
            pltpu.make_async_remote_copy(
                src_ref=a_send.at[n, (px * CORES + lax.rem(pt, CORES)) * ny + dy], dst_ref=a_recv.at[n, mine],
                send_sem=a_ssem.at[n], recv_sem=a_rsem.at[n],
                device_id=(z * NX + px, pt), device_id_type=MESH).start()

    def send_along_z(n):
        g, c = n // chunks, n % chunks
        await_bytes(a_recv.at[n], a_rsem.at[n])
        pltpu.make_async_copy(a_recv.at[n], kept_ref.at[n], keep_sem.at[n]).start()
        b_send[n] = tn_dot(moves[g], a_recv[n]).astype(BF)
        for i in range(half):
            dz = order[g * half + i]
            src = b_send.at[n, pl.ds(i * cap, cap)]
            if dz == 0:
                pltpu.make_async_copy(src, back_ref.at[c, line], b_rsem.at[n]).start()
            else:
                pltpu.make_async_remote_copy(
                    src_ref=src, dst_ref=back_ref.at[c, line], send_sem=b_ssem.at[n], recv_sem=b_rsem.at[n],
                    device_id=(lax.rem(z + dz, nz) * NX + x, trk), device_id_type=MESH).start()

    def ready(f):
        await_bytes(q_recv.at[f], q_rsem.at[f])

    def moves_of(g):
        goal = iota((per, half * cap), 1)
        goal_z = iota((per, half * cap), 0) // CAP == goal // cap
        goal_at = (goal % cap).astype(F32)
        for v in range(npl):
            hit = goal_z & (target_ref[g, :, v : v + 1] == goal_at)
            moves[g, v * per : (v + 1) * per, :] = jnp.where(hit, 1.0, 0.0).astype(BF)

    for copy in copies:
        copy.wait()
    ready(0)
    attend(0, 0)
    attend(0, 1)
    ready(1)
    attend(1, 0)
    send_in_plane(0)
    attend(1, 1)
    send_in_plane(1)
    moves_of(0)
    ready(2)
    attend(2, 0)
    attend(2, 1)
    ready(3)
    attend(3, 0)
    send_in_plane(2)
    send_along_z(0)
    attend(3, 1)
    send_in_plane(3)
    send_along_z(1)
    moves_of(1)
    send_along_z(2)
    send_along_z(3)

    await_bytes(ids_y.at[pl.ds(0, ny - 1)], yi_send)
    await_bytes(emb_z.at[0, pl.ds(0, ny - 1)], y_send)
    await_bytes(emb_z.at[pl.ds(0, nz - 1)], z_send)
    await_bytes(ids_z.at[pl.ds(0, nz - 1)], zi_send)
    await_bytes(most_all.at[pl.ds(0, nx - 1)], most_ssem)
    await_bytes(most_all, most_rsem)
    most_ref[...] = jnp.max(most_all[...], axis=0)
    for f in range(half):
        await_bytes(q_send.at[f, pl.ds(0, (nx - 1) * lot)], q_ssem.at[f])
    for n in range(2 * chunks):
        remote = sum(1 for i in range(half) if order[n // chunks * half + i] != 0)
        await_bytes(a_send.at[n, pl.ds(0, npl - 1)], a_ssem.at[n])
        await_bytes(b_send.at[n, pl.ds(0, remote * cap)], b_ssem.at[n])
        await_bytes(back_ref.at[0, pl.ds(0, half * cap)], b_rsem.at[n])
        await_bytes(kept_ref.at[n], keep_sem.at[n])


def rest_kernel(
    nz, nt, cap, chunks,
    kept_ref, target_ref,
    back_ref,
    kept, moves, b_send, load_sem, b_ssem, b_rsem,
):
    z, x, trk, me = place(nt)
    npl = NX * nt
    order = z_order(nz)
    half = nz // 2
    per = half * CAP
    line = pl.ds(pl.multiple_of(z * cap, cap), cap)
    greet(nz, nt)
    load = pltpu.make_async_copy(kept_ref, kept, load_sem)
    load.start()
    load.wait()
    goal = iota((per, half * cap), 1)
    goal_z = iota((per, half * cap), 0) // CAP == goal // cap
    goal_at = (goal % cap + cap).astype(F32)
    for g in range(2):
        for v in range(npl):
            hit = goal_z & (target_ref[g, :, v : v + 1] == goal_at)
            moves[g, v * per : (v + 1) * per, :] = jnp.where(hit, 1.0, 0.0).astype(BF)
    for n in range(2 * chunks):
        g, c = n // chunks, n % chunks
        b_send[n] = tn_dot(moves[g], kept[n]).astype(BF)
        for i in range(half):
            dz = order[g * half + i]
            src = b_send.at[n, pl.ds(i * cap, cap)]
            if dz == 0:
                pltpu.make_async_copy(src, back_ref.at[c, line], b_rsem.at[n]).start()
            else:
                pltpu.make_async_remote_copy(
                    src_ref=src, dst_ref=back_ref.at[c, line], send_sem=b_ssem.at[n], recv_sem=b_rsem.at[n],
                    device_id=(lax.rem(z + dz, nz) * NX + x, trk), device_id_type=MESH).start()
    for n in range(2 * chunks):
        remote = sum(1 for i in range(half) if order[n // chunks * half + i] != 0)
        await_bytes(b_send.at[n, pl.ds(0, remote * cap)], b_ssem.at[n])
        await_bytes(back_ref.at[0, pl.ds(0, half * cap)], b_rsem.at[n])


def track_kernel(
    chunks, lists, cap, *refs,
):
    backs, refs = refs[:lists], refs[lists:]
    (
        slot_ref, embed_ref, gain_ref, count_ref, scale_ref, bgain_ref, bh_ref, wb_ref,
        wt_any, wm_any, wh_any,
        refined_ref, box_ref,
        projected, mixed, wt_ref, wm_ref, wh_ref, load_sem,
    ) = refs
    loads = [
        pltpu.make_async_copy(far, near, load_sem.at[i])
        for i, (far, near) in enumerate(((wt_any, wt_ref), (wm_any, wm_ref), (wh_any, wh_ref)))
    ]
    for load in loads:
        load.start()
    rows, width = embed_ref.shape
    entries = slot_ref.shape[0]
    listing = entries // rows
    slots = backs[0].shape[1]
    column = iota((entries, slots), 1)
    attended = 0.0
    for k in range(lists):
        sought = (column // cap) * (CAP * NX * CAMS) + column % cap + k * cap
        pick = jnp.where(slot_ref[...] == sought, 1.0, 0.0).astype(BF)
        attended = attended + jnp.concatenate(
            [jnp.dot(pick, backs[k][c], preferred_element_type=F32) for c in range(chunks)], axis=1)
    states = layer_norm(embed_ref[...].astype(F32)) * gain_ref[...]
    states = jnp.broadcast_to(states[:, None, :], (rows, listing, width)).reshape(entries, width)
    residual = states + attended
    normed = layer_norm(residual).astype(BF)
    loads[0].wait()
    projected[...] = jnp.dot(normed, wt_ref[...], preferred_element_type=F32).astype(BF)
    track = iota((rows, entries), 0)
    place_at = iota((rows, entries), 1)
    per_track = count_ref[...].astype(F32).astype(BF)
    by_track = jnp.dot(per_track, jnp.where(place_at // listing == track, 1.0, 0.0).astype(BF), preferred_element_type=F32)
    by_place = jnp.dot(per_track, jnp.where(place_at % rows == track, 1.0, 0.0).astype(BF), preferred_element_type=F32)
    block = 128
    head = width // HEADS
    row = iota((block, block), 0) // listing
    col = iota((block, block), 1)
    for b in range(entries // block):
        at = slice(b * block, (b + 1) * block)
        open_keys = (row == col // listing) & ((col % listing).astype(F32) < by_track[:, at])
        scores = []
        for h in range(HEADS):
            q = projected[at, h * head : (h + 1) * head]
            k = projected[at, width + h * head : width + (h + 1) * head]
            scores.append(nt_dot(q, k) * (scale_ref[0, h] * head ** (-0.5)))
        scores = jnp.where(open_keys[None], jnp.stack(scores, axis=0), MASKED)
        weights = jnp.exp(scores - jnp.max(scores, axis=-1, keepdims=True))
        probs = (weights * (1.0 / jnp.sum(weights, axis=-1, keepdims=True))).astype(BF)
        for h in range(HEADS):
            v = projected[at, 2 * width + h * head : 2 * width + (h + 1) * head]
            mixed[at, h * head : (h + 1) * head] = jnp.dot(probs[h], v, preferred_element_type=F32).astype(BF)
    loads[1].wait()
    updated = residual + jnp.dot(mixed[...], wm_ref[...], preferred_element_type=F32)
    refined_ref[...] = jnp.where(slot_ref[...] >= 0, updated, 0.0).astype(BF)
    box_input = (layer_norm(updated) * bgain_ref[...]).astype(BF)
    loads[2].wait()
    hidden = jax.nn.gelu(jnp.dot(box_input, wh_ref[...], preferred_element_type=F32) + bh_ref[...]).astype(BF)
    i0 = iota((entries, entries), 0)
    turn = jnp.where(iota((entries, entries), 1) == i0 % rows * listing + i0 // rows, 1.0, 0.0).astype(BF)
    hidden = jnp.dot(turn, hidden, preferred_element_type=F32).astype(BF)
    boxes = nt_dot(wb_ref[...], hidden)
    boxes = jnp.where((iota(boxes.shape, 1) // rows).astype(F32) < by_place, boxes, 0.0)
    for j in range(listing):
        box_ref[:, j, :] = boxes[:, j * rows : (j + 1) * rows]


def local(
    track_embed, view_ids, view_count, key_feats, value_feats, track_gain, w_temporal,
    temporal_scale, w_merge, box_gain, w_hidden, b_hidden, w_box,
):
    tm_count = lax.axis_size("tm")
    nt = lax.axis_size("trk")
    nz = tm_count // NX
    ny = nt // CORES
    npl = NX * nt
    rows, width = track_embed.shape
    listing = view_ids.shape[1]
    entries = rows * listing
    tokens = key_feats.shape[2]
    per = nz * CAP
    total = npl * per
    longest = npl * CAP
    cap = longest // 2
    chunks = 2
    z = lax.axis_index("tm") // NX

    valid = jnp.arange(listing, dtype=jnp.int32)[None, :] < view_count[:, None]
    shown = jnp.where(valid, view_ids, -1)
    codes = time_code(z * NX + jnp.arange(NX, dtype=jnp.int32), width)
    flat = (shown * rows + jnp.arange(rows, dtype=jnp.int32)[:, None]).reshape(entries)
    plane = flat // (npl * rows)
    ahead = (flat[None, :] < flat[:, None]) & (flat[None, :] >= (plane * (npl * rows))[:, None])
    slot = plane * longest + jnp.sum(ahead.astype(jnp.int32), axis=1)
    slot = jnp.where(valid.reshape(entries), slot, -1)[:, None]

    in_plane_of = jnp.arange(nz, dtype=jnp.int32)
    crowd = jnp.max(jnp.sum((plane[None, :] == in_plane_of[:, None]).astype(jnp.int32), axis=1))
    turned = jnp.concatenate(
        [jnp.tile(shown.T, (1, ny)), jnp.broadcast_to(crowd, (8, ny * rows))], axis=0)

    anywhere = pl.BlockSpec(memory_space=pl.ANY)
    vmem = pl.BlockSpec(memory_space=pltpu.VMEM)
    dma = pltpu.SemaphoreType.DMA
    gain = track_gain[None, :]
    keys = key_feats.reshape(tokens, width)
    values = value_feats.reshape(tokens, width)
    count = 2 * chunks
    wide = width // chunks
    per = nz // 2 * CAP
    grows = npl * per
    back, kept, target, most = pl.pallas_call(
        functools.partial(mega_kernel, nz, nt, rows, cap, chunks),
        out_shape=(
            jax.ShapeDtypeStruct((chunks, nz * cap, wide), BF),
            jax.ShapeDtypeStruct((count, grows, wide), BF),
            jax.ShapeDtypeStruct((2, per, npl), F32),
            jax.ShapeDtypeStruct((8, ny * rows), jnp.int32),
        ),
        in_specs=[vmem] * 4 + [anywhere] * 2,
        out_specs=(anywhere, anywhere, vmem, vmem),
        scratch_shapes=[
            pltpu.VMEM((nz, ny, rows, width), BF),
            pltpu.VMEM((ny, listing + 8, ny * rows), jnp.int32),
            pltpu.VMEM((nz, listing + 8, ny * rows), jnp.int32),
            pltpu.VMEM((3, nz, ny * rows, width), BF),
            pltpu.VMEM((nz // 2, grows // 2, width), BF),
            pltpu.VMEM((nz // 2, grows // 2, width), BF),
            pltpu.VMEM((2 * tokens, width), BF),
            pltpu.VMEM((2 * tokens, width), BF),
            pltpu.VMEM((count, npl, per, wide), BF),
            pltpu.VMEM((count, grows, wide), BF),
            pltpu.VMEM((2, grows, nz // 2 * cap), BF),
            pltpu.VMEM((count, nz // 2 * cap, wide), BF),
            pltpu.VMEM((8, ny * rows), jnp.int32),
            pltpu.VMEM((NX * CORES, 8, ny * rows), jnp.int32),
            dma, dma, dma, dma, dma, dma((2 * nz,)), dma, dma((nz,)), dma((2,)), dma((2,)), dma((2,)),
            dma((nz // 2,)), dma((nz // 2,)), dma((count,)), dma((count,)), dma((count,)), dma((count,)), dma, dma, dma((count,)),
        ],
        compiler_params=pltpu.CompilerParams(
            collective_id=0, has_side_effects=True, vmem_limit_bytes=60 * 1024 * 1024),
        name="mega",
    )(track_embed, turned, codes, gain, keys, values)

    boxes_wide = w_box.shape[1]
    shared = (
        slot, track_embed, gain, view_count[None, :], temporal_scale[None, :], box_gain[None, :], b_hidden[None, :], w_box.T,
        w_temporal, w_merge, w_hidden,
    )

    def finish(*backs):
        return pl.pallas_call(
            functools.partial(track_kernel, chunks, len(backs), cap),
            out_shape=(
                jax.ShapeDtypeStruct((entries, width), BF),
                jax.ShapeDtypeStruct((boxes_wide, listing, rows), F32),
            ),
            in_specs=[vmem] * (len(backs) + 4) + [pl.BlockSpec(memory_space=pltpu.SMEM)] + [vmem] * 3 + [anywhere] * 3,
            out_specs=(vmem, vmem),
            scratch_shapes=[
                pltpu.VMEM((entries, 3 * width), BF),
                pltpu.VMEM((entries, width), BF),
                pltpu.VMEM(w_temporal.shape, BF),
                pltpu.VMEM(w_merge.shape, BF),
                pltpu.VMEM(w_hidden.shape, BF),
                dma((3,)),
            ],
            compiler_params=pltpu.CompilerParams(vmem_limit_bytes=56 * 1024 * 1024),
            name="track",
        )(*backs, *shared)

    def finish_long():
        rest = pl.pallas_call(
            functools.partial(rest_kernel, nz, nt, cap, chunks),
            out_shape=jax.ShapeDtypeStruct((chunks, nz * cap, wide), BF),
            in_specs=[anywhere, vmem],
            out_specs=anywhere,
            scratch_shapes=[
                pltpu.VMEM((count, grows, wide), BF),
                pltpu.VMEM((2, grows, nz // 2 * cap), BF),
                pltpu.VMEM((count, nz // 2 * cap, wide), BF),
                dma, dma((count,)), dma((count,)),
            ],
            compiler_params=pltpu.CompilerParams(
                collective_id=1, has_side_effects=True, vmem_limit_bytes=32 * 1024 * 1024),
            name="rest",
        )(kept, target)
        return finish(back, rest)

    refined, boxes = lax.cond(most[0, 0] > cap, finish_long, lambda: finish(back))
    return refined.reshape(rows, listing, width), jnp.transpose(boxes, (2, 1, 0))


def solution(mesh):
    placed = (
        P(("tm", "trk"), None),
        P(("tm", "trk"), None),
        P(("tm", "trk")),
        P("tm", "trk", None, None),
        P("tm", "trk", None, None),
    ) + (P(),) * 8
    return jax.shard_map(
        local,
        mesh=mesh,
        in_specs=placed,
        out_specs=(P(("tm", "trk"), None, None), P(("tm", "trk"), None, None)),
        check_vma=False,
    )
```

```python
import functools
import math

import jax
import jax.numpy as jnp
from jax import lax
from jax.experimental import pallas as pl
from jax.experimental.pallas import tpu as pltpu
from jax.sharding import PartitionSpec as P

HEADS = 8
CAMS = 8
CAP = 4
CORES = 2
NX = 4
EPS = 1e-05
MASKED = -1e30
MESH = pl.DeviceIdType.MESH
BF = jnp.bfloat16
F32 = jnp.float32


def layer_norm(values):
    centre = jnp.mean(values, axis=-1, keepdims=True)
    shifted = values - centre
    spread = jnp.mean(shifted * shifted, axis=-1, keepdims=True)
    return shifted * lax.rsqrt(spread + EPS)


def time_code(frame_ids, model_width):
    half_width = model_width // 2
    freq_index = jnp.arange(half_width).astype(F32)
    freq_rates = jnp.exp(freq_index * (-2.0 * math.log(10000.0) / model_width))
    angles = frame_ids.astype(F32)[..., None] * freq_rates
    return jnp.concatenate([jnp.sin(angles), jnp.cos(angles)], axis=-1)


def iota(shape, dim):
    return lax.broadcasted_iota(jnp.int32, shape, dim)


def nt_dot(a, b):
    return lax.dot_general(a, b, (((1,), (1,)), ((), ())), preferred_element_type=F32)


def tn_dot(a, b):
    return lax.dot_general(a, b, (((0,), (0,)), ((), ())), preferred_element_type=F32)


def place(nt):
    tm = lax.axis_index("tm")
    trk = lax.axis_index("trk")
    z = tm // NX
    x = tm % NX
    return z, x, trk, x * nt + trk


def greet(nz, nt):
    z, x, trk, me = place(nt)
    npl = NX * nt
    barrier = pltpu.get_barrier_semaphore()

    @pl.loop(1, npl)
    def _(k):
        p = lax.rem(me + k, npl)
        pl.semaphore_signal(barrier, inc=1, device_id=(z * NX + p // nt, p % nt), device_id_type=MESH)

    @pl.loop(1, nz)
    def _(k):
        zz = lax.rem(z + k, nz)
        pl.semaphore_signal(barrier, inc=1, device_id=(zz * NX + x, trk), device_id_type=MESH)

    pl.semaphore_wait(barrier, npl - 1 + nz - 1)


def await_bytes(like, sem):
    pltpu.make_async_copy(like, like, sem).wait()


def z_order(nz):
    half = nz // 2
    return [k for d in range(1, half) for k in (d, nz - d)] + [half, 0]


def mega_kernel(
    nz, nt, rows, cap, chunks,
    embed_ref, ids_ref, code_ref, gain_ref, key_ref, value_ref,
    back_ref, kept_ref, target_ref, most_ref,
    emb_z, ids_y, ids_z, parts, q_send, q_recv, kk_ref, vv_ref, a_send, a_recv, moves, b_send, most_one, most_all,
    y_send, y_recv, yi_send, yi_recv, z_send, z_recv, zi_send, zi_recv, kv_own, kv_send, kv_recv,
    q_ssem, q_rsem, a_ssem, a_rsem, b_ssem, b_rsem, most_ssem, most_rsem, keep_sem,
):
    z, x, trk, me = place(nt)
    y, core = trk // CORES, trk % CORES
    ny = nt // CORES
    npl = NX * nt
    nx = NX * CORES
    me_x = x * CORES + core
    width = embed_ref.shape[1]
    tokens = key_ref.shape[0]
    order = z_order(nz)
    half = nz // 2
    per = half * CAP
    lot = ny * 2 * CAP
    lanes = ny * rows
    head = 128
    wide = width // chunks
    scale = head ** (-0.5) * math.log2(math.e)
    listing = ids_ref.shape[0] - 8
    mine = pl.ds(pl.multiple_of(me * per, per), per)
    line = pl.ds(pl.multiple_of(z * cap, cap), cap)
    greet(nz, nt)

    own_e = pltpu.make_async_copy(embed_ref, emb_z.at[0, 0], y_recv)
    own_e.start()
    own_i = pltpu.make_async_copy(ids_ref, ids_y.at[0], yi_recv)
    own_i.start()
    for k in range(1, ny):
        to = (z * NX + x, lax.rem(y + k, ny) * CORES + core)
        pltpu.make_async_remote_copy(
            src_ref=ids_ref, dst_ref=ids_y.at[ny - k], send_sem=yi_send, recv_sem=yi_recv,
            device_id=to, device_id_type=MESH).start()
    for k in range(1, ny):
        to = (z * NX + x, lax.rem(y + k, ny) * CORES + core)
        pltpu.make_async_remote_copy(
            src_ref=embed_ref, dst_ref=emb_z.at[0, ny - k], send_sem=y_send, recv_sem=y_recv,
            device_id=to, device_id_type=MESH).start()

    before = (z * NX + x, lax.rem(trk + nt - 1, nt))
    first, second = pl.ds(0, tokens), pl.ds(tokens, tokens)
    copies = []
    for i, (own, both) in enumerate(((key_ref, kk_ref), (value_ref, vv_ref))):
        copies.append(pltpu.make_async_copy(own, both.at[first], kv_own.at[i]))
        copies.append(pltpu.make_async_remote_copy(
            src_ref=own, dst_ref=both.at[second], send_sem=kv_send.at[i], recv_sem=kv_recv.at[i],
            device_id=before, device_id_type=MESH))

    await_bytes(ids_y, yi_recv)
    for copy in copies:
        copy.start()
    lane = iota(ids_y.shape[1:], 1) // rows
    ids = ids_y[0]
    most = ids_y[0, listing:, :]
    for i in range(1, ny):
        ids = jnp.where(lane == i, ids_y[i], ids)
        most = jnp.maximum(most, ids_y[i, listing:, :])
    ids_z[0, :listing, :] = ids[:listing]
    ids_z[0, listing:, :] = most
    await_bytes(emb_z.at[0], y_recv)

    def to_z(source, step, part):
        target = (source - step) % nz
        device = (lax.rem(z + nz + step, nz) * NX + x, trk)
        if part == 0:
            pltpu.make_async_remote_copy(
                src_ref=ids_z.at[source], dst_ref=ids_z.at[target], send_sem=zi_send, recv_sem=zi_recv.at[target],
                device_id=device, device_id_type=MESH).start()
        few = pl.ds(part * (ny // 2), ny // 2)
        pltpu.make_async_remote_copy(
            src_ref=emb_z.at[source, few], dst_ref=emb_z.at[target, few], send_sem=z_send,
            recv_sem=z_recv.at[2 * target + part], device_id=device, device_id_type=MESH).start()

    def arrive(slot, part):
        if part == 0:
            await_bytes(ids_z.at[slot], zi_recv.at[slot])
        await_bytes(emb_z.at[slot, pl.ds(part * (ny // 2), ny // 2)], z_recv.at[2 * slot + part])

    for part in range(2):
        to_z(0, 1, part)
        to_z(0, -1, part)

    view_x = iota((nx, lanes), 0)
    view_x = (z * NX + view_x // CORES) * nt + y * CORES + view_x % CORES
    view_p = z * npl + iota((npl, lanes), 0)
    c0 = iota((lanes, lanes), 0)
    c1 = iota((lanes, lanes), 1)
    earlier = jnp.where((c0 < c1) & (c0 // rows == c1 // rows), 1.0, 0.0).astype(BF)
    lane_at = iota((nx, lanes), 1) // rows
    slot_row = iota((per, lanes), 0)
    same_z = slot_row // CAP == iota((per, lanes), 1) // rows
    slot_r = (slot_row % CAP).astype(F32)
    own_lane = iota((per, lanes), 1) < rows
    v0 = iota((npl, npl), 0)
    v1 = iota((npl, npl), 1)
    before_v = jnp.where(v0 < v1, 1.0, 0.0).astype(BF)
    tr = (iota((per, npl), 0) % CAP).astype(F32)

    def names(ids, view):
        named = jnp.zeros(view.shape, F32)
        for j in range(listing):
            named = jnp.where(ids[j : j + 1, :] == view, 1.0, named)
        return named

    ranked, found = {}, {}

    def prepare(slot):
        ids = ids_z[slot, :listing, :]
        named = names(ids, view_x)
        rank = jnp.dot(named.astype(BF), earlier, preferred_element_type=F32)
        ranked[slot] = jnp.where(named > 0.5, rank, -1.0)
        here = jnp.where((slot_row // CAP == order.index(slot) % half) & own_lane, 1.0, 0.0).astype(BF)
        found[slot] = nt_dot(here, names(ids, view_p).astype(BF))
        states = layer_norm(emb_z[slot].reshape(lanes, width).astype(F32)) * gain_ref[...]
        high = states.astype(BF)
        rest = states - high.astype(F32)
        middle = rest.astype(BF)
        parts[0, slot] = high
        parts[1, slot] = middle
        parts[2, slot] = (rest - middle.astype(F32)).astype(BF)

    def build(f):
        slots = order[2 * f : 2 * f + 2]
        for side in range(ny // 2):
            here = jnp.zeros((nx, lanes), F32)
            sources = []
            for i in range(4):
                dy, slot = 2 * side + i // 2, slots[i % 2]
                shift = (i - dy) * rows % lanes
                moved = pltpu.roll(ranked[slot], shift, 1) if shift else ranked[slot]
                here = jnp.where(lane_at == i, moved, here)
                sources.append((slot, slice(dy * rows, (dy + 1) * rows)))
            picks = [jnp.where(same_z & (here[v : v + 1, :] == slot_r), 1.0, 0.0).astype(BF) for v in range(nx)]
            pick = jnp.concatenate(picks, axis=0)
            pick = jnp.concatenate([pick, pick, pick], axis=1)
            source = jnp.concatenate([parts[k, slot, at] for k in range(3) for slot, at in sources], axis=0)
            made = jnp.dot(pick, source, preferred_element_type=F32)
            for v in range(nx):
                frame = v // CORES
                one = made[v * per : (v + 1) * per] + code_ref[frame : frame + 1, :]
                q_send[f, v * lot + side * per : v * lot + (side + 1) * per, :] = one.astype(BF)
        block_x = pl.ds(pl.multiple_of(me_x * lot, lot), lot)
        pltpu.make_async_copy(q_send.at[f, block_x], q_recv.at[f, block_x], q_rsem.at[f]).start()
        for k in range(1, nx):
            p = lax.rem(me_x + k, nx)
            pltpu.make_async_remote_copy(
                src_ref=q_send.at[f, pl.ds(pl.multiple_of(p * lot, lot), lot)], dst_ref=q_recv.at[f, block_x],
                send_sem=q_ssem.at[f], recv_sem=q_rsem.at[f],
                device_id=(z * NX + lax.div(p, CORES), y * CORES + lax.rem(p, CORES)), device_id_type=MESH).start()

    def aim(g):
        slots = order[g * half : (g + 1) * half]
        counts = found[slots[0]]
        for slot in slots[1:]:
            counts = counts + found[slot]
        base = jnp.dot(counts.astype(BF), before_v, preferred_element_type=F32)
        target_ref[g] = jnp.where(tr < counts, base + tr, -1.0)

    prepare(0)
    for k in range(1, half):
        for part in range(2):
            arrive(nz - k, part)
            if k < half - 1 or part == 0:
                to_z(nz - k, 1, part)
            arrive(k, part)
            if k < half - 1 or part == 1:
                to_z(k, -1, part)
        prepare(nz - k)
        prepare(k)
        build(k - 1)
    for part in range(2):
        arrive(half, part)
    prepare(half)
    build(half - 1)
    aim(0)
    aim(1)

    most = ids_z[0, listing:, :]
    for i in range(1, nz):
        most = jnp.maximum(most, ids_z[i, listing:, :])
    most_one[...] = most
    pltpu.make_async_copy(most_one, most_all.at[me_x], most_rsem).start()
    for k in range(1, nx):
        p = lax.rem(me_x + k, nx)
        pltpu.make_async_remote_copy(
            src_ref=most_one, dst_ref=most_all.at[me_x], send_sem=most_ssem, recv_sem=most_rsem,
            device_id=(z * NX + lax.div(p, CORES), y * CORES + lax.rem(p, CORES)), device_id_type=MESH).start()

    def attend(f, c):
        n, part = f // 2 * chunks + c, f % 2 * 2 * CAP

        def score(h):
            some = slice(c * wide + h * head, c * wide + (h + 1) * head)
            return nt_dot(q_recv[f, :, some], kk_ref[:, some])

        ahead = score(0)
        for h in range(wide // head):
            scores = ahead
            if h + 1 < wide // head:
                ahead = score(h + 1)
            top = jnp.max(scores, axis=-1, keepdims=True)
            weights = jnp.exp2((scores - top) * scale)
            sums = jnp.sum(weights, axis=-1, keepdims=True)
            some = slice(c * wide + h * head, c * wide + (h + 1) * head)
            o = jnp.dot(weights.astype(BF), vv_ref[:, some], preferred_element_type=F32) / sums
            a_send[n, :, part : part + 2 * CAP, h * head : (h + 1) * head] = o.reshape(npl, 2 * CAP, head).astype(BF)

    def send_in_plane(n):
        pltpu.make_async_copy(a_send.at[n, me_x * ny], a_recv.at[n, mine], a_rsem.at[n]).start()

        @pl.loop(1, npl)
        def _(k):
            p = lax.rem(me + k * (nt + 1), npl)
            px, pt = lax.div(p, nt), lax.rem(p, nt)
            dy = lax.rem(lax.div(pt, CORES) + ny - y, ny)
            pltpu.make_async_remote_copy(
                src_ref=a_send.at[n, (px * CORES + lax.rem(pt, CORES)) * ny + dy], dst_ref=a_recv.at[n, mine],
                send_sem=a_ssem.at[n], recv_sem=a_rsem.at[n],
                device_id=(z * NX + px, pt), device_id_type=MESH).start()

    def send_along_z(n):
        g, c = n // chunks, n % chunks
        await_bytes(a_recv.at[n], a_rsem.at[n])
        pltpu.make_async_copy(a_recv.at[n], kept_ref.at[n], keep_sem.at[n]).start()
        b_send[n] = tn_dot(moves[g], a_recv[n]).astype(BF)
        for i in range(half):
            dz = order[g * half + i]
            src = b_send.at[n, pl.ds(i * cap, cap)]
            if dz == 0:
                pltpu.make_async_copy(src, back_ref.at[c, line], b_rsem.at[n]).start()
            else:
                pltpu.make_async_remote_copy(
                    src_ref=src, dst_ref=back_ref.at[c, line], send_sem=b_ssem.at[n], recv_sem=b_rsem.at[n],
                    device_id=(lax.rem(z + dz, nz) * NX + x, trk), device_id_type=MESH).start()

    def ready(f):
        await_bytes(q_recv.at[f], q_rsem.at[f])

    def moves_of(g):
        goal = iota((per, half * cap), 1)
        goal_z = iota((per, half * cap), 0) // CAP == goal // cap
        goal_at = (goal % cap).astype(F32)
        for v in range(npl):
            hit = goal_z & (target_ref[g, :, v : v + 1] == goal_at)
            moves[g, v * per : (v + 1) * per, :] = jnp.where(hit, 1.0, 0.0).astype(BF)

    moves_of(0)
    moves_of(1)
    for copy in copies:
        copy.wait()
    ready(0)
    attend(0, 0)
    attend(0, 1)
    ready(1)
    attend(1, 0)
    send_in_plane(0)
    attend(1, 1)
    send_in_plane(1)
    ready(2)
    attend(2, 0)
    attend(2, 1)
    ready(3)
    attend(3, 0)
    send_in_plane(2)
    send_along_z(0)
    attend(3, 1)
    send_in_plane(3)
    send_along_z(1)
    send_along_z(2)
    send_along_z(3)

    await_bytes(ids_y.at[pl.ds(0, ny - 1)], yi_send)
    await_bytes(emb_z.at[0, pl.ds(0, ny - 1)], y_send)
    await_bytes(emb_z.at[pl.ds(0, nz - 1)], z_send)
    await_bytes(ids_z.at[pl.ds(0, nz - 1)], zi_send)
    await_bytes(most_all.at[pl.ds(0, nx - 1)], most_ssem)
    await_bytes(most_all, most_rsem)
    most_ref[...] = jnp.max(most_all[...], axis=0)
    for f in range(half):
        await_bytes(q_send.at[f, pl.ds(0, (nx - 1) * lot)], q_ssem.at[f])
    for n in range(2 * chunks):
        remote = sum(1 for i in range(half) if order[n // chunks * half + i] != 0)
        await_bytes(a_send.at[n, pl.ds(0, npl - 1)], a_ssem.at[n])
        await_bytes(b_send.at[n, pl.ds(0, remote * cap)], b_ssem.at[n])
        await_bytes(back_ref.at[0, pl.ds(0, half * cap)], b_rsem.at[n])
        await_bytes(kept_ref.at[n], keep_sem.at[n])


def rest_kernel(
    nz, nt, cap, chunks,
    kept_ref, target_ref,
    back_ref,
    kept, moves, b_send, load_sem, b_ssem, b_rsem,
):
    z, x, trk, me = place(nt)
    npl = NX * nt
    order = z_order(nz)
    half = nz // 2
    per = half * CAP
    line = pl.ds(pl.multiple_of(z * cap, cap), cap)
    greet(nz, nt)
    load = pltpu.make_async_copy(kept_ref, kept, load_sem)
    load.start()
    load.wait()
    goal = iota((per, half * cap), 1)
    goal_z = iota((per, half * cap), 0) // CAP == goal // cap
    goal_at = (goal % cap + cap).astype(F32)
    for g in range(2):
        for v in range(npl):
            hit = goal_z & (target_ref[g, :, v : v + 1] == goal_at)
            moves[g, v * per : (v + 1) * per, :] = jnp.where(hit, 1.0, 0.0).astype(BF)
    for n in range(2 * chunks):
        g, c = n // chunks, n % chunks
        b_send[n] = tn_dot(moves[g], kept[n]).astype(BF)
        for i in range(half):
            dz = order[g * half + i]
            src = b_send.at[n, pl.ds(i * cap, cap)]
            if dz == 0:
                pltpu.make_async_copy(src, back_ref.at[c, line], b_rsem.at[n]).start()
            else:
                pltpu.make_async_remote_copy(
                    src_ref=src, dst_ref=back_ref.at[c, line], send_sem=b_ssem.at[n], recv_sem=b_rsem.at[n],
                    device_id=(lax.rem(z + dz, nz) * NX + x, trk), device_id_type=MESH).start()
    for n in range(2 * chunks):
        remote = sum(1 for i in range(half) if order[n // chunks * half + i] != 0)
        await_bytes(b_send.at[n, pl.ds(0, remote * cap)], b_ssem.at[n])
        await_bytes(back_ref.at[0, pl.ds(0, half * cap)], b_rsem.at[n])


def track_kernel(
    chunks, lists, cap, *refs,
):
    backs, refs = refs[:lists], refs[lists:]
    (
        slot_ref, embed_ref, gain_ref, count_ref, scale_ref, bgain_ref, bh_ref, wb_ref,
        wt_any, wm_any, wh_any,
        refined_ref, box_ref,
        projected, mixed, wt_ref, wm_ref, wh_ref, load_sem,
    ) = refs
    loads = [
        pltpu.make_async_copy(far, near, load_sem.at[i])
        for i, (far, near) in enumerate(((wt_any, wt_ref), (wm_any, wm_ref), (wh_any, wh_ref)))
    ]
    for load in loads:
        load.start()
    rows, width = embed_ref.shape
    entries = slot_ref.shape[0]
    listing = entries // rows
    slots = backs[0].shape[1]
    column = iota((entries, slots), 1)
    attended = 0.0
    for k in range(lists):
        sought = (column // cap) * (CAP * NX * CAMS) + column % cap + k * cap
        pick = jnp.where(slot_ref[...] == sought, 1.0, 0.0).astype(BF)
        attended = attended + jnp.concatenate(
            [jnp.dot(pick, backs[k][c], preferred_element_type=F32) for c in range(chunks)], axis=1)
    states = layer_norm(embed_ref[...].astype(F32)) * gain_ref[...]
    states = jnp.broadcast_to(states[:, None, :], (rows, listing, width)).reshape(entries, width)
    residual = states + attended
    normed = layer_norm(residual).astype(BF)
    loads[0].wait()
    projected[...] = jnp.dot(normed, wt_ref[...], preferred_element_type=F32).astype(BF)
    track = iota((rows, entries), 0)
    place_at = iota((rows, entries), 1)
    per_track = count_ref[...].astype(F32).astype(BF)
    by_track = jnp.dot(per_track, jnp.where(place_at // listing == track, 1.0, 0.0).astype(BF), preferred_element_type=F32)
    by_place = jnp.dot(per_track, jnp.where(place_at % rows == track, 1.0, 0.0).astype(BF), preferred_element_type=F32)
    block = 128
    head = width // HEADS
    row = iota((block, block), 0) // listing
    col = iota((block, block), 1)
    for b in range(entries // block):
        at = slice(b * block, (b + 1) * block)
        open_keys = (row == col // listing) & ((col % listing).astype(F32) < by_track[:, at])
        scores = []
        for h in range(HEADS):
            q = projected[at, h * head : (h + 1) * head]
            k = projected[at, width + h * head : width + (h + 1) * head]
            scores.append(nt_dot(q, k) * (scale_ref[0, h] * head ** (-0.5)))
        scores = jnp.where(open_keys[None], jnp.stack(scores, axis=0), MASKED)
        weights = jnp.exp(scores - jnp.max(scores, axis=-1, keepdims=True))
        probs = (weights * (1.0 / jnp.sum(weights, axis=-1, keepdims=True))).astype(BF)
        for h in range(HEADS):
            v = projected[at, 2 * width + h * head : 2 * width + (h + 1) * head]
            mixed[at, h * head : (h + 1) * head] = jnp.dot(probs[h], v, preferred_element_type=F32).astype(BF)
    loads[1].wait()
    updated = residual + jnp.dot(mixed[...], wm_ref[...], preferred_element_type=F32)
    refined_ref[...] = jnp.where(slot_ref[...] >= 0, updated, 0.0).astype(BF)
    box_input = (layer_norm(updated) * bgain_ref[...]).astype(BF)
    loads[2].wait()
    hidden = jax.nn.gelu(jnp.dot(box_input, wh_ref[...], preferred_element_type=F32) + bh_ref[...]).astype(BF)
    i0 = iota((entries, entries), 0)
    turn = jnp.where(iota((entries, entries), 1) == i0 % rows * listing + i0 // rows, 1.0, 0.0).astype(BF)
    hidden = jnp.dot(turn, hidden, preferred_element_type=F32).astype(BF)
    boxes = nt_dot(wb_ref[...], hidden)
    boxes = jnp.where((iota(boxes.shape, 1) // rows).astype(F32) < by_place, boxes, 0.0)
    for j in range(listing):
        box_ref[:, j, :] = boxes[:, j * rows : (j + 1) * rows]


def local(
    track_embed, view_ids, view_count, key_feats, value_feats, track_gain, w_temporal,
    temporal_scale, w_merge, box_gain, w_hidden, b_hidden, w_box,
):
    tm_count = lax.axis_size("tm")
    nt = lax.axis_size("trk")
    nz = tm_count // NX
    ny = nt // CORES
    npl = NX * nt
    rows, width = track_embed.shape
    listing = view_ids.shape[1]
    entries = rows * listing
    tokens = key_feats.shape[2]
    per = nz * CAP
    total = npl * per
    longest = npl * CAP
    cap = longest // 2
    chunks = 2
    z = lax.axis_index("tm") // NX

    valid = jnp.arange(listing, dtype=jnp.int32)[None, :] < view_count[:, None]
    shown = jnp.where(valid, view_ids, -1)
    codes = time_code(z * NX + jnp.arange(NX, dtype=jnp.int32), width)
    flat = (shown * rows + jnp.arange(rows, dtype=jnp.int32)[:, None]).reshape(entries)
    plane = flat // (npl * rows)
    ahead = (flat[None, :] < flat[:, None]) & (flat[None, :] >= (plane * (npl * rows))[:, None])
    slot = plane * longest + jnp.sum(ahead.astype(jnp.int32), axis=1)
    slot = jnp.where(valid.reshape(entries), slot, -1)[:, None]

    in_plane_of = jnp.arange(nz, dtype=jnp.int32)
    crowd = jnp.max(jnp.sum((plane[None, :] == in_plane_of[:, None]).astype(jnp.int32), axis=1))
    turned = jnp.concatenate(
        [jnp.tile(shown.T, (1, ny)), jnp.broadcast_to(crowd, (8, ny * rows))], axis=0)

    anywhere = pl.BlockSpec(memory_space=pl.ANY)
    vmem = pl.BlockSpec(memory_space=pltpu.VMEM)
    dma = pltpu.SemaphoreType.DMA
    gain = track_gain[None, :]
    keys = key_feats.reshape(tokens, width)
    values = value_feats.reshape(tokens, width)
    count = 2 * chunks
    wide = width // chunks
    per = nz // 2 * CAP
    grows = npl * per
    back, kept, target, most = pl.pallas_call(
        functools.partial(mega_kernel, nz, nt, rows, cap, chunks),
        out_shape=(
            jax.ShapeDtypeStruct((chunks, nz * cap, wide), BF),
            jax.ShapeDtypeStruct((count, grows, wide), BF),
            jax.ShapeDtypeStruct((2, per, npl), F32),
            jax.ShapeDtypeStruct((8, ny * rows), jnp.int32),
        ),
        in_specs=[vmem] * 4 + [anywhere] * 2,
        out_specs=(anywhere, anywhere, vmem, vmem),
        scratch_shapes=[
            pltpu.VMEM((nz, ny, rows, width), BF),
            pltpu.VMEM((ny, listing + 8, ny * rows), jnp.int32),
            pltpu.VMEM((nz, listing + 8, ny * rows), jnp.int32),
            pltpu.VMEM((3, nz, ny * rows, width), BF),
            pltpu.VMEM((nz // 2, grows // 2, width), BF),
            pltpu.VMEM((nz // 2, grows // 2, width), BF),
            pltpu.VMEM((2 * tokens, width), BF),
            pltpu.VMEM((2 * tokens, width), BF),
            pltpu.VMEM((count, npl, per, wide), BF),
            pltpu.VMEM((count, grows, wide), BF),
            pltpu.VMEM((2, grows, nz // 2 * cap), BF),
            pltpu.VMEM((count, nz // 2 * cap, wide), BF),
            pltpu.VMEM((8, ny * rows), jnp.int32),
            pltpu.VMEM((NX * CORES, 8, ny * rows), jnp.int32),
            dma, dma, dma, dma, dma, dma((2 * nz,)), dma, dma((nz,)), dma((2,)), dma((2,)), dma((2,)),
            dma((nz // 2,)), dma((nz // 2,)), dma((count,)), dma((count,)), dma((count,)), dma((count,)), dma, dma, dma((count,)),
        ],
        compiler_params=pltpu.CompilerParams(
            collective_id=0, has_side_effects=True, vmem_limit_bytes=52 * 1024 * 1024),
        name="mega",
    )(track_embed, turned, codes, gain, keys, values)

    boxes_wide = w_box.shape[1]
    shared = (
        slot, track_embed, gain, view_count[None, :], temporal_scale[None, :], box_gain[None, :], b_hidden[None, :], w_box.T,
        w_temporal, w_merge, w_hidden,
    )

    def finish(*backs):
        return pl.pallas_call(
            functools.partial(track_kernel, chunks, len(backs), cap),
            out_shape=(
                jax.ShapeDtypeStruct((entries, width), BF),
                jax.ShapeDtypeStruct((boxes_wide, listing, rows), F32),
            ),
            in_specs=[vmem] * (len(backs) + 4) + [pl.BlockSpec(memory_space=pltpu.SMEM)] + [vmem] * 3 + [anywhere] * 3,
            out_specs=(vmem, vmem),
            scratch_shapes=[
                pltpu.VMEM((entries, 3 * width), BF),
                pltpu.VMEM((entries, width), BF),
                pltpu.VMEM(w_temporal.shape, BF),
                pltpu.VMEM(w_merge.shape, BF),
                pltpu.VMEM(w_hidden.shape, BF),
                dma((3,)),
            ],
            compiler_params=pltpu.CompilerParams(vmem_limit_bytes=56 * 1024 * 1024),
            name="track",
        )(*backs, *shared)

    def finish_long():
        rest = pl.pallas_call(
            functools.partial(rest_kernel, nz, nt, cap, chunks),
            out_shape=jax.ShapeDtypeStruct((chunks, nz * cap, wide), BF),
            in_specs=[anywhere, vmem],
            out_specs=anywhere,
            scratch_shapes=[
                pltpu.VMEM((count, grows, wide), BF),
                pltpu.VMEM((2, grows, nz // 2 * cap), BF),
                pltpu.VMEM((count, nz // 2 * cap, wide), BF),
                dma, dma((count,)), dma((count,)),
            ],
            compiler_params=pltpu.CompilerParams(
                collective_id=1, has_side_effects=True, vmem_limit_bytes=32 * 1024 * 1024),
            name="rest",
        )(kept, target)
        return finish(back, rest)

    refined, boxes = lax.cond(most[0, 0] > cap, finish_long, lambda: finish(back))
    return refined.reshape(rows, listing, width), jnp.transpose(boxes, (2, 1, 0))


def solution(mesh):
    placed = (
        P(("tm", "trk"), None),
        P(("tm", "trk"), None),
        P(("tm", "trk")),
        P("tm", "trk", None, None),
        P("tm", "trk", None, None),
    ) + (P(),) * 8
    return jax.shard_map(
        local,
        mesh=mesh,
        in_specs=placed,
        out_specs=(P(("tm", "trk"), None, None), P(("tm", "trk"), None, None)),
        check_vma=False,
    )
```

```python
import functools
import math

import jax
import jax.numpy as jnp
from jax import lax
from jax.experimental import pallas as pl
from jax.experimental.pallas import tpu as pltpu
from jax.sharding import PartitionSpec as P

HEADS = 8
CAMS = 8
CAP = 4
CORES = 2
NX = 4
EPS = 1e-05
MASKED = -1e30
MESH = pl.DeviceIdType.MESH
BF = jnp.bfloat16
F32 = jnp.float32


def layer_norm(values):
    centre = jnp.mean(values, axis=-1, keepdims=True)
    shifted = values - centre
    spread = jnp.mean(shifted * shifted, axis=-1, keepdims=True)
    return shifted * lax.rsqrt(spread + EPS)


def time_code(frame_ids, model_width):
    half_width = model_width // 2
    freq_index = jnp.arange(half_width).astype(F32)
    freq_rates = jnp.exp(freq_index * (-2.0 * math.log(10000.0) / model_width))
    angles = frame_ids.astype(F32)[..., None] * freq_rates
    return jnp.concatenate([jnp.sin(angles), jnp.cos(angles)], axis=-1)


def iota(shape, dim):
    return lax.broadcasted_iota(jnp.int32, shape, dim)


def nt_dot(a, b):
    return lax.dot_general(a, b, (((1,), (1,)), ((), ())), preferred_element_type=F32)


def tn_dot(a, b):
    return lax.dot_general(a, b, (((0,), (0,)), ((), ())), preferred_element_type=F32)


def place(nt):
    tm = lax.axis_index("tm")
    trk = lax.axis_index("trk")
    z = tm // NX
    x = tm % NX
    return z, x, trk, x * nt + trk


def greet(nz, nt):
    z, x, trk, me = place(nt)
    npl = NX * nt
    barrier = pltpu.get_barrier_semaphore()

    @pl.loop(1, npl)
    def _(k):
        p = lax.rem(me + k, npl)
        pl.semaphore_signal(barrier, inc=1, device_id=(z * NX + p // nt, p % nt), device_id_type=MESH)

    @pl.loop(1, nz)
    def _(k):
        zz = lax.rem(z + k, nz)
        pl.semaphore_signal(barrier, inc=1, device_id=(zz * NX + x, trk), device_id_type=MESH)

    pl.semaphore_wait(barrier, npl - 1 + nz - 1)


def await_bytes(like, sem):
    pltpu.make_async_copy(like, like, sem).wait()


def z_order(nz):
    half = nz // 2
    return [k for d in range(1, half) for k in (d, nz - d)] + [half, 0]


def mega_kernel(
    nz, nt, rows, cap, chunks,
    embed_ref, ids_ref, code_ref, gain_ref, key_ref, value_ref,
    back_ref, kept_ref, target_ref, most_ref,
    emb_z, ids_y, ids_z, parts, q_send, q_recv, kk_ref, vv_ref, a_send, a_recv, moves, b_send, most_one, most_all,
    y_send, y_recv, yi_send, yi_recv, z_send, z_recv, zi_send, zi_recv, kv_own, kv_send, kv_recv,
    q_ssem, q_rsem, a_ssem, a_rsem, b_ssem, b_rsem, most_ssem, most_rsem, keep_sem,
):
    z, x, trk, me = place(nt)
    y, core = trk // CORES, trk % CORES
    ny = nt // CORES
    npl = NX * nt
    nx = NX * CORES
    me_x = x * CORES + core
    width = embed_ref.shape[1]
    tokens = key_ref.shape[0]
    order = z_order(nz)
    half = nz // 2
    per = half * CAP
    lot = ny * 2 * CAP
    lanes = ny * rows
    head = 128
    wide = width // chunks
    scale = head ** (-0.5) * math.log2(math.e)
    listing = ids_ref.shape[0] - 8
    mine = pl.ds(pl.multiple_of(me * per, per), per)
    line = pl.ds(pl.multiple_of(z * cap, cap), cap)
    greet(nz, nt)

    own_e = pltpu.make_async_copy(embed_ref, emb_z.at[0, 0], y_recv)
    own_e.start()
    own_i = pltpu.make_async_copy(ids_ref, ids_y.at[0], yi_recv)
    own_i.start()
    for k in range(1, ny):
        to = (z * NX + x, lax.rem(y + k, ny) * CORES + core)
        pltpu.make_async_remote_copy(
            src_ref=ids_ref, dst_ref=ids_y.at[ny - k], send_sem=yi_send, recv_sem=yi_recv,
            device_id=to, device_id_type=MESH).start()
    for k in range(1, ny):
        to = (z * NX + x, lax.rem(y + k, ny) * CORES + core)
        pltpu.make_async_remote_copy(
            src_ref=embed_ref, dst_ref=emb_z.at[0, ny - k], send_sem=y_send, recv_sem=y_recv,
            device_id=to, device_id_type=MESH).start()

    before = (z * NX + x, lax.rem(trk + nt - 1, nt))
    first, second = pl.ds(0, tokens), pl.ds(tokens, tokens)
    copies = []
    for i, (own, both) in enumerate(((key_ref, kk_ref), (value_ref, vv_ref))):
        copies.append(pltpu.make_async_copy(own, both.at[first], kv_own.at[i]))
        copies.append(pltpu.make_async_remote_copy(
            src_ref=own, dst_ref=both.at[second], send_sem=kv_send.at[i], recv_sem=kv_recv.at[i],
            device_id=before, device_id_type=MESH))

    await_bytes(ids_y, yi_recv)
    for copy in copies:
        copy.start()
    lane = iota(ids_y.shape[1:], 1) // rows
    ids = ids_y[0]
    most = ids_y[0, listing:, :]
    for i in range(1, ny):
        ids = jnp.where(lane == i, ids_y[i], ids)
        most = jnp.maximum(most, ids_y[i, listing:, :])
    ids_z[0, :listing, :] = ids[:listing]
    ids_z[0, listing:, :] = most
    await_bytes(emb_z.at[0], y_recv)

    def to_z(source, step, part):
        target = (source - step) % nz
        device = (lax.rem(z + nz + step, nz) * NX + x, trk)
        if part == 0:
            pltpu.make_async_remote_copy(
                src_ref=ids_z.at[source], dst_ref=ids_z.at[target], send_sem=zi_send, recv_sem=zi_recv.at[target],
                device_id=device, device_id_type=MESH).start()
        few = pl.ds(part * (ny // 2), ny // 2)
        pltpu.make_async_remote_copy(
            src_ref=emb_z.at[source, few], dst_ref=emb_z.at[target, few], send_sem=z_send,
            recv_sem=z_recv.at[2 * target + part], device_id=device, device_id_type=MESH).start()

    def arrive(slot, part):
        if part == 0:
            await_bytes(ids_z.at[slot], zi_recv.at[slot])
        await_bytes(emb_z.at[slot, pl.ds(part * (ny // 2), ny // 2)], z_recv.at[2 * slot + part])

    for part in range(2):
        to_z(0, 1, part)
        to_z(0, -1, part)

    view_x = iota((nx, lanes), 0)
    view_x = (z * NX + view_x // CORES) * nt + y * CORES + view_x % CORES
    view_p = z * npl + iota((npl, lanes), 0)
    c0 = iota((lanes, lanes), 0)
    c1 = iota((lanes, lanes), 1)
    earlier = jnp.where((c0 < c1) & (c0 // rows == c1 // rows), 1.0, 0.0).astype(BF)
    lane_at = iota((nx, lanes), 1) // rows
    slot_row = iota((per, lanes), 0)
    same_z = slot_row // CAP == iota((per, lanes), 1) // rows
    slot_r = (slot_row % CAP).astype(F32)
    own_lane = iota((per, lanes), 1) < rows
    v0 = iota((npl, npl), 0)
    v1 = iota((npl, npl), 1)
    before_v = jnp.where(v0 < v1, 1.0, 0.0).astype(BF)
    tr = (iota((per, npl), 0) % CAP).astype(F32)

    def names(ids, view):
        named = jnp.zeros(view.shape, F32)
        for j in range(listing):
            named = jnp.where(ids[j : j + 1, :] == view, 1.0, named)
        return named

    ranked, found = {}, {}

    def prepare(slot):
        ids = ids_z[slot, :listing, :]
        named = names(ids, view_x)
        rank = jnp.dot(named.astype(BF), earlier, preferred_element_type=F32)
        ranked[slot] = jnp.where(named > 0.5, rank, -1.0)
        here = jnp.where((slot_row // CAP == order.index(slot) % half) & own_lane, 1.0, 0.0).astype(BF)
        found[slot] = nt_dot(here, names(ids, view_p).astype(BF))
        states = layer_norm(emb_z[slot].reshape(lanes, width).astype(F32)) * gain_ref[...]
        high = states.astype(BF)
        rest = states - high.astype(F32)
        middle = rest.astype(BF)
        parts[0, slot] = high
        parts[1, slot] = middle
        parts[2, slot] = (rest - middle.astype(F32)).astype(BF)

    def build(f):
        slots = order[2 * f : 2 * f + 2]
        for side in range(ny // 2):
            here = jnp.zeros((nx, lanes), F32)
            sources = []
            for i in range(4):
                dy, slot = 2 * side + i // 2, slots[i % 2]
                shift = (i - dy) * rows % lanes
                moved = pltpu.roll(ranked[slot], shift, 1) if shift else ranked[slot]
                here = jnp.where(lane_at == i, moved, here)
                sources.append((slot, slice(dy * rows, (dy + 1) * rows)))
            picks = [jnp.where(same_z & (here[v : v + 1, :] == slot_r), 1.0, 0.0).astype(BF) for v in range(nx)]
            pick = jnp.concatenate(picks, axis=0)
            pick = jnp.concatenate([pick, pick, pick], axis=1)
            source = jnp.concatenate([parts[k, slot, at] for k in range(3) for slot, at in sources], axis=0)
            made = jnp.dot(pick, source, preferred_element_type=F32)
            for v in range(nx):
                frame = v // CORES
                one = made[v * per : (v + 1) * per] + code_ref[frame : frame + 1, :]
                q_send[f, v * lot + side * per : v * lot + (side + 1) * per, :] = one.astype(BF)
        block_x = pl.ds(pl.multiple_of(me_x * lot, lot), lot)
        pltpu.make_async_copy(q_send.at[f, block_x], q_recv.at[f, block_x], q_rsem.at[f]).start()
        for k in range(1, nx):
            p = lax.rem(me_x + k, nx)
            pltpu.make_async_remote_copy(
                src_ref=q_send.at[f, pl.ds(pl.multiple_of(p * lot, lot), lot)], dst_ref=q_recv.at[f, block_x],
                send_sem=q_ssem.at[f], recv_sem=q_rsem.at[f],
                device_id=(z * NX + lax.div(p, CORES), y * CORES + lax.rem(p, CORES)), device_id_type=MESH).start()

    def aim(g):
        slots = order[g * half : (g + 1) * half]
        counts = found[slots[0]]
        for slot in slots[1:]:
            counts = counts + found[slot]
        base = jnp.dot(counts.astype(BF), before_v, preferred_element_type=F32)
        target_ref[g] = jnp.where(tr < counts, base + tr, -1.0)

    prepare(0)
    for k in range(1, half):
        for part in range(2):
            arrive(nz - k, part)
            if k < half - 1 or part == 0:
                to_z(nz - k, 1, part)
            arrive(k, part)
            if k < half - 1 or part == 1:
                to_z(k, -1, part)
        prepare(nz - k)
        prepare(k)
        build(k - 1)
    for part in range(2):
        arrive(half, part)
    prepare(half)
    build(half - 1)
    aim(0)
    aim(1)

    most = ids_z[0, listing:, :]
    for i in range(1, nz):
        most = jnp.maximum(most, ids_z[i, listing:, :])
    most_one[...] = most
    pltpu.make_async_copy(most_one, most_all.at[me_x], most_rsem).start()
    for k in range(1, nx):
        p = lax.rem(me_x + k, nx)
        pltpu.make_async_remote_copy(
            src_ref=most_one, dst_ref=most_all.at[me_x], send_sem=most_ssem, recv_sem=most_rsem,
            device_id=(z * NX + lax.div(p, CORES), y * CORES + lax.rem(p, CORES)), device_id_type=MESH).start()

    def attend(f, c):
        n, part = f // 2 * chunks + c, f % 2 * 2 * CAP

        def score(h):
            some = pl.ds(pl.multiple_of(c * wide + h * head, head), head)
            return nt_dot(q_recv[f, :, some], kk_ref[:, some])

        ahead = score(0)
        for h in range(wide // head):
            scores = ahead
            if h + 1 < wide // head:
                ahead = score(h + 1)
            top = jnp.max(scores, axis=-1, keepdims=True)
            weights = jnp.exp2((scores - top) * scale)
            sums = jnp.sum(weights, axis=-1, keepdims=True)
            some = pl.ds(pl.multiple_of(c * wide + h * head, head), head)
            o = jnp.dot(weights.astype(BF), vv_ref[:, some], preferred_element_type=F32) / sums
            a_send[n, :, part : part + 2 * CAP, h * head : (h + 1) * head] = o.reshape(npl, 2 * CAP, head).astype(BF)

    def send_in_plane(n):
        pltpu.make_async_copy(a_send.at[n, me_x * ny], a_recv.at[n, mine], a_rsem.at[n]).start()

        @pl.loop(1, npl)
        def _(k):
            p = lax.rem(me + k * (nt + 1), npl)
            px, pt = lax.div(p, nt), lax.rem(p, nt)
            dy = lax.rem(lax.div(pt, CORES) + ny - y, ny)
            pltpu.make_async_remote_copy(
                src_ref=a_send.at[n, (px * CORES + lax.rem(pt, CORES)) * ny + dy], dst_ref=a_recv.at[n, mine],
                send_sem=a_ssem.at[n], recv_sem=a_rsem.at[n],
                device_id=(z * NX + px, pt), device_id_type=MESH).start()

    def send_along_z(n):
        g, c = n // chunks, n % chunks
        await_bytes(a_recv.at[n], a_rsem.at[n])
        pltpu.make_async_copy(a_recv.at[n], kept_ref.at[n], keep_sem.at[n]).start()
        b_send[n] = tn_dot(moves[g], a_recv[n]).astype(BF)
        for i in range(half):
            dz = order[g * half + i]
            src = b_send.at[n, pl.ds(i * cap, cap)]
            if dz == 0:
                pltpu.make_async_copy(src, back_ref.at[c, line], b_rsem.at[n]).start()
            else:
                pltpu.make_async_remote_copy(
                    src_ref=src, dst_ref=back_ref.at[c, line], send_sem=b_ssem.at[n], recv_sem=b_rsem.at[n],
                    device_id=(lax.rem(z + dz, nz) * NX + x, trk), device_id_type=MESH).start()

    def ready(f):
        await_bytes(q_recv.at[f], q_rsem.at[f])

    def moves_of(g):
        goal = iota((per, half * cap), 1)
        goal_z = iota((per, half * cap), 0) // CAP == goal // cap
        goal_at = (goal % cap).astype(F32)
        for v in range(npl):
            hit = goal_z & (target_ref[g, :, v : v + 1] == goal_at)
            moves[g, v * per : (v + 1) * per, :] = jnp.where(hit, 1.0, 0.0).astype(BF)

    moves_of(0)
    moves_of(1)
    for copy in copies:
        copy.wait()
    ready(0)

    @pl.loop(0, chunks)
    def _(c):
        attend(0, c)

    ready(1)

    @pl.loop(0, chunks)
    def _(c):
        attend(1, c)
        send_in_plane(c)

    ready(2)

    @pl.loop(0, chunks)
    def _(c):
        attend(2, c)

    ready(3)
    attend(3, 0)
    send_in_plane(2)
    send_along_z(0)
    attend(3, 1)
    send_in_plane(3)
    send_along_z(1)
    send_along_z(2)
    send_along_z(3)

    await_bytes(ids_y.at[pl.ds(0, ny - 1)], yi_send)
    await_bytes(emb_z.at[0, pl.ds(0, ny - 1)], y_send)
    await_bytes(emb_z.at[pl.ds(0, nz - 1)], z_send)
    await_bytes(ids_z.at[pl.ds(0, nz - 1)], zi_send)
    await_bytes(most_all.at[pl.ds(0, nx - 1)], most_ssem)
    await_bytes(most_all, most_rsem)
    most_ref[...] = jnp.max(most_all[...], axis=0)
    for f in range(half):
        await_bytes(q_send.at[f, pl.ds(0, (nx - 1) * lot)], q_ssem.at[f])
    for n in range(2 * chunks):
        remote = sum(1 for i in range(half) if order[n // chunks * half + i] != 0)
        await_bytes(a_send.at[n, pl.ds(0, npl - 1)], a_ssem.at[n])
        await_bytes(b_send.at[n, pl.ds(0, remote * cap)], b_ssem.at[n])
        await_bytes(back_ref.at[0, pl.ds(0, half * cap)], b_rsem.at[n])
        await_bytes(kept_ref.at[n], keep_sem.at[n])


def rest_kernel(
    nz, nt, cap, chunks,
    kept_ref, target_ref,
    back_ref,
    kept, moves, b_send, load_sem, b_ssem, b_rsem,
):
    z, x, trk, me = place(nt)
    npl = NX * nt
    order = z_order(nz)
    half = nz // 2
    per = half * CAP
    line = pl.ds(pl.multiple_of(z * cap, cap), cap)
    greet(nz, nt)
    load = pltpu.make_async_copy(kept_ref, kept, load_sem)
    load.start()
    load.wait()
    goal = iota((per, half * cap), 1)
    goal_z = iota((per, half * cap), 0) // CAP == goal // cap
    goal_at = (goal % cap + cap).astype(F32)
    for g in range(2):
        for v in range(npl):
            hit = goal_z & (target_ref[g, :, v : v + 1] == goal_at)
            moves[g, v * per : (v + 1) * per, :] = jnp.where(hit, 1.0, 0.0).astype(BF)
    for n in range(2 * chunks):
        g, c = n // chunks, n % chunks
        b_send[n] = tn_dot(moves[g], kept[n]).astype(BF)
        for i in range(half):
            dz = order[g * half + i]
            src = b_send.at[n, pl.ds(i * cap, cap)]
            if dz == 0:
                pltpu.make_async_copy(src, back_ref.at[c, line], b_rsem.at[n]).start()
            else:
                pltpu.make_async_remote_copy(
                    src_ref=src, dst_ref=back_ref.at[c, line], send_sem=b_ssem.at[n], recv_sem=b_rsem.at[n],
                    device_id=(lax.rem(z + dz, nz) * NX + x, trk), device_id_type=MESH).start()
    for n in range(2 * chunks):
        remote = sum(1 for i in range(half) if order[n // chunks * half + i] != 0)
        await_bytes(b_send.at[n, pl.ds(0, remote * cap)], b_ssem.at[n])
        await_bytes(back_ref.at[0, pl.ds(0, half * cap)], b_rsem.at[n])


def track_kernel(
    chunks, lists, cap, *refs,
):
    backs, refs = refs[:lists], refs[lists:]
    (
        slot_ref, embed_ref, gain_ref, count_ref, scale_ref, bgain_ref, bh_ref, wb_ref,
        wt_any, wm_any, wh_any,
        refined_ref, box_ref,
        projected, mixed, wt_ref, wm_ref, wh_ref, load_sem,
    ) = refs
    loads = [
        pltpu.make_async_copy(far, near, load_sem.at[i])
        for i, (far, near) in enumerate(((wt_any, wt_ref), (wm_any, wm_ref), (wh_any, wh_ref)))
    ]
    for load in loads:
        load.start()
    rows, width = embed_ref.shape
    entries = slot_ref.shape[0]
    listing = entries // rows
    slots = backs[0].shape[1]
    column = iota((entries, slots), 1)
    attended = 0.0
    for k in range(lists):
        sought = (column // cap) * (CAP * NX * CAMS) + column % cap + k * cap
        pick = jnp.where(slot_ref[...] == sought, 1.0, 0.0).astype(BF)
        attended = attended + jnp.concatenate(
            [jnp.dot(pick, backs[k][c], preferred_element_type=F32) for c in range(chunks)], axis=1)
    states = layer_norm(embed_ref[...].astype(F32)) * gain_ref[...]
    states = jnp.broadcast_to(states[:, None, :], (rows, listing, width)).reshape(entries, width)
    residual = states + attended
    normed = layer_norm(residual).astype(BF)
    loads[0].wait()
    projected[...] = jnp.dot(normed, wt_ref[...], preferred_element_type=F32).astype(BF)
    track = iota((rows, entries), 0)
    place_at = iota((rows, entries), 1)
    per_track = count_ref[...].astype(F32).astype(BF)
    by_track = jnp.dot(per_track, jnp.where(place_at // listing == track, 1.0, 0.0).astype(BF), preferred_element_type=F32)
    by_place = jnp.dot(per_track, jnp.where(place_at % rows == track, 1.0, 0.0).astype(BF), preferred_element_type=F32)
    block = 128
    head = width // HEADS
    row = iota((block, block), 0) // listing
    col = iota((block, block), 1)
    for b in range(entries // block):
        at = slice(b * block, (b + 1) * block)
        open_keys = (row == col // listing) & ((col % listing).astype(F32) < by_track[:, at])
        scores = []
        for h in range(HEADS):
            q = projected[at, h * head : (h + 1) * head]
            k = projected[at, width + h * head : width + (h + 1) * head]
            scores.append(nt_dot(q, k) * (scale_ref[0, h] * head ** (-0.5)))
        scores = jnp.where(open_keys[None], jnp.stack(scores, axis=0), MASKED)
        weights = jnp.exp(scores - jnp.max(scores, axis=-1, keepdims=True))
        probs = (weights * (1.0 / jnp.sum(weights, axis=-1, keepdims=True))).astype(BF)
        for h in range(HEADS):
            v = projected[at, 2 * width + h * head : 2 * width + (h + 1) * head]
            mixed[at, h * head : (h + 1) * head] = jnp.dot(probs[h], v, preferred_element_type=F32).astype(BF)
    loads[1].wait()
    updated = residual + jnp.dot(mixed[...], wm_ref[...], preferred_element_type=F32)
    refined_ref[...] = jnp.where(slot_ref[...] >= 0, updated, 0.0).astype(BF)
    box_input = (layer_norm(updated) * bgain_ref[...]).astype(BF)
    loads[2].wait()
    hidden = jax.nn.gelu(jnp.dot(box_input, wh_ref[...], preferred_element_type=F32) + bh_ref[...]).astype(BF)
    i0 = iota((entries, entries), 0)
    turn = jnp.where(iota((entries, entries), 1) == i0 % rows * listing + i0 // rows, 1.0, 0.0).astype(BF)
    hidden = jnp.dot(turn, hidden, preferred_element_type=F32).astype(BF)
    boxes = nt_dot(wb_ref[...], hidden)
    boxes = jnp.where((iota(boxes.shape, 1) // rows).astype(F32) < by_place, boxes, 0.0)
    for j in range(listing):
        box_ref[:, j, :] = boxes[:, j * rows : (j + 1) * rows]


def local(
    track_embed, view_ids, view_count, key_feats, value_feats, track_gain, w_temporal,
    temporal_scale, w_merge, box_gain, w_hidden, b_hidden, w_box,
):
    tm_count = lax.axis_size("tm")
    nt = lax.axis_size("trk")
    nz = tm_count // NX
    ny = nt // CORES
    npl = NX * nt
    rows, width = track_embed.shape
    listing = view_ids.shape[1]
    entries = rows * listing
    tokens = key_feats.shape[2]
    per = nz * CAP
    total = npl * per
    longest = npl * CAP
    cap = longest // 2
    chunks = 2
    z = lax.axis_index("tm") // NX

    valid = jnp.arange(listing, dtype=jnp.int32)[None, :] < view_count[:, None]
    shown = jnp.where(valid, view_ids, -1)
    codes = time_code(z * NX + jnp.arange(NX, dtype=jnp.int32), width)
    flat = (shown * rows + jnp.arange(rows, dtype=jnp.int32)[:, None]).reshape(entries)
    plane = flat // (npl * rows)
    ahead = (flat[None, :] < flat[:, None]) & (flat[None, :] >= (plane * (npl * rows))[:, None])
    slot = plane * longest + jnp.sum(ahead.astype(jnp.int32), axis=1)
    slot = jnp.where(valid.reshape(entries), slot, -1)[:, None]

    in_plane_of = jnp.arange(nz, dtype=jnp.int32)
    crowd = jnp.max(jnp.sum((plane[None, :] == in_plane_of[:, None]).astype(jnp.int32), axis=1))
    turned = jnp.concatenate(
        [jnp.tile(shown.T, (1, ny)), jnp.broadcast_to(crowd, (8, ny * rows))], axis=0)

    anywhere = pl.BlockSpec(memory_space=pl.ANY)
    vmem = pl.BlockSpec(memory_space=pltpu.VMEM)
    dma = pltpu.SemaphoreType.DMA
    gain = track_gain[None, :]
    keys = key_feats.reshape(tokens, width)
    values = value_feats.reshape(tokens, width)
    count = 2 * chunks
    wide = width // chunks
    per = nz // 2 * CAP
    grows = npl * per
    back, kept, target, most = pl.pallas_call(
        functools.partial(mega_kernel, nz, nt, rows, cap, chunks),
        out_shape=(
            jax.ShapeDtypeStruct((chunks, nz * cap, wide), BF),
            jax.ShapeDtypeStruct((count, grows, wide), BF),
            jax.ShapeDtypeStruct((2, per, npl), F32),
            jax.ShapeDtypeStruct((8, ny * rows), jnp.int32),
        ),
        in_specs=[vmem] * 4 + [anywhere] * 2,
        out_specs=(anywhere, anywhere, vmem, vmem),
        scratch_shapes=[
            pltpu.VMEM((nz, ny, rows, width), BF),
            pltpu.VMEM((ny, listing + 8, ny * rows), jnp.int32),
            pltpu.VMEM((nz, listing + 8, ny * rows), jnp.int32),
            pltpu.VMEM((3, nz, ny * rows, width), BF),
            pltpu.VMEM((nz // 2, grows // 2, width), BF),
            pltpu.VMEM((nz // 2, grows // 2, width), BF),
            pltpu.VMEM((2 * tokens, width), BF),
            pltpu.VMEM((2 * tokens, width), BF),
            pltpu.VMEM((count, npl, per, wide), BF),
            pltpu.VMEM((count, grows, wide), BF),
            pltpu.VMEM((2, grows, nz // 2 * cap), BF),
            pltpu.VMEM((count, nz // 2 * cap, wide), BF),
            pltpu.VMEM((8, ny * rows), jnp.int32),
            pltpu.VMEM((NX * CORES, 8, ny * rows), jnp.int32),
            dma, dma, dma, dma, dma, dma((2 * nz,)), dma, dma((nz,)), dma((2,)), dma((2,)), dma((2,)),
            dma((nz // 2,)), dma((nz // 2,)), dma((count,)), dma((count,)), dma((count,)), dma((count,)), dma, dma, dma((count,)),
        ],
        compiler_params=pltpu.CompilerParams(
            collective_id=0, has_side_effects=True, vmem_limit_bytes=52 * 1024 * 1024),
        name="mega",
    )(track_embed, turned, codes, gain, keys, values)

    boxes_wide = w_box.shape[1]
    shared = (
        slot, track_embed, gain, view_count[None, :], temporal_scale[None, :], box_gain[None, :], b_hidden[None, :], w_box.T,
        w_temporal, w_merge, w_hidden,
    )

    def finish(*backs):
        return pl.pallas_call(
            functools.partial(track_kernel, chunks, len(backs), cap),
            out_shape=(
                jax.ShapeDtypeStruct((entries, width), BF),
                jax.ShapeDtypeStruct((boxes_wide, listing, rows), F32),
            ),
            in_specs=[vmem] * (len(backs) + 4) + [pl.BlockSpec(memory_space=pltpu.SMEM)] + [vmem] * 3 + [anywhere] * 3,
            out_specs=(vmem, vmem),
            scratch_shapes=[
                pltpu.VMEM((entries, 3 * width), BF),
                pltpu.VMEM((entries, width), BF),
                pltpu.VMEM(w_temporal.shape, BF),
                pltpu.VMEM(w_merge.shape, BF),
                pltpu.VMEM(w_hidden.shape, BF),
                dma((3,)),
            ],
            compiler_params=pltpu.CompilerParams(vmem_limit_bytes=56 * 1024 * 1024),
            name="track",
        )(*backs, *shared)

    def finish_long():
        rest = pl.pallas_call(
            functools.partial(rest_kernel, nz, nt, cap, chunks),
            out_shape=jax.ShapeDtypeStruct((chunks, nz * cap, wide), BF),
            in_specs=[anywhere, vmem],
            out_specs=anywhere,
            scratch_shapes=[
                pltpu.VMEM((count, grows, wide), BF),
                pltpu.VMEM((2, grows, nz // 2 * cap), BF),
                pltpu.VMEM((count, nz // 2 * cap, wide), BF),
                dma, dma((count,)), dma((count,)),
            ],
            compiler_params=pltpu.CompilerParams(
                collective_id=1, has_side_effects=True, vmem_limit_bytes=32 * 1024 * 1024),
            name="rest",
        )(kept, target)
        return finish(back, rest)

    refined, boxes = lax.cond(most[0, 0] > cap, finish_long, lambda: finish(back))
    return refined.reshape(rows, listing, width), jnp.transpose(boxes, (2, 1, 0))


def solution(mesh):
    placed = (
        P(("tm", "trk"), None),
        P(("tm", "trk"), None),
        P(("tm", "trk")),
        P("tm", "trk", None, None),
        P("tm", "trk", None, None),
    ) + (P(),) * 8
    return jax.shard_map(
        local,
        mesh=mesh,
        in_specs=placed,
        out_specs=(P(("tm", "trk"), None, None), P(("tm", "trk"), None, None)),
        check_vma=False,
    )
```
